128 devices in a mesh: crest: 16 (over x, y), section: 8 (over z, core).
Axes of the slice: x: 4, y: 4, z: 4, core: 2. Of those that a mesh axis runs over, the one named last changes fastest.
Arguments:
- pressure_head: float32 [64, 256, 256], P('crest', 'section'), may hold values from -12 to 12
- zone_ids: int32 [64, 256, 256], P('crest', 'section'), may hold values from 0 to 7
- retention_alpha: float32 [8], replicated, may hold values from 0.5 to 4
- retention_exponent: float32 [8], replicated, may hold values from 1.4 to 2.6
- conductivity: float32 [8], replicated, may hold values from 0.1 to 1
- sent_columns: int32 [128, 128, 64], P(('crest', 'section')), may hold values from 0 to 127
- displacement: float32 [3, 131072], P(None, ('crest', 'section')), may hold values from -0.12 to 0.12
- stress_old: float32 [8, 6, 131072], P(None, None, ('crest', 'section')), may hold values from -6 to 6
- connectivity: int32 [8, 131072], P(None, ('crest', 'section')), may hold values from 0 to 1535, as said below
- shared_nodes: int32 [65536], P(('crest', 'section')), may hold values from 0 to 1023, as said below
- element_zone: int32 [131072], P(('crest', 'section')), may hold values from 0 to 7
- element_slot: int32 [131072], P(('crest', 'section')), may hold values from 0 to 8191
- element_depth: int32 [131072], P(('crest', 'section')), may hold values from 0 to 15
- cohesion: float32 [8], replicated, may hold values from 0.2 to 2
- friction: float32 [8], replicated, may hold values from 0.3 to 0.9
Outputs:
- head_out: float32 [64, 256, 256], P('crest', 'section')
- stress_new: float32 [8, 6, 131072], P(None, None, ('crest', 'section'))
- plastic_release: float32 [8, 131072], P(None, ('crest', 'section'))
- node_forces: float32 [3, 131072], P(None, ('crest', 'section'))
The draws below stay inside these ranges and needn't reach their ends.
Inputs may be any that keep to these rules, and one draw needn't show every extreme that they name: `connectivity`: entries below 1024 are the partition's own nodes; entry 1024 + g names ghost g, the g-th entry of the next partition's shared list; the last partition uses no ghosts. `shared_nodes`: the 512 entries of a partition are distinct nodes of it.
All inputs are finite; a program needn't handle non-finite values.
Results may differ from the reference program's by a relative error of at most 0.0003.
Values sent between devices are 32-bit elements; how exact they have to be, the bound alone decides.
No kernel may reach another device: no remote copies, remote signals or barrier semaphores. Data moves between devices by JAX's collectives and lax.ppermute only.
A program may use at most 64 MiB of HBM per device.

```python
import math
import jax
import jax.numpy as jnp
import numpy as np
from jax import lax

CX = 4
CY = 32
NZ = 256
BAND = 16
SWEEPS = 3
ZONES = 8
E_DEV = 1024
SLOTS = 64
NPART = 128
NX = 64
NY = 256
NODES_DEV = 1024
GHOST = 512
ELEMS = 131072
NODES = 131072
N_CREST = 16
N_SECTION = 8


def draw_connectivity(key, part):
    block_id = jnp.arange(ELEMS, dtype=jnp.int32) // E_DEV
    upper = jnp.where(block_id == NPART - 1, NODES_DEV, NODES_DEV + GHOST).astype(jnp.int32)
    values = jax.random.randint(key, (8, ELEMS), 0, upper[None, :], dtype=jnp.int32)
    values = values.at[0, 0].set(NODES_DEV + GHOST - 1)
    return values.at[1, 0].set(0)


def draw_shared_nodes(key, part):
    keys = jax.random.split(jax.random.fold_in(key, 11), NPART)

    def one_block(block_key):
        return jax.random.permutation(block_key, NODES_DEV)[:GHOST].astype(jnp.int32)
    return jax.vmap(one_block)(keys).reshape(-1)


def set_ends(values, rng, smallest, top_value):
    longest = values.shape.index(max(values.shape))
    spots = []
    for shift in (0, 1):
        where = [jax.random.randint(jax.random.fold_in(rng, axis), (), 0, length) for axis, length in enumerate(values.shape)]
        where[longest] = (where[longest] + shift) % values.shape[longest]
        spots.append(tuple(where))
    return values.at[spots[0]].set(smallest).at[spots[1]].set(top_value)


def shard_levels(key, shape, cuts, smallest, top_value):
    loudness, own = 1.0, jax.random.fold_in(key, 6)
    for position, parts in cuts:
        heights = jnp.exp(jax.random.uniform(jax.random.fold_in(own, position), (parts,), jnp.float32, smallest / len(cuts), top_value / len(cuts)))
        loudness = loudness * jnp.repeat(heights, shape[position] // parts).reshape([-1 if axis == position else 1 for axis in range(len(shape))])
    return loudness


def bell_draw(stream_key, dims, width, limit, pieces=(), kind=jnp.bfloat16):
    factor_of = shard_levels(stream_key, dims, pieces, -0.22, 0.18) if pieces else 1.0
    drawn = jax.random.normal(stream_key, dims, jnp.float32) * width * factor_of
    return jnp.minimum(jnp.maximum(drawn, -limit), limit).astype(kind)


def setup_inputs(seed: int = 0) -> dict:
    key_of = jax.random.split(jax.random.key(seed), 16)
    pressure_head = bell_draw(key_of[0], (NX, NY, NZ), 2.0, 12.0, ((0, 16), (1, 8)), jnp.float32)
    zone_ids = set_ends(jax.random.randint(key_of[1], (NX, NY, NZ), 0, ZONES), jax.random.fold_in(key_of[1], 1), 0, ZONES - 1).astype(jnp.int32)
    retention_alpha = jnp.clip(jnp.exp(jax.random.uniform(key_of[2], (ZONES,), jnp.float32, math.log(0.5), math.log(4.0))), 0.5, 4.0)
    retention_exponent = jnp.clip(jax.random.uniform(key_of[3], (ZONES,), jnp.float32, 1.4, 2.6), 1.4, 2.6)
    conductivity = jnp.clip(jnp.exp(jax.random.uniform(key_of[4], (ZONES,), jnp.float32, math.log(0.1), math.log(1.0))), 0.1, 1.0)
    sent_columns = set_ends(jax.random.randint(key_of[5], (NPART, NPART, SLOTS), 0, CX * CY), jax.random.fold_in(key_of[5], 1), 0, (CX * CY) - 1).astype(jnp.int32)
    displacement = bell_draw(key_of[6], (3, NODES), 0.02, 0.12, ((1, 128),), jnp.float32)
    stress_old = bell_draw(key_of[7], (8, 6, ELEMS), 1.0, 6.0, ((2, 128),), jnp.float32)
    connectivity = draw_connectivity(jax.random.fold_in(key_of[15], 71), 0)
    shared_nodes = draw_shared_nodes(jax.random.fold_in(key_of[15], 71), 0)
    element_zone = set_ends(jax.random.randint(key_of[10], (ELEMS,), 0, ZONES), jax.random.fold_in(key_of[10], 1), 0, ZONES - 1).astype(jnp.int32)
    element_slot = set_ends(jax.random.randint(key_of[11], (ELEMS,), 0, NPART * SLOTS), jax.random.fold_in(key_of[11], 1), 0, (NPART * SLOTS) - 1).astype(jnp.int32)
    element_depth = set_ends(jax.random.randint(key_of[12], (ELEMS,), 0, BAND), jax.random.fold_in(key_of[12], 1), 0, BAND - 1).astype(jnp.int32)
    cohesion = jnp.clip(jnp.exp(jax.random.uniform(key_of[13], (ZONES,), jnp.float32, math.log(0.2), math.log(2.0))), 0.2, 2.0)
    friction = jnp.clip(jax.random.uniform(key_of[14], (ZONES,), jnp.float32, 0.3, 0.9), 0.3, 0.9)
    return {"pressure_head": pressure_head, "zone_ids": zone_ids, "retention_alpha": retention_alpha, "retention_exponent": retention_exponent, "conductivity": conductivity, "sent_columns": sent_columns, "displacement": displacement, "stress_old": stress_old, "connectivity": connectivity, "shared_nodes": shared_nodes, "element_zone": element_zone, "element_slot": element_slot, "element_depth": element_depth, "cohesion": cohesion, "friction": friction}


STORAGE = 0.5
THETA_GAP = 0.35
TIME_STEP = 0.05
REDUCTION = 1.4
YOUNG = 200.0
POISSON = 0.3
NEIGHBOURS = ((1, 0, 0, 0.0), (-1, 0, 0, 0.0), (0, 1, 0, 0.0), (0, -1, 0, 0.0), (0, 0, 1, 1.0), (0, 0, -1, -1.0))

def corner_signs(index):
    return (2 * (index & 1) - 1, 2 * (index >> 1 & 1) - 1, 2 * (index >> 2 & 1) - 1)

def strain_matrix():
    matrix = np.zeros((48, 24))
    inv_root = 1.0 / np.sqrt(3.0)
    for gauss_point in range(8):
        gauss = [value * inv_root for value in corner_signs(gauss_point)]
        row_start = 6 * gauss_point
        for node_corner in range(8):
            sign_x, sign_y, sign_z = corner_signs(node_corner)
            grad_x = 0.25 * sign_x * (1 + gauss[1] * sign_y) * (1 + gauss[2] * sign_z)
            grad_y = 0.25 * sign_y * (1 + gauss[0] * sign_x) * (1 + gauss[2] * sign_z)
            grad_z = 0.25 * sign_z * (1 + gauss[0] * sign_x) * (1 + gauss[1] * sign_y)
            matrix[row_start + 0, node_corner] = grad_x
            matrix[row_start + 1, 8 + node_corner] = grad_y
            matrix[row_start + 2, 16 + node_corner] = grad_z
            matrix[row_start + 3, node_corner] = grad_y
            matrix[row_start + 3, 8 + node_corner] = grad_x
            matrix[row_start + 4, 8 + node_corner] = grad_z
            matrix[row_start + 4, 16 + node_corner] = grad_y
            matrix[row_start + 5, 16 + node_corner] = grad_x
            matrix[row_start + 5, node_corner] = grad_z
    return matrix

def zone_field(zones, values):
    result = jnp.zeros(zones.shape, jnp.float32)
    for zone in range(values.shape[0]):
        result = jnp.where(zones == zone, values[zone], result)
    return result

def van_genuchten(head_now, alpha, expo, cond_sat):
    expo_safe = jnp.where(expo > 0, expo, 2.0)
    m_expo = 1.0 - 1.0 / expo_safe
    scaled = alpha * jnp.maximum(-head_now, 0.0)
    power_n = scaled ** expo_safe
    saturation = (1.0 + power_n) ** (-m_expo)
    inner = 1.0 - (1.0 - saturation ** (1.0 / m_expo)) ** m_expo
    cond = cond_sat * jnp.sqrt(saturation) * inner * inner
    capacity = STORAGE + THETA_GAP * alpha * expo_safe * m_expo * scaled ** (expo_safe - 1.0) * (1.0 + power_n) ** (-m_expo - 1.0)
    return (saturation, cond, capacity)

def sweep_update(head_pad, cond_pad, capacity):
    head_z = jnp.pad(head_pad, ((0, 0), (0, 0), (1, 1)))
    cond_z = jnp.pad(cond_pad, ((0, 0), (0, 0), (1, 1)))
    size_x = head_pad.shape[0] - 2
    size_y = head_pad.shape[1] - 2
    size_z = head_pad.shape[2]
    head_here = head_z[1:1 + size_x, 1:1 + size_y, 1:1 + size_z]
    cond_here = cond_z[1:1 + size_x, 1:1 + size_y, 1:1 + size_z]
    inflow = jnp.zeros_like(head_here)
    for shift_x, shift_y, shift_z, lift in NEIGHBOURS:
        head_there = head_z[1 + shift_x:1 + shift_x + size_x, 1 + shift_y:1 + shift_y + size_y, 1 + shift_z:1 + shift_z + size_z]
        cond_there = cond_z[1 + shift_x:1 + shift_x + size_x, 1 + shift_y:1 + shift_y + size_y, 1 + shift_z:1 + shift_z + size_z]
        inflow = inflow + jnp.sqrt(cond_here * cond_there) * (head_there - head_here + lift)
    return head_here + TIME_STEP * inflow / capacity

def return_map(strain, stress_old, pore, cohesion_e, friction_e):
    lame_first = YOUNG * POISSON / ((1.0 + POISSON) * (1.0 - 2.0 * POISSON))
    modulus = YOUNG / (2.0 * (1.0 + POISSON))
    volume = strain[:, 0] + strain[:, 1] + strain[:, 2]
    normals = [stress_old[:, i] + lame_first * volume + 2.0 * modulus * strain[:, i] + pore for i in range(3)]
    shears = [stress_old[:, i] + modulus * strain[:, i] for i in range(3, 6)]
    mean_stress = (normals[0] + normals[1] + normals[2]) / 3.0
    devs = [value - mean_stress for value in normals]
    deviator = jnp.sqrt(0.5 * (devs[0] ** 2 + devs[1] ** 2 + devs[2] ** 2) + shears[0] ** 2 + shears[1] ** 2 + shears[2] ** 2)
    tan_red = friction_e / REDUCTION
    cos_red = 1.0 / jnp.sqrt(1.0 + tan_red * tan_red)
    sin_red = tan_red * cos_red
    denom = jnp.sqrt(3.0) * (3.0 - sin_red)
    slope = 6.0 * sin_red / denom
    bound_value = 6.0 * (cohesion_e / REDUCTION) * cos_red / denom
    allow = jnp.maximum(bound_value - slope * mean_stress, 0.0)
    yielded = deviator > allow
    scale = jnp.where(yielded, allow / jnp.where(yielded, deviator, 1.0), 1.0)
    new_parts = [mean_stress + scale * devs[i] - pore for i in range(3)] + [scale * shears[i] for i in range(3)]
    return (jnp.stack(new_parts, axis=1), (1.0 - scale) * deviator)

def reference(pressure_head, zone_ids, retention_alpha, retention_exponent, conductivity, sent_columns, displacement, stress_old, connectivity, shared_nodes, element_zone, element_slot, element_depth, cohesion, friction):
    alpha_field = zone_field(zone_ids, retention_alpha)
    expo_field = zone_field(zone_ids, retention_exponent)
    sat_field = zone_field(zone_ids, conductivity)
    head_now = pressure_head
    plan_pad = ((1, 1), (1, 1), (0, 0))
    for sweep in range(SWEEPS):
        saturation, cond, capacity = van_genuchten(head_now, alpha_field, expo_field, sat_field)
        head_now = sweep_update(jnp.pad(head_now, plan_pad), jnp.pad(cond, plan_pad), capacity)
    saturation = van_genuchten(head_now, alpha_field, expo_field, sat_field)[0]
    pore_field = saturation * head_now

    def to_blocks(field):
        return field.reshape(N_CREST, CX, N_SECTION, CY, NZ).transpose(0, 2, 1, 3, 4).reshape(NPART, CX * CY, NZ)
    partition = (jnp.arange(ELEMS, dtype=jnp.int32) // E_DEV).astype(jnp.int32)
    source = element_slot // SLOTS
    within = element_slot % SLOTS
    column = sent_columns[source, partition, within]
    depth_index = (partition * BAND % NZ + element_depth).astype(jnp.int32)
    pore = to_blocks(pore_field)[source, column, depth_index]
    owned = connectivity < NODES_DEV
    following = jnp.minimum(partition + 1, NPART - 1)[None, :]
    ghost_slot = jnp.clip(connectivity - NODES_DEV, 0, GHOST - 1)
    shared_table = shared_nodes.reshape(NPART, GHOST)
    global_index = jnp.where(owned, partition[None, :] * NODES_DEV + connectivity, following * NODES_DEV + shared_table[following, ghost_slot]).astype(jnp.int32)
    strain_rows = jnp.asarray(strain_matrix(), jnp.float32)
    force_rows = jnp.asarray(strain_matrix().T * 0.125, jnp.float32)
    elem_disp = displacement[:, global_index].reshape(24, ELEMS)
    strain = jnp.dot(strain_rows, elem_disp, precision=lax.Precision.HIGHEST).reshape(8, 6, ELEMS)
    cohesion_e = zone_field(element_zone, cohesion)
    friction_e = zone_field(element_zone, friction)
    stress_new, release = return_map(strain, stress_old, pore, cohesion_e, friction_e)
    elem_force = jnp.dot(force_rows, stress_new.reshape(48, ELEMS), precision=lax.Precision.HIGHEST).reshape(3, 8 * ELEMS)
    flat_index = global_index.reshape(-1)
    node_forces = jnp.stack([jax.ops.segment_sum(elem_force[comp], flat_index, num_segments=NODES) for comp in range(3)])
    return (head_now, stress_new, release, node_forces)
```

```python
import jax
import jax.numpy as jnp
import numpy as np
from jax import lax
from jax.experimental import pallas as pl
from jax.experimental.pallas import tpu as pltpu
from jax.sharding import PartitionSpec as P

BAND = 16
SWEEPS = 3
WIDE = 3

STORAGE = 0.5
THETA_GAP = 0.35
TIME_STEP = 0.05
REDUCTION = 1.4
YOUNG = 200.0
POISSON = 0.3

AXES = ("crest", "section")
VMEM_LIMIT = 48 * 1024 * 1024


def corner_signs(index):
    return (2 * (index & 1) - 1, 2 * (index >> 1 & 1) - 1, 2 * (index >> 2 & 1) - 1)


def strain_matrix():
    matrix = np.zeros((48, 24))
    inv_root = 1.0 / np.sqrt(3.0)
    for gauss_point in range(8):
        gauss = [value * inv_root for value in corner_signs(gauss_point)]
        row_start = 6 * gauss_point
        for node_corner in range(8):
            sign_x, sign_y, sign_z = corner_signs(node_corner)
            grad_x = 0.25 * sign_x * (1 + gauss[1] * sign_y) * (1 + gauss[2] * sign_z)
            grad_y = 0.25 * sign_y * (1 + gauss[0] * sign_x) * (1 + gauss[2] * sign_z)
            grad_z = 0.25 * sign_z * (1 + gauss[0] * sign_x) * (1 + gauss[1] * sign_y)
            matrix[row_start + 0, node_corner] = grad_x
            matrix[row_start + 1, 8 + node_corner] = grad_y
            matrix[row_start + 2, 16 + node_corner] = grad_z
            matrix[row_start + 3, node_corner] = grad_y
            matrix[row_start + 3, 8 + node_corner] = grad_x
            matrix[row_start + 4, 8 + node_corner] = grad_z
            matrix[row_start + 4, 16 + node_corner] = grad_y
            matrix[row_start + 5, 16 + node_corner] = grad_x
            matrix[row_start + 5, node_corner] = grad_z
    return matrix


def component_major():
    order = [6 * gauss_point + comp for comp in range(6) for gauss_point in range(8)]
    return strain_matrix()[order]


def take_lanes(row, lanes):
    return jnp.take_along_axis(jnp.broadcast_to(row, lanes.shape), lanes, axis=1, mode="promise_in_bounds")


def pick(values_ref, index, first=0):
    lane = lax.broadcasted_iota(jnp.int32, (8, 128), 1)
    table = jnp.zeros((8, 128), jnp.float32)
    for zone in range(values_ref.shape[0]):
        table = jnp.where(lane == first + zone, values_ref[zone], table)
    return table if index is None else take_lanes(table, index)


def pack_section(head_ref, zone_ref, disp_ref, shared_ref, forward_ref, backward_ref):
    rows = head_ref.shape[1]
    planes = head_ref.shape[0]
    for x in range(planes):
        at = WIDE * x
        forward_ref[at : at + WIDE, :] = head_ref[x, rows - WIDE : rows, :]
        backward_ref[at : at + WIDE, :] = head_ref[x, 0:WIDE, :]
        at += WIDE * planes
        forward_ref[at : at + WIDE, :] = zone_ref[x, rows - WIDE : rows, :].astype(jnp.float32) + 1.0
        backward_ref[at : at + WIDE, :] = zone_ref[x, 0:WIDE, :].astype(jnp.float32) + 1.0
    index = shared_ref[...]
    index = jnp.concatenate([index, index], axis=0)
    lanes, segment = index & 127, index >> 7
    for comp in range(3):
        found = jnp.zeros((8, 128), jnp.float32)
        for s in range(disp_ref.shape[1] // 128):
            row = disp_ref[comp : comp + 1, s * 128 : (s + 1) * 128]
            found = jnp.where(segment == s, take_lanes(row, lanes), found)
        for s in range(4):
            at = 2 * WIDE * planes + 2 * comp + s // 2
            backward_ref[at : at + 1, (s % 2) * 128 : (s % 2 + 1) * 128] = found[s : s + 1]
    backward_ref[30:32, :] = jnp.zeros((2, 256), jnp.float32)


def pack_crest(place_ref, head_ref, zone_ref, before_ref, after_ref, low_ref, high_ref):
    planes, rows = head_ref.shape[0], head_ref.shape[1]
    inside = jnp.where(place_ref[0] < place_ref[1] - 1, 1.0, 0.0)
    for x in range(planes):
        for field in range(2):
            at = field * WIDE * planes + WIDE * x
            own = head_ref[x] if field == 0 else zone_ref[x].astype(jnp.float32) + 1.0
            tail = jnp.concatenate(
                [
                    after_ref[at : at + WIDE, :] * inside,
                    jnp.zeros((2, own.shape[1]), jnp.float32),
                    before_ref[at : at + WIDE, :],
                ],
                axis=0,
            )
            if x < WIDE:
                low_ref[field, x, 0:rows, :] = own
                low_ref[field, x, rows : rows + 8, :] = tail
            if x >= planes - WIDE:
                high_ref[field, x - planes + WIDE, 0:rows, :] = own
                high_ref[field, x - planes + WIDE, rows : rows + 8, :] = tail


def seepage(
    alpha_ref,
    expo_ref,
    ks_ref,
    low_ref,
    high_ref,
    before_ref,
    after_ref,
    wanted_ref,
    head_ref,
    out_ref,
    h,
    alpha_f,
    expo_f,
    m_f,
    root_f,
    r_f,
    cap_f,
    table,
    deep,
    index,
):
    planes = head_ref.shape[0]
    rows = head_ref.shape[1]
    total = planes + 2 * WIDE
    height, depth = h.shape[1], h.shape[2]
    lane8 = lax.broadcasted_iota(jnp.int32, (8, 128), 1)
    alpha_t = pick(alpha_ref, None, 1)
    expo_t = pick(expo_ref, None, 1)
    expo_t = jnp.where(expo_t > 0, expo_t, 2.0)
    m_t = 1.0 - 1.0 / expo_t
    root_t = jnp.sqrt(pick(ks_ref, None, 1))

    def fields(x, source, plane):
        h[x] = source[0, plane]
        for row in range(0, height, 8):
            for col in range(0, depth, 128):
                zone = source[1, plane, row : row + 8, col : col + 128].astype(jnp.int32)
                alpha_f[x, row : row + 8, col : col + 128] = take_lanes(alpha_t, zone)
                expo_f[x, row : row + 8, col : col + 128] = take_lanes(expo_t, zone)
                m_f[x, row : row + 8, col : col + 128] = take_lanes(m_t, zone)
                root_f[x, row : row + 8, col : col + 128] = take_lanes(root_t, zone)

    @pl.loop(0, WIDE)
    def _(x):
        fields(x, before_ref, x)
        fields(WIDE + x, low_ref, x)
        fields(WIDE + planes + x, after_ref, x)

    fields(2 * WIDE, high_ref, WIDE - 1)

    def log_terms(x):
        scaled = alpha_f[x] * jnp.maximum(-h[x], 0.0)
        expo = expo_f[x]
        log_a = jnp.log(jnp.maximum(scaled, 1e-30))
        log_p = expo * log_a
        log_1p = jnp.log(1.0 + jnp.exp(log_p))
        return expo, log_a, log_p, log_1p

    def retention(x):
        expo, log_a, log_p, log_1p = log_terms(x)
        m = m_f[x]
        inner = 1.0 - jnp.exp(m * (log_p - log_1p))
        r_f[x] = root_f[x] * jnp.exp(-0.25 * m * log_1p) * inner
        power = jnp.exp(log_p - log_a - (m + 1.0) * log_1p)
        cap_f[x] = TIME_STEP / (STORAGE + THETA_GAP * alpha_f[x] * (expo - 1.0) * power)

    inner_z = lax.broadcasted_iota(jnp.int32, (height, depth), 1) < depth - 1

    def face(x):
        return r_f[x] * r_f[x + 1] * (h[x + 1] - h[x])

    for sweep in range(SWEEPS):

        @pl.loop(sweep, total - sweep)
        def _(x):
            retention(x)

        def update(x, came):
            here, r = h[x], r_f[x]
            goes = face(x)
            flux_y = r * pltpu.roll(r, height - 1, 0) * (pltpu.roll(here, height - 1, 0) - here)
            flux_z = r * pltpu.roll(r, depth - 1, 1) * (pltpu.roll(here, depth - 1, 1) - here + 1.0)
            flux_z = jnp.where(inner_z, flux_z, 0.0)
            inflow = goes - came + (flux_y - pltpu.roll(flux_y, 1, 0)) + (flux_z - pltpu.roll(flux_z, 1, 1))
            h[x] = here + cap_f[x] * inflow
            return goes

        lax.fori_loop(sweep + 1, total - sweep - 1, update, face(sweep))

    for x in range(planes):
        _, _, _, log_1p = log_terms(WIDE + x)
        here = h[WIDE + x][0:rows]
        head_ref[x] = here
        table[x * rows : (x + 1) * rows, :] = jnp.exp(-m_f[WIDE + x] * log_1p)[0:rows] * here
    deep[...] = table[...].T
    index[:, 0:64] = wanted_ref[...]
    index[:, 64:128] = wanted_ref[...]
    bands = depth // BAND

    @pl.loop(0, bands)
    def _(b):
        upper = deep[pl.ds(pl.multiple_of(b * BAND, 8), 8), :]
        lower = deep[pl.ds(pl.multiple_of(b * BAND + 8, 8), 8), :]
        for group in range(wanted_ref.shape[0] // bands):
            d = group * bands + b
            columns = jnp.broadcast_to(index[pl.ds(d, 1), :], (8, 128))
            out_ref[d] = jnp.where(lane8 < 64, take_lanes(upper, columns), take_lanes(lower, columns))


def trial_state(matrix_ref, disp_ref, ghost_ref, conn_ref, stress_ref, trial_ref, nodes, corners):
    for comp in range(3):
        for s in range(8):
            nodes[comp * 12 + s : comp * 12 + s + 1, :] = disp_ref[comp : comp + 1, s * 128 : (s + 1) * 128]
        for s in range(4):
            at = 24 + 2 * comp + s // 2
            nodes[comp * 12 + 8 + s : comp * 12 + 9 + s, :] = ghost_ref[at : at + 1, (s % 2) * 128 : (s % 2 + 1) * 128]
    elems = conn_ref.shape[1]

    @pl.loop(0, elems, step=128)
    def _(e):
        e = pl.multiple_of(e, 128)
        index = conn_ref[:, pl.ds(e, 128)]
        lanes, segment = index & 127, index >> 7
        found = [jnp.zeros((8, 128), jnp.float32) for _ in range(3)]
        for s in range(12):
            here = segment == s
            for comp in range(3):
                row = nodes[comp * 12 + s : comp * 12 + s + 1, :]
                found[comp] = jnp.where(here, take_lanes(row, lanes), found[comp])
        for comp in range(3):
            corners[comp * 8 : comp * 8 + 8, pl.ds(e, 128)] = found[comp]

    strain = jnp.dot(
        matrix_ref[...], corners[...], precision=lax.Precision.HIGHEST, preferred_element_type=jnp.float32
    )
    lame_first = YOUNG * POISSON / ((1.0 + POISSON) * (1.0 - 2.0 * POISSON))
    modulus = YOUNG / (2.0 * (1.0 + POISSON))
    part = [strain[8 * i : 8 * i + 8] for i in range(6)]
    volume = lame_first * (part[0] + part[1] + part[2])
    normals = [stress_ref[:, i, :] + volume + 2.0 * modulus * part[i] for i in range(3)]
    shears = [stress_ref[:, i, :] + modulus * part[i] for i in range(3, 6)]
    mean = (normals[0] + normals[1] + normals[2]) * (1.0 / 3.0)
    devs = [value - mean for value in normals]
    trial_ref[6] = mean
    trial_ref[7] = jnp.sqrt(
        0.5 * (devs[0] ** 2 + devs[1] ** 2 + devs[2] ** 2) + shears[0] ** 2 + shears[1] ** 2 + shears[2] ** 2
    )
    for i in range(3):
        trial_ref[i] = devs[i]
        trial_ref[3 + i] = shears[i]


def halves(value):
    high = value.astype(jnp.bfloat16).astype(jnp.float32)
    return high, value - high


def final_state(
    cohesion_ref,
    friction_ref,
    matrix_ref,
    band_ref,
    slot_ref,
    depth_ref,
    zone_ref,
    trial_ref,
    conn_ref,
    stress_ref,
    release_ref,
    own_ref,
    ghost_ref,
    force_h,
    force_l,
):
    slot, depth = slot_ref[...], depth_ref[...]
    wanted_row = (slot >> 6) * 8 + (depth & 7)
    wanted_lane = (depth >> 3) * 64 + (slot & 63)

    def look(at, found):
        at = pl.multiple_of(at * 8, 8)
        for row in range(8):
            value = take_lanes(band_ref[pl.ds(at + row, 1), :], wanted_lane)
            found = jnp.where(wanted_row == at + row, value, found)
        return found

    pore = lax.fori_loop(0, band_ref.shape[0] // 8, look, jnp.zeros((8, 128), jnp.float32))
    zone = zone_ref[...]
    tan_red = pick(friction_ref, zone) * (1.0 / REDUCTION)
    cos_red = 1.0 / jnp.sqrt(1.0 + tan_red * tan_red)
    sin_red = tan_red * cos_red
    common = 6.0 / (np.sqrt(3.0).astype(np.float32) * (3.0 - sin_red))
    slope = common * sin_red
    bound = common * (pick(cohesion_ref, zone) * (1.0 / REDUCTION)) * cos_red

    def spread(value):
        return jnp.concatenate([value[r : r + 1] for r in range(8)], axis=1)

    allow = jnp.maximum(spread(bound - slope * pore) - spread(slope) * trial_ref[6], 0.0)
    deviator = trial_ref[7]
    yielded = deviator > allow
    scale = jnp.where(yielded, allow / jnp.where(yielded, deviator, 1.0), 1.0)
    release_ref[...] = (1.0 - scale) * deviator
    mean = trial_ref[6]
    parts = [mean + scale * trial_ref[i] for i in range(3)] + [scale * trial_ref[3 + i] for i in range(3)]
    for i in range(6):
        stress_ref[:, i, :] = parts[i]
    force = jnp.dot(
        matrix_ref[...],
        jnp.concatenate(parts, axis=0),
        precision=lax.Precision.HIGHEST,
        preferred_element_type=jnp.float32,
    )
    high, low = halves(force)
    force_h[...] = high
    force_l[...] = low
    elems = conn_ref.shape[1]
    in_segment = lax.broadcasted_iota(jnp.int32, (16, elems), 0)
    in_lane = lax.broadcasted_iota(jnp.int32, (128, elems), 0)

    def gathered(corner, total):
        node = conn_ref[pl.ds(corner, 1), :]
        here = jnp.broadcast_to(node >> 7, in_segment.shape) == in_segment
        rows = []
        for source in (force_h, force_l):
            for comp in range(3):
                value = jnp.broadcast_to(source[pl.ds(comp * 8 + corner, 1), :], in_segment.shape)
                rows.append(jnp.where(here, value, 0.0))
        left = jnp.concatenate(rows, axis=0).astype(jnp.bfloat16)
        right = jnp.where(jnp.broadcast_to(node & 127, in_lane.shape) == in_lane, 1.0, 0.0).astype(jnp.bfloat16)
        return total + lax.dot_general(left, right, (((1,), (1,)), ((), ())), preferred_element_type=jnp.float32)

    total = lax.fori_loop(0, 8, gathered, jnp.zeros((96, 128), jnp.float32))
    total = total[0:48] + total[48:96]
    for comp in range(3):
        own_ref[comp * 8 : comp * 8 + 8, :] = total[comp * 16 : comp * 16 + 8]
        ghost_ref[comp * 4 : comp * 4 + 4, :] = total[comp * 16 + 8 : comp * 16 + 12]


def add_returned(own_ref, ghost_ref, shared_ref, out_ref):
    shared = shared_ref[...]
    in_lane = lax.broadcasted_iota(jnp.int32, (128, 128), 0)
    in_segment = lax.broadcasted_iota(jnp.int32, (8, 128), 0)
    lefts, rights = [], []
    for s in range(4):
        node = shared[s : s + 1]
        rights.append(jnp.where(jnp.broadcast_to(node & 127, in_lane.shape) == in_lane, 1.0, 0.0))
        here = jnp.broadcast_to(node >> 7, in_segment.shape) == in_segment
        rows = []
        for comp in range(3):
            value = ghost_ref[comp * 4 + s : comp * 4 + s + 1, :]
            high, low = halves(value)
            for piece in (high, low):
                rows.append(jnp.where(here, jnp.broadcast_to(piece, in_segment.shape), 0.0))
        lefts.append(jnp.concatenate(rows, axis=0))
    left = jnp.concatenate(lefts, axis=1).astype(jnp.bfloat16)
    right = jnp.concatenate(rights, axis=1).astype(jnp.bfloat16)
    added = lax.dot_general(left, right, (((1,), (1,)), ((), ())), preferred_element_type=jnp.float32)
    for comp in range(3):
        total = own_ref[comp * 8 : comp * 8 + 8, :] + added[comp * 16 : comp * 16 + 8] + added[comp * 16 + 8 : comp * 16 + 16]
        for s in range(8):
            out_ref[comp : comp + 1, s * 128 : (s + 1) * 128] = total[s : s + 1]


VM = pl.BlockSpec(memory_space=pltpu.VMEM)
SM = pl.BlockSpec(memory_space=pltpu.SMEM)


def call(body, specs, outs, scratch, name):
    return pl.pallas_call(
        body,
        in_specs=specs,
        out_specs=tuple(VM for _ in outs),
        out_shape=tuple(jax.ShapeDtypeStruct(shape, jnp.float32) for shape in outs),
        scratch_shapes=scratch,
        compiler_params=pltpu.CompilerParams(vmem_limit_bytes=VMEM_LIMIT),
        name=name,
    )


def steps(count, by):
    return [(i, i + by) for i in range(count) if 0 <= i + by < count]


def per_device(
    pressure_head,
    zone_ids,
    retention_alpha,
    retention_exponent,
    conductivity,
    sent_columns,
    displacement,
    stress_old,
    connectivity,
    shared_nodes,
    element_zone,
    element_slot,
    element_depth,
    cohesion,
    friction,
):
    crest, section = (lax.axis_size(axis) for axis in AXES)
    devices = crest * section
    planes, rows, depth = pressure_head.shape
    height = rows + 8
    elems = connectivity.shape[1]
    nodes = displacement.shape[1]
    shared = shared_nodes.reshape(4, 128)
    place = jnp.stack([lax.axis_index("section"), jnp.int32(section)])

    forward, backward = call(
        pack_section, [VM] * 4, [(2 * WIDE * planes, depth), (32, depth)], [], "pack_section"
    )(pressure_head, zone_ids, displacement, shared)
    before = lax.ppermute(forward, "section", steps(section, 1))
    after = lax.ppermute(backward, AXES, steps(devices, -1))

    edge = (2, WIDE, height, depth)
    low, high = call(pack_crest, [SM] + [VM] * 4, [edge, edge], [], "pack_crest")(
        place, pressure_head, zone_ids, before, after
    )
    west = lax.ppermute(high, "crest", steps(crest, 1))
    east = lax.ppermute(low, "crest", steps(crest, -1))

    matrix = component_major()
    (trial,) = call(
        trial_state,
        [VM] * 5,
        [(8, 8, elems)],
        [pltpu.VMEM((40, 128), jnp.float32), pltpu.VMEM((24, elems), jnp.float32)],
        "trial_state",
    )(jnp.asarray(matrix, jnp.float32), displacement, after, connectivity, stress_old)

    total = planes + 2 * WIDE
    field = pltpu.VMEM((total, height, depth), jnp.float32)
    head_out, outgoing = call(
        seepage,
        [SM] * 3 + [VM] * 5,
        [pressure_head.shape, (devices, 8, 128)],
        [field] * 7
        + [
            pltpu.VMEM((planes * rows, depth), jnp.float32),
            pltpu.VMEM((depth, planes * rows), jnp.float32),
            pltpu.VMEM((devices, 128), jnp.int32),
        ],
        "seepage",
    )(retention_alpha, retention_exponent, conductivity, low, high, west, east, sent_columns[0])
    incoming = lax.all_to_all(outgoing, AXES, split_axis=0, concat_axis=0, tiled=True)

    stress_new, release, own, ghost = call(
        final_state,
        [SM] * 2 + [VM] * 7,
        [stress_old.shape, (8, elems), (24, 128), (12, 128)],
        [pltpu.VMEM((24, elems), jnp.float32)] * 2,
        "final_state",
    )(
        cohesion,
        friction,
        jnp.asarray(matrix.T * 0.125, jnp.float32),
        incoming.reshape(devices * 8, 128),
        element_slot.reshape(8, 128),
        element_depth.reshape(8, 128),
        element_zone.reshape(8, 128),
        trial,
        connectivity,
    )
    returned = lax.ppermute(ghost, AXES, steps(devices, 1))
    (node_forces,) = call(add_returned, [VM] * 3, [(3, nodes)], [], "add_returned")(own, returned, shared)
    return (head_out, stress_new, release, node_forces)


def solution(mesh):
    return jax.shard_map(
        per_device,
        mesh=mesh,
        in_specs=(
            P("crest", "section", None),
            P("crest", "section", None),
            P(),
            P(),
            P(),
            P(("crest", "section"), None, None),
            P(None, ("crest", "section")),
            P(None, None, ("crest", "section")),
            P(None, ("crest", "section")),
            P(("crest", "section")),
            P(("crest", "section")),
            P(("crest", "section")),
            P(("crest", "section")),
            P(),
            P(),
        ),
        out_specs=(
            P("crest", "section", None),
            P(None, None, ("crest", "section")),
            P(None, ("crest", "section")),
            P(None, ("crest", "section")),
        ),
        check_vma=False,
    )
```

```python
import jax
import jax.numpy as jnp
import numpy as np
from jax import lax
from jax.experimental import pallas as pl
from jax.experimental.pallas import tpu as pltpu
from jax.sharding import PartitionSpec as P

BAND = 16
SWEEPS = 3
WIDE = 3

STORAGE = 0.5
THETA_GAP = 0.35
TIME_STEP = 0.05
REDUCTION = 1.4
YOUNG = 200.0
POISSON = 0.3

AXES = ("crest", "section")
VMEM_LIMIT = 48 * 1024 * 1024


def corner_signs(index):
    return (2 * (index & 1) - 1, 2 * (index >> 1 & 1) - 1, 2 * (index >> 2 & 1) - 1)


def strain_matrix():
    matrix = np.zeros((48, 24))
    inv_root = 1.0 / np.sqrt(3.0)
    for gauss_point in range(8):
        gauss = [value * inv_root for value in corner_signs(gauss_point)]
        row_start = 6 * gauss_point
        for node_corner in range(8):
            sign_x, sign_y, sign_z = corner_signs(node_corner)
            grad_x = 0.25 * sign_x * (1 + gauss[1] * sign_y) * (1 + gauss[2] * sign_z)
            grad_y = 0.25 * sign_y * (1 + gauss[0] * sign_x) * (1 + gauss[2] * sign_z)
            grad_z = 0.25 * sign_z * (1 + gauss[0] * sign_x) * (1 + gauss[1] * sign_y)
            matrix[row_start + 0, node_corner] = grad_x
            matrix[row_start + 1, 8 + node_corner] = grad_y
            matrix[row_start + 2, 16 + node_corner] = grad_z
            matrix[row_start + 3, node_corner] = grad_y
            matrix[row_start + 3, 8 + node_corner] = grad_x
            matrix[row_start + 4, 8 + node_corner] = grad_z
            matrix[row_start + 4, 16 + node_corner] = grad_y
            matrix[row_start + 5, 16 + node_corner] = grad_x
            matrix[row_start + 5, node_corner] = grad_z
    return matrix


def component_major():
    order = [6 * gauss_point + comp for comp in range(6) for gauss_point in range(8)]
    return strain_matrix()[order]


def take_lanes(row, lanes):
    return jnp.take_along_axis(jnp.broadcast_to(row, lanes.shape), lanes, axis=1, mode="promise_in_bounds")


def pick(values_ref, index, first=0):
    lane = lax.broadcasted_iota(jnp.int32, (8, 128), 1)
    table = jnp.zeros((8, 128), jnp.float32)
    for zone in range(values_ref.shape[0]):
        table = jnp.where(lane == first + zone, values_ref[zone], table)
    return table if index is None else take_lanes(table, index)


def pack_section(head_ref, zone_ref, disp_ref, shared_ref, forward_ref, backward_ref):
    rows = head_ref.shape[1]
    planes = head_ref.shape[0]
    for x in range(planes):
        at = WIDE * x
        forward_ref[at : at + WIDE, :] = head_ref[x, rows - WIDE : rows, :]
        backward_ref[at : at + WIDE, :] = head_ref[x, 0:WIDE, :]
        at += WIDE * planes
        forward_ref[at : at + WIDE, :] = zone_ref[x, rows - WIDE : rows, :].astype(jnp.float32) + 1.0
        backward_ref[at : at + WIDE, :] = zone_ref[x, 0:WIDE, :].astype(jnp.float32) + 1.0
    index = shared_ref[...]
    index = jnp.concatenate([index, index], axis=0)
    lanes, segment = index & 127, index >> 7
    for comp in range(3):
        found = jnp.zeros((8, 128), jnp.float32)
        for s in range(disp_ref.shape[1] // 128):
            row = disp_ref[comp : comp + 1, s * 128 : (s + 1) * 128]
            found = jnp.where(segment == s, take_lanes(row, lanes), found)
        for s in range(4):
            at = 2 * WIDE * planes + 2 * comp + s // 2
            backward_ref[at : at + 1, (s % 2) * 128 : (s % 2 + 1) * 128] = found[s : s + 1]
    backward_ref[30:32, :] = jnp.zeros((2, 256), jnp.float32)


def pack_crest(place_ref, head_ref, zone_ref, before_ref, after_ref, low_ref, high_ref):
    planes, rows = head_ref.shape[0], head_ref.shape[1]
    inside = jnp.where(place_ref[0] < place_ref[1] - 1, 1.0, 0.0)
    for x in range(planes):
        for field in range(2):
            at = field * WIDE * planes + WIDE * x
            own = head_ref[x] if field == 0 else zone_ref[x].astype(jnp.float32) + 1.0
            tail = jnp.concatenate(
                [
                    after_ref[at : at + WIDE, :] * inside,
                    jnp.zeros((2, own.shape[1]), jnp.float32),
                    before_ref[at : at + WIDE, :],
                ],
                axis=0,
            )
            if x < WIDE:
                low_ref[field, x, 0:rows, :] = own
                low_ref[field, x, rows : rows + 8, :] = tail
            if x >= planes - WIDE:
                high_ref[field, x - planes + WIDE, 0:rows, :] = own
                high_ref[field, x - planes + WIDE, rows : rows + 8, :] = tail


def seepage(
    alpha_ref,
    expo_ref,
    ks_ref,
    low_ref,
    high_ref,
    before_ref,
    after_ref,
    wanted_ref,
    head_ref,
    out_ref,
    h,
    alpha_f,
    expo_f,
    m_f,
    root_f,
    r_f,
    cap_f,
    table,
    deep,
    index,
):
    planes = head_ref.shape[0]
    rows = head_ref.shape[1]
    total = planes + 2 * WIDE
    height, depth = h.shape[1], h.shape[2]
    lane8 = lax.broadcasted_iota(jnp.int32, (8, 128), 1)
    zones = alpha_ref.shape[0]
    alpha_t = [jnp.full((8, depth), alpha_ref[z], jnp.float32) for z in range(zones)]
    expo_t = [jnp.full((8, depth), expo_ref[z], jnp.float32) for z in range(zones)]
    expo_t = [jnp.where(value > 0, value, 2.0) for value in expo_t]
    m_t = [1.0 - 1.0 / value for value in expo_t]
    root_t = [jnp.sqrt(jnp.full((8, depth), ks_ref[z], jnp.float32)) for z in range(zones)]

    def fields(x, source, plane):
        h[x] = source[0, plane]
        for row in range(0, height, 8):
            zone = source[1, plane, row : row + 8, :].astype(jnp.int32) - 1
            bits = [(zone & (1 << bit)) != 0 for bit in range(3)]

            def choose(values):
                for bit in bits:
                    values = [jnp.where(bit, values[i + 1], values[i]) for i in range(0, len(values), 2)]
                return values[0]

            alpha_f[x, row : row + 8, :] = choose(alpha_t)
            expo_f[x, row : row + 8, :] = choose(expo_t)
            m_f[x, row : row + 8, :] = choose(m_t)
            root_f[x, row : row + 8, :] = jnp.where(zone >= 0, choose(root_t), 0.0)

    @pl.loop(0, WIDE)
    def _(x):
        fields(x, before_ref, x)
        fields(WIDE + x, low_ref, x)
        fields(WIDE + planes + x, after_ref, x)

    fields(2 * WIDE, high_ref, WIDE - 1)

    def log_terms(x):
        scaled = alpha_f[x] * jnp.maximum(-h[x], 0.0)
        expo = expo_f[x]
        log_a = jnp.log(jnp.maximum(scaled, 1e-30))
        log_p = expo * log_a
        log_1p = jnp.log(1.0 + jnp.exp(log_p))
        return expo, log_a, log_p, log_1p

    def retention(x):
        expo, log_a, log_p, log_1p = log_terms(x)
        m = m_f[x]
        inner = 1.0 - jnp.exp(m * (log_p - log_1p))
        r_f[x] = root_f[x] * jnp.exp(-0.25 * m * log_1p) * inner
        power = jnp.exp(log_p - log_a - (m + 1.0) * log_1p)
        cap_f[x] = TIME_STEP / (STORAGE + THETA_GAP * alpha_f[x] * (expo - 1.0) * power)

    inner_z = lax.broadcasted_iota(jnp.int32, (height, depth), 1) < depth - 1

    def face(x):
        return r_f[x] * r_f[x + 1] * (h[x + 1] - h[x])

    for sweep in range(SWEEPS):

        @pl.loop(sweep, total - sweep)
        def _(x):
            retention(x)

        def update(x, came):
            here, r = h[x], r_f[x]
            goes = face(x)
            flux_y = r * pltpu.roll(r, height - 1, 0) * (pltpu.roll(here, height - 1, 0) - here)
            flux_z = r * pltpu.roll(r, depth - 1, 1) * (pltpu.roll(here, depth - 1, 1) - here + 1.0)
            flux_z = jnp.where(inner_z, flux_z, 0.0)
            inflow = goes - came + (flux_y - pltpu.roll(flux_y, 1, 0)) + (flux_z - pltpu.roll(flux_z, 1, 1))
            h[x] = here + cap_f[x] * inflow
            return goes

        lax.fori_loop(sweep + 1, total - sweep - 1, update, face(sweep))

    for x in range(planes):
        _, _, _, log_1p = log_terms(WIDE + x)
        here = h[WIDE + x][0:rows]
        head_ref[x] = here
        table[x * rows : (x + 1) * rows, :] = jnp.exp(-m_f[WIDE + x] * log_1p)[0:rows] * here
    deep[...] = table[...].T
    index[:, 0:64] = wanted_ref[...]
    index[:, 64:128] = wanted_ref[...]
    bands = depth // BAND

    @pl.loop(0, bands)
    def _(b):
        upper = deep[pl.ds(pl.multiple_of(b * BAND, 8), 8), :]
        lower = deep[pl.ds(pl.multiple_of(b * BAND + 8, 8), 8), :]
        for group in range(wanted_ref.shape[0] // bands):
            d = group * bands + b
            columns = jnp.broadcast_to(index[pl.ds(d, 1), :], (8, 128))
            out_ref[d] = jnp.where(lane8 < 64, take_lanes(upper, columns), take_lanes(lower, columns))


def trial_state(matrix_ref, disp_ref, ghost_ref, conn_ref, stress_ref, trial_ref, nodes, corners):
    for comp in range(3):
        for s in range(8):
            nodes[comp * 12 + s : comp * 12 + s + 1, :] = disp_ref[comp : comp + 1, s * 128 : (s + 1) * 128]
        for s in range(4):
            at = 24 + 2 * comp + s // 2
            nodes[comp * 12 + 8 + s : comp * 12 + 9 + s, :] = ghost_ref[at : at + 1, (s % 2) * 128 : (s % 2 + 1) * 128]
    elems = conn_ref.shape[1]

    @pl.loop(0, elems, step=128)
    def _(e):
        e = pl.multiple_of(e, 128)
        index = conn_ref[:, pl.ds(e, 128)]
        lanes, segment = index & 127, index >> 7
        found = [jnp.zeros((8, 128), jnp.float32) for _ in range(3)]
        for s in range(12):
            here = segment == s
            for comp in range(3):
                row = nodes[comp * 12 + s : comp * 12 + s + 1, :]
                found[comp] = jnp.where(here, take_lanes(row, lanes), found[comp])
        for comp in range(3):
            corners[comp * 8 : comp * 8 + 8, pl.ds(e, 128)] = found[comp]

    strain = jnp.dot(
        matrix_ref[...], corners[...], precision=lax.Precision.HIGHEST, preferred_element_type=jnp.float32
    )
    lame_first = YOUNG * POISSON / ((1.0 + POISSON) * (1.0 - 2.0 * POISSON))
    modulus = YOUNG / (2.0 * (1.0 + POISSON))
    part = [strain[8 * i : 8 * i + 8] for i in range(6)]
    volume = lame_first * (part[0] + part[1] + part[2])
    normals = [stress_ref[i] + volume + 2.0 * modulus * part[i] for i in range(3)]
    shears = [stress_ref[i] + modulus * part[i] for i in range(3, 6)]
    mean = (normals[0] + normals[1] + normals[2]) * (1.0 / 3.0)
    devs = [value - mean for value in normals]
    trial_ref[6] = mean
    trial_ref[7] = jnp.sqrt(
        0.5 * (devs[0] ** 2 + devs[1] ** 2 + devs[2] ** 2) + shears[0] ** 2 + shears[1] ** 2 + shears[2] ** 2
    )
    for i in range(3):
        trial_ref[i] = devs[i]
        trial_ref[3 + i] = shears[i]


def halves(value):
    high = value.astype(jnp.bfloat16).astype(jnp.float32)
    return high, value - high


def final_state(
    cohesion_ref,
    friction_ref,
    matrix_ref,
    band_ref,
    slot_ref,
    depth_ref,
    zone_ref,
    trial_ref,
    conn_ref,
    stress_ref,
    release_ref,
    own_ref,
    ghost_ref,
):
    slot, depth = slot_ref[...], depth_ref[...]
    wanted_row = (slot >> 6) * 8 + (depth & 7)
    wanted_lane = (depth >> 3) * 64 + (slot & 63)

    def spread(value):
        return jnp.concatenate([value[r : r + 1] for r in range(8)], axis=1)

    elems = conn_ref.shape[1]
    found_row = lax.broadcasted_iota(jnp.int32, (band_ref.shape[0], elems), 0) == spread(wanted_row)
    high, low = halves(band_ref[...])
    found = lax.dot_general(
        jnp.concatenate([high, low], axis=1).astype(jnp.bfloat16),
        jnp.where(found_row, 1.0, 0.0).astype(jnp.bfloat16),
        (((0,), (0,)), ((), ())),
        preferred_element_type=jnp.float32,
    )
    found = found[0:128] + found[128:256]
    in_lane = lax.broadcasted_iota(jnp.int32, (128, elems), 0)
    pore = jnp.sum(jnp.where(in_lane == spread(wanted_lane), found, 0.0), axis=0, keepdims=True)
    zone = zone_ref[...]
    tan_red = pick(friction_ref, zone) * (1.0 / REDUCTION)
    cos_red = 1.0 / jnp.sqrt(1.0 + tan_red * tan_red)
    sin_red = tan_red * cos_red
    common = 6.0 / (np.sqrt(3.0).astype(np.float32) * (3.0 - sin_red))
    slope = common * sin_red
    bound = common * (pick(cohesion_ref, zone) * (1.0 / REDUCTION)) * cos_red

    allow = jnp.maximum(spread(bound) - spread(slope) * (trial_ref[6] + pore), 0.0)
    deviator = trial_ref[7]
    yielded = deviator > allow
    scale = jnp.where(yielded, allow / jnp.where(yielded, deviator, 1.0), 1.0)
    release_ref[...] = (1.0 - scale) * deviator
    mean = trial_ref[6]
    parts = [mean + scale * trial_ref[i] for i in range(3)] + [scale * trial_ref[3 + i] for i in range(3)]
    for i in range(6):
        stress_ref[i] = parts[i]
    force = jnp.dot(
        matrix_ref[...],
        jnp.concatenate(parts, axis=0),
        precision=lax.Precision.HIGHEST,
        preferred_element_type=jnp.float32,
    )
    in_segment = lax.broadcasted_iota(jnp.int32, (16, elems), 0)
    high, low = halves(force)
    total = jnp.zeros((96, 128), jnp.float32)
    for corner in range(8):
        node = conn_ref[corner : corner + 1, :]
        here = jnp.broadcast_to(node >> 7, in_segment.shape) == in_segment
        rows = []
        for source in (high, low):
            for comp in range(3):
                value = source[comp * 8 + corner : comp * 8 + corner + 1, :]
                rows.append(jnp.where(here, jnp.broadcast_to(value, in_segment.shape), 0.0))
        left = jnp.concatenate(rows, axis=0).astype(jnp.bfloat16)
        right = jnp.where(jnp.broadcast_to(node & 127, in_lane.shape) == in_lane, 1.0, 0.0).astype(jnp.bfloat16)
        total += lax.dot_general(left, right, (((1,), (1,)), ((), ())), preferred_element_type=jnp.float32)
    total = total[0:48] + total[48:96]
    for comp in range(3):
        own_ref[comp * 8 : comp * 8 + 8, :] = total[comp * 16 : comp * 16 + 8]
        ghost_ref[comp * 4 : comp * 4 + 4, :] = total[comp * 16 + 8 : comp * 16 + 12]


def add_returned(own_ref, ghost_ref, shared_ref, out_ref):
    shared = shared_ref[...]
    in_lane = lax.broadcasted_iota(jnp.int32, (128, 128), 0)
    in_segment = lax.broadcasted_iota(jnp.int32, (8, 128), 0)
    lefts, rights = [], []
    for s in range(4):
        node = shared[s : s + 1]
        rights.append(jnp.where(jnp.broadcast_to(node & 127, in_lane.shape) == in_lane, 1.0, 0.0))
        here = jnp.broadcast_to(node >> 7, in_segment.shape) == in_segment
        rows = []
        for comp in range(3):
            value = ghost_ref[comp * 4 + s : comp * 4 + s + 1, :]
            high, low = halves(value)
            for piece in (high, low):
                rows.append(jnp.where(here, jnp.broadcast_to(piece, in_segment.shape), 0.0))
        lefts.append(jnp.concatenate(rows, axis=0))
    left = jnp.concatenate(lefts, axis=1).astype(jnp.bfloat16)
    right = jnp.concatenate(rights, axis=1).astype(jnp.bfloat16)
    added = lax.dot_general(left, right, (((1,), (1,)), ((), ())), preferred_element_type=jnp.float32)
    for comp in range(3):
        total = own_ref[comp * 8 : comp * 8 + 8, :] + added[comp * 16 : comp * 16 + 8] + added[comp * 16 + 8 : comp * 16 + 16]
        for s in range(8):
            out_ref[comp : comp + 1, s * 128 : (s + 1) * 128] = total[s : s + 1]


VM = pl.BlockSpec(memory_space=pltpu.VMEM)
SM = pl.BlockSpec(memory_space=pltpu.SMEM)


def call(body, specs, outs, scratch, name):
    return pl.pallas_call(
        body,
        in_specs=specs,
        out_specs=tuple(VM for _ in outs),
        out_shape=tuple(jax.ShapeDtypeStruct(shape, jnp.float32) for shape in outs),
        scratch_shapes=scratch,
        compiler_params=pltpu.CompilerParams(vmem_limit_bytes=VMEM_LIMIT),
        name=name,
    )


def steps(count, by):
    return [(i, i + by) for i in range(count) if 0 <= i + by < count]


def per_device(
    pressure_head,
    zone_ids,
    retention_alpha,
    retention_exponent,
    conductivity,
    sent_columns,
    displacement,
    stress_old,
    connectivity,
    shared_nodes,
    element_zone,
    element_slot,
    element_depth,
    cohesion,
    friction,
):
    crest, section = (lax.axis_size(axis) for axis in AXES)
    devices = crest * section
    planes, rows, depth = pressure_head.shape
    height = rows + 8
    elems = connectivity.shape[1]
    nodes = displacement.shape[1]
    shared = shared_nodes.reshape(4, 128)
    place = jnp.stack([lax.axis_index("section"), jnp.int32(section)])

    forward, backward = call(
        pack_section, [VM] * 4, [(2 * WIDE * planes, depth), (32, depth)], [], "pack_section"
    )(pressure_head, zone_ids, displacement, shared)
    before = lax.ppermute(forward, "section", steps(section, 1))
    after = lax.ppermute(backward, AXES, steps(devices, -1))

    edge = (2, WIDE, height, depth)
    low, high = call(pack_crest, [SM] + [VM] * 4, [edge, edge], [], "pack_crest")(
        place, pressure_head, zone_ids, before, after
    )
    west = lax.ppermute(high, "crest", steps(crest, 1))
    east = lax.ppermute(low, "crest", steps(crest, -1))

    matrix = component_major()
    (trial,) = call(
        trial_state,
        [VM] * 5,
        [(8, 8, elems)],
        [pltpu.VMEM((40, 128), jnp.float32), pltpu.VMEM((24, elems), jnp.float32)],
        "trial_state",
    )(jnp.asarray(matrix, jnp.float32), displacement, after, connectivity, stress_old.transpose(1, 0, 2))

    trial, low = lax.optimization_barrier((trial, low))
    total = planes + 2 * WIDE
    field = pltpu.VMEM((total, height, depth), jnp.float32)
    head_out, outgoing = call(
        seepage,
        [SM] * 3 + [VM] * 5,
        [pressure_head.shape, (devices, 8, 128)],
        [field] * 7
        + [
            pltpu.VMEM((planes * rows, depth), jnp.float32),
            pltpu.VMEM((depth, planes * rows), jnp.float32),
            pltpu.VMEM((devices, 128), jnp.int32),
        ],
        "seepage",
    )(retention_alpha, retention_exponent, conductivity, low, high, west, east, sent_columns[0])
    incoming = lax.all_to_all(outgoing, AXES, split_axis=0, concat_axis=0, tiled=True)

    stress_new, release, own, ghost = call(
        final_state,
        [SM] * 2 + [VM] * 7,
        [(6, 8, elems), (8, elems), (24, 128), (12, 128)],
        [],
        "final_state",
    )(
        cohesion,
        friction,
        jnp.asarray(matrix.T * 0.125, jnp.float32),
        incoming.reshape(devices * 8, 128),
        element_slot.reshape(8, 128),
        element_depth.reshape(8, 128),
        element_zone.reshape(8, 128),
        trial,
        connectivity,
    )
    returned = lax.ppermute(ghost, AXES, steps(devices, 1))
    (node_forces,) = call(add_returned, [VM] * 3, [(3, nodes)], [], "add_returned")(own, returned, shared)
    return (head_out, stress_new.transpose(1, 0, 2), release, node_forces)


def solution(mesh):
    return jax.shard_map(
        per_device,
        mesh=mesh,
        in_specs=(
            P("crest", "section", None),
            P("crest", "section", None),
            P(),
            P(),
            P(),
            P(("crest", "section"), None, None),
            P(None, ("crest", "section")),
            P(None, None, ("crest", "section")),
            P(None, ("crest", "section")),
            P(("crest", "section")),
            P(("crest", "section")),
            P(("crest", "section")),
            P(("crest", "section")),
            P(),
            P(),
        ),
        out_specs=(
            P("crest", "section", None),
            P(None, None, ("crest", "section")),
            P(None, ("crest", "section")),
            P(None, ("crest", "section")),
        ),
        check_vma=False,
    )
```

```python
import functools

import jax
import jax.numpy as jnp
import numpy as np
from jax import lax
from jax.experimental import pallas as pl
from jax.experimental.pallas import tpu as pltpu
from jax.sharding import PartitionSpec as P

BAND = 16
SWEEPS = 3
WIDE = 3

STORAGE = 0.5
THETA_GAP = 0.35
TIME_STEP = 0.05
REDUCTION = 1.4
YOUNG = 200.0
POISSON = 0.3

AXES = ("crest", "section")
VMEM_LIMIT = 32 * 1024 * 1024


def corner_signs(index):
    return (2 * (index & 1) - 1, 2 * (index >> 1 & 1) - 1, 2 * (index >> 2 & 1) - 1)


def strain_matrix():
    matrix = np.zeros((48, 24))
    inv_root = 1.0 / np.sqrt(3.0)
    for gauss_point in range(8):
        gauss = [value * inv_root for value in corner_signs(gauss_point)]
        row_start = 6 * gauss_point
        for node_corner in range(8):
            sign_x, sign_y, sign_z = corner_signs(node_corner)
            grad_x = 0.25 * sign_x * (1 + gauss[1] * sign_y) * (1 + gauss[2] * sign_z)
            grad_y = 0.25 * sign_y * (1 + gauss[0] * sign_x) * (1 + gauss[2] * sign_z)
            grad_z = 0.25 * sign_z * (1 + gauss[0] * sign_x) * (1 + gauss[1] * sign_y)
            matrix[row_start + 0, node_corner] = grad_x
            matrix[row_start + 1, 8 + node_corner] = grad_y
            matrix[row_start + 2, 16 + node_corner] = grad_z
            matrix[row_start + 3, node_corner] = grad_y
            matrix[row_start + 3, 8 + node_corner] = grad_x
            matrix[row_start + 4, 8 + node_corner] = grad_z
            matrix[row_start + 4, 16 + node_corner] = grad_y
            matrix[row_start + 5, 16 + node_corner] = grad_x
            matrix[row_start + 5, node_corner] = grad_z
    return matrix


def component_major():
    order = [6 * gauss_point + comp for comp in range(6) for gauss_point in range(8)]
    return strain_matrix()[order]


def take_lanes(row, lanes):
    return jnp.take_along_axis(jnp.broadcast_to(row, lanes.shape), lanes, axis=1, mode="promise_in_bounds")


def pick(values_ref, index, first=0):
    lane = lax.broadcasted_iota(jnp.int32, (8, 128), 1)
    table = jnp.zeros((8, 128), jnp.float32)
    for zone in range(values_ref.shape[0]):
        table = jnp.where(lane == first + zone, values_ref[zone], table)
    return table if index is None else take_lanes(table, index)


def pack_edges(
    head_hbm,
    zone_hbm,
    disp_hbm,
    shared_hbm,
    forward_ref,
    backward_ref,
    low_ref,
    high_ref,
    head_ref,
    zone_ref,
    disp_ref,
    shared_ref,
    sems,
):
    copies = [
        pltpu.make_async_copy(source, target, sems.at[i])
        for i, (source, target) in enumerate(
            [(head_hbm, head_ref), (zone_hbm, zone_ref), (disp_hbm, disp_ref), (shared_hbm, shared_ref)]
        )
    ]
    for copy in copies:
        copy.start()
    for copy in copies:
        copy.wait()
    planes, rows = head_ref.shape[0], head_ref.shape[1]
    for x in range(planes):
        for field in range(2):
            own = head_ref[x] if field == 0 else zone_ref[x].astype(jnp.float32) + 1.0
            at = field * WIDE * planes + WIDE * x
            forward_ref[at : at + WIDE, :] = own[rows - WIDE : rows, :]
            backward_ref[at : at + WIDE, :] = own[0:WIDE, :]
            if x < WIDE:
                low_ref[field, x] = own
            if x >= planes - WIDE:
                high_ref[field, x - planes + WIDE] = own
    index = shared_ref[...]
    index = jnp.concatenate([index, index], axis=0)
    lanes, segment = index & 127, index >> 7
    for comp in range(3):
        found = jnp.zeros((8, 128), jnp.float32)
        for s in range(disp_ref.shape[1] // 128):
            row = disp_ref[comp : comp + 1, s * 128 : (s + 1) * 128]
            found = jnp.where(segment == s, take_lanes(row, lanes), found)
        for s in range(4):
            at = 2 * WIDE * planes + 2 * comp + s // 2
            backward_ref[at : at + 1, (s % 2) * 128 : (s % 2 + 1) * 128] = found[s : s + 1]
    backward_ref[30:32, :] = jnp.zeros((2, 256), jnp.float32)


def pack_corners(sections, place_ref, before_ref, after_ref, low_ref, high_ref):
    planes = low_ref.shape[1] + high_ref.shape[1]
    behind = jnp.where(place_ref[0] > 0, 1.0, 0.0)
    ahead = jnp.where(place_ref[0] < sections - 1, 1.0, 0.0)
    for x in range(planes):
        for field in range(2):
            at = field * WIDE * planes + WIDE * x
            tail = jnp.concatenate(
                [
                    after_ref[at : at + WIDE, :] * ahead,
                    jnp.zeros((2, after_ref.shape[1]), jnp.float32),
                    before_ref[at : at + WIDE, :] * behind,
                ],
                axis=0,
            )
            if x < 2:
                low_ref[field, x] = tail
            else:
                high_ref[field, x - 2] = tail


def seepage(
    crests,
    place_ref,
    tables_ref,
    index,
    low_ref,
    high_ref,
    low_tail_ref,
    high_tail_ref,
    before_ref,
    after_ref,
    before_tail_ref,
    after_tail_ref,
    head_ref,
    out_ref,
    h,
    alpha_f,
    less_f,
    m_f,
    root_f,
    gain_f,
    r_f,
    cap_f,
    table,
    deep,
):
    planes = head_ref.shape[0]
    rows = head_ref.shape[1]
    total = planes + 2 * WIDE
    height, depth = h.shape[1], h.shape[2]
    lane8 = lax.broadcasted_iota(jnp.int32, (8, 128), 1)
    zones = tables_ref.shape[0] // 4
    alpha_t, less_t, m_t, root_t = (
        [jnp.broadcast_to(tables_ref[f * zones + z : f * zones + z + 1, :], (8, depth)) for z in range(zones)]
        for f in range(4)
    )
    behind = jnp.where(place_ref[1] > 0, 1.0, 0.0)
    ahead = jnp.where(place_ref[1] < crests - 1, 1.0, 0.0)

    def fields(x, row, head, zone):
        at = slice(row, row + 8)
        h[x, at, :] = head
        zone = zone.astype(jnp.int32) - 1
        bits = [(zone & (1 << bit)) != 0 for bit in range(3)]

        def choose(values):
            for bit in bits:
                values = [jnp.where(bit, values[i + 1], values[i]) for i in range(0, len(values), 2)]
            return values[0]

        alpha, less = choose(alpha_t), choose(less_t)
        alpha_f[x, at, :] = alpha
        less_f[x, at, :] = less
        m_f[x, at, :] = choose(m_t)
        root_f[x, at, :] = jnp.where(zone >= 0, choose(root_t), 0.0)
        gain_f[x, at, :] = THETA_GAP * alpha * less

    def body_rows(x, source, plane, inside=None):
        for row in range(0, rows, 8):
            zone = source[1, plane, row : row + 8, :]
            fields(x, row, source[0, plane, row : row + 8, :], zone if inside is None else zone * inside)

    @pl.loop(0, WIDE)
    def _(x):
        body_rows(x, before_ref, x, behind)
        body_rows(WIDE + x, low_ref, x)
        body_rows(WIDE + planes + x, after_ref, x, ahead)

    body_rows(2 * WIDE, high_ref, WIDE - 1)

    @pl.loop(0, 2)
    def _(x):
        fields(1 + x, rows, before_tail_ref[0, x], before_tail_ref[1, x] * behind)
        fields(3 + x, rows, low_tail_ref[0, x], low_tail_ref[1, x])
        fields(5 + x, rows, high_tail_ref[0, x], high_tail_ref[1, x])
        fields(7 + x, rows, after_tail_ref[0, x], after_tail_ref[1, x] * ahead)

    for x in (0, total - 1):
        for field in (h, alpha_f, less_f, m_f, root_f, gain_f):
            field[x, rows:height, :] = jnp.zeros((height - rows, depth), jnp.float32)

    def base(x):
        scaled = alpha_f[x] * jnp.maximum(-h[x], 0.0)
        power = jnp.exp(less_f[x] * jnp.log(jnp.maximum(scaled, 1e-30)))
        plus = 1.0 + power * scaled
        return power, plus, jnp.log(plus)

    def retention(x):
        power, plus, log_plus = base(x)
        fourth = jnp.exp(m_f[x] * log_plus)
        square = fourth * fourth
        part = power * (square * square)
        r_f[x] = root_f[x] * fourth * (1.0 - part)
        cap_f[x] = TIME_STEP * plus / (STORAGE * plus + gain_f[x] * part)

    inner_z = lax.broadcasted_iota(jnp.int32, (height, depth), 1) < depth - 1

    def face(x):
        return r_f[x] * r_f[x + 1] * (h[x + 1] - h[x])

    for sweep in range(SWEEPS):

        @pl.loop(sweep, total - sweep)
        def _(x):
            retention(x)

        def update(x, came):
            here, r = h[x], r_f[x]
            goes = face(x)
            flux_y = r * pltpu.roll(r, height - 1, 0) * (pltpu.roll(here, height - 1, 0) - here)
            flux_z = r * pltpu.roll(r, depth - 1, 1) * (pltpu.roll(here, depth - 1, 1) - here + 1.0)
            flux_z = jnp.where(inner_z, flux_z, 0.0)
            inflow = goes - came + (flux_y - pltpu.roll(flux_y, 1, 0)) + (flux_z - pltpu.roll(flux_z, 1, 1))
            h[x] = here + cap_f[x] * inflow
            return goes

        lax.fori_loop(sweep + 1, total - sweep - 1, update, face(sweep))

    for x in range(planes):
        _, _, log_plus = base(WIDE + x)
        here = h[WIDE + x][0:rows]
        head_ref[x] = here
        table[x * rows : (x + 1) * rows, :] = jnp.exp(4.0 * m_f[WIDE + x] * log_plus)[0:rows] * here
    deep[...] = table[...].T
    bands = depth // BAND

    @pl.loop(0, bands)
    def _(b):
        upper = deep[pl.ds(pl.multiple_of(b * BAND, 8), 8), :]
        lower = deep[pl.ds(pl.multiple_of(b * BAND + 8, 8), 8), :]
        for group in range(out_ref.shape[0] // bands):
            d = group * bands + b
            columns = jnp.broadcast_to(index[pl.ds(d, 1), :], (8, 128))
            out_ref[d] = jnp.where(lane8 < 64, take_lanes(upper, columns), take_lanes(lower, columns))


def element_rows(value):
    return jnp.concatenate([value[r : r + 1] for r in range(8)], axis=1)


def selectors(
    order_ref,
    disp_hbm,
    stress_hbm,
    conn_hbm,
    strain_hbm,
    force_hbm,
    slot_hbm,
    depth_hbm,
    zone_hbm,
    wanted_hbm,
    alpha_hbm,
    expo_hbm,
    ks_hbm,
    cohesion_hbm,
    friction_hbm,
    disp_ref,
    stress_ref,
    conn_ref,
    strain_ref,
    force_ref,
    row_ref,
    node_ref,
    strength_ref,
    lane_ref,
    tables_ref,
    index_ref,
    slot_ref,
    depth_ref,
    zone_ref,
    wanted_ref,
    alpha_ref,
    expo_ref,
    ks_ref,
    cohesion_ref,
    friction_ref,
    sems,
):
    del order_ref
    pairs = [
        (conn_hbm, conn_ref),
        (slot_hbm, slot_ref),
        (depth_hbm, depth_ref),
        (zone_hbm, zone_ref),
        (wanted_hbm, wanted_ref),
        (alpha_hbm, alpha_ref),
        (expo_hbm, expo_ref),
        (ks_hbm, ks_ref),
        (cohesion_hbm, cohesion_ref),
        (friction_hbm, friction_ref),
        (disp_hbm, disp_ref),
        (stress_hbm, stress_ref),
        (strain_hbm, strain_ref),
        (force_hbm, force_ref),
    ]
    copies = [pltpu.make_async_copy(source, target, sems.at[i]) for i, (source, target) in enumerate(pairs)]
    for copy in copies:
        copy.start()
    for copy in copies:
        copy.wait()
    elems = conn_ref.shape[1]
    slot, depth = slot_ref[...], depth_ref[...]
    row = element_rows((slot >> 6) * 8 + (depth & 7))
    lane_ref[...] = element_rows((depth >> 3) * 64 + (slot & 63))
    in_lane = lax.broadcasted_iota(jnp.int32, (128, elems), 0)

    @pl.loop(0, row_ref.shape[0] // 128)
    def _(part):
        first = pl.multiple_of(part * 128, 128)
        row_ref[pl.ds(first, 128), :] = jnp.where(in_lane == row - first, 1.0, 0.0).astype(jnp.bfloat16)

    @pl.loop(0, 8)
    def _(corner):
        node = conn_ref[pl.ds(corner, 1), :] & 127
        node_ref[corner] = jnp.where(in_lane == node, 1.0, 0.0).astype(jnp.bfloat16)

    zone = zone_ref[...]
    tan_red = pick(friction_ref, zone) * (1.0 / REDUCTION)
    cos_red = 1.0 / jnp.sqrt(1.0 + tan_red * tan_red)
    sin_red = tan_red * cos_red
    common = 6.0 / (np.sqrt(3.0).astype(np.float32) * (3.0 - sin_red))
    strength_ref[0:1, :] = element_rows(common * (pick(cohesion_ref, zone) * (1.0 / REDUCTION)) * cos_red)
    strength_ref[1:2, :] = element_rows(common * sin_red)

    zones, width = alpha_ref.shape[0], tables_ref.shape[1]
    for z in range(zones):
        expo = jnp.full((1, width), expo_ref[z], jnp.float32)
        expo = jnp.where(expo > 0, expo, 2.0)
        tables_ref[z : z + 1, :] = jnp.full((1, width), alpha_ref[z], jnp.float32)
        tables_ref[zones + z : zones + z + 1, :] = expo - 1.0
        tables_ref[2 * zones + z : 2 * zones + z + 1, :] = -0.25 * (1.0 - 1.0 / expo)
        tables_ref[3 * zones + z : 3 * zones + z + 1, :] = jnp.sqrt(jnp.full((1, width), ks_ref[z], jnp.float32))
    wanted = wanted_ref[...]
    index_ref[...] = jnp.concatenate([wanted, wanted], axis=0).T


def trial_state(matrix_ref, disp_ref, ghost_ref, conn_ref, stress_ref, trial_ref, nodes, corners):
    for comp in range(3):
        for s in range(8):
            nodes[comp * 12 + s : comp * 12 + s + 1, :] = disp_ref[comp : comp + 1, s * 128 : (s + 1) * 128]
        for s in range(4):
            at = 24 + 2 * comp + s // 2
            nodes[comp * 12 + 8 + s : comp * 12 + 9 + s, :] = ghost_ref[at : at + 1, (s % 2) * 128 : (s % 2 + 1) * 128]
    elems = conn_ref.shape[1]

    @pl.loop(0, elems, step=128)
    def _(e):
        e = pl.multiple_of(e, 128)
        index = conn_ref[:, pl.ds(e, 128)]
        lanes, segment = index & 127, index >> 7
        found = [jnp.zeros((8, 128), jnp.float32) for _ in range(3)]
        for s in range(12):
            here = segment == s
            for comp in range(3):
                row = nodes[comp * 12 + s : comp * 12 + s + 1, :]
                found[comp] = jnp.where(here, take_lanes(row, lanes), found[comp])
        for comp in range(3):
            corners[comp * 8 : comp * 8 + 8, pl.ds(e, 128)] = found[comp]

    strain = jnp.dot(
        matrix_ref[...], corners[...], precision=lax.Precision.HIGHEST, preferred_element_type=jnp.float32
    )
    lame_first = YOUNG * POISSON / ((1.0 + POISSON) * (1.0 - 2.0 * POISSON))
    modulus = YOUNG / (2.0 * (1.0 + POISSON))
    part = [strain[8 * i : 8 * i + 8] for i in range(6)]
    volume = lame_first * (part[0] + part[1] + part[2])
    normals = [stress_ref[i] + volume + 2.0 * modulus * part[i] for i in range(3)]
    shears = [stress_ref[i] + modulus * part[i] for i in range(3, 6)]
    mean = (normals[0] + normals[1] + normals[2]) * (1.0 / 3.0)
    devs = [value - mean for value in normals]
    trial_ref[6] = mean
    trial_ref[7] = jnp.sqrt(
        0.5 * (devs[0] ** 2 + devs[1] ** 2 + devs[2] ** 2) + shears[0] ** 2 + shears[1] ** 2 + shears[2] ** 2
    )
    for i in range(3):
        trial_ref[i] = devs[i]
        trial_ref[3 + i] = shears[i]


def halves(value):
    high = value.astype(jnp.bfloat16).astype(jnp.float32)
    return high, value - high


def final_state(
    matrix_ref, band_ref, row_ref, lane_ref, node_ref, strength_ref, trial_ref, conn_ref, stress_ref, release_ref, own_ref, ghost_ref
):
    elems = conn_ref.shape[1]
    high, low = halves(band_ref[...])
    found = lax.dot_general(
        jnp.concatenate([high, low], axis=1).astype(jnp.bfloat16),
        row_ref[...],
        (((0,), (0,)), ((), ())),
        preferred_element_type=jnp.float32,
    )
    found = found[0:128] + found[128:256]
    in_lane = lax.broadcasted_iota(jnp.int32, (128, elems), 0)
    pore = jnp.sum(jnp.where(in_lane == lane_ref[...], found, 0.0), axis=0, keepdims=True)
    allow = jnp.maximum(strength_ref[0:1, :] - strength_ref[1:2, :] * (trial_ref[6] + pore), 0.0)
    deviator = trial_ref[7]
    yielded = deviator > allow
    scale = jnp.where(yielded, allow / jnp.where(yielded, deviator, 1.0), 1.0)
    release_ref[...] = (1.0 - scale) * deviator
    mean = trial_ref[6]
    parts = [mean + scale * trial_ref[i] for i in range(3)] + [scale * trial_ref[3 + i] for i in range(3)]
    for i in range(6):
        stress_ref[i] = parts[i]
    force = jnp.dot(
        matrix_ref[...],
        jnp.concatenate(parts, axis=0),
        precision=lax.Precision.HIGHEST,
        preferred_element_type=jnp.float32,
    )
    in_segment = lax.broadcasted_iota(jnp.int32, (16, elems), 0)
    high, low = halves(force)
    total = jnp.zeros((96, 128), jnp.float32)
    for corner in range(8):
        node = conn_ref[corner : corner + 1, :]
        here = jnp.broadcast_to(node >> 7, in_segment.shape) == in_segment
        rows = []
        for source in (high, low):
            for comp in range(3):
                value = source[comp * 8 + corner : comp * 8 + corner + 1, :]
                rows.append(jnp.where(here, jnp.broadcast_to(value, in_segment.shape), 0.0))
        left = jnp.concatenate(rows, axis=0).astype(jnp.bfloat16)
        total += lax.dot_general(left, node_ref[corner], (((1,), (1,)), ((), ())), preferred_element_type=jnp.float32)
    total = total[0:48] + total[48:96]
    for comp in range(3):
        own_ref[comp * 8 : comp * 8 + 8, :] = total[comp * 16 : comp * 16 + 8]
        ghost_ref[comp * 4 : comp * 4 + 4, :] = total[comp * 16 + 8 : comp * 16 + 12]


def add_returned(own_ref, ghost_ref, shared_ref, out_ref):
    shared = shared_ref[...]
    in_lane = lax.broadcasted_iota(jnp.int32, (128, 128), 0)
    in_segment = lax.broadcasted_iota(jnp.int32, (8, 128), 0)
    lefts, rights = [], []
    for s in range(4):
        node = shared[s : s + 1]
        rights.append(jnp.where(jnp.broadcast_to(node & 127, in_lane.shape) == in_lane, 1.0, 0.0))
        here = jnp.broadcast_to(node >> 7, in_segment.shape) == in_segment
        rows = []
        for comp in range(3):
            value = ghost_ref[comp * 4 + s : comp * 4 + s + 1, :]
            high, low = halves(value)
            for piece in (high, low):
                rows.append(jnp.where(here, jnp.broadcast_to(piece, in_segment.shape), 0.0))
        lefts.append(jnp.concatenate(rows, axis=0))
    left = jnp.concatenate(lefts, axis=1).astype(jnp.bfloat16)
    right = jnp.concatenate(rights, axis=1).astype(jnp.bfloat16)
    added = lax.dot_general(left, right, (((1,), (1,)), ((), ())), preferred_element_type=jnp.float32)
    for comp in range(3):
        total = own_ref[comp * 8 : comp * 8 + 8, :] + added[comp * 16 : comp * 16 + 8] + added[comp * 16 + 8 : comp * 16 + 16]
        for s in range(8):
            out_ref[comp : comp + 1, s * 128 : (s + 1) * 128] = total[s : s + 1]


VM = pl.BlockSpec(memory_space=pltpu.VMEM)
SM = pl.BlockSpec(memory_space=pltpu.SMEM)


HBM = pl.BlockSpec(memory_space=pltpu.HBM)


def call(body, specs, outs, scratch, name, types=None):
    types = types or [jnp.float32] * len(outs)
    return pl.pallas_call(
        body,
        in_specs=specs,
        out_specs=tuple(VM for _ in outs),
        out_shape=tuple(jax.ShapeDtypeStruct(shape, kind) for shape, kind in zip(outs, types)),
        scratch_shapes=scratch,
        compiler_params=pltpu.CompilerParams(vmem_limit_bytes=VMEM_LIMIT),
        name=name,
    )


def in_hbm(value):
    return pltpu.with_memory_space_constraint(value, pltpu.HBM)


def steps(count, by):
    return [(i, (i + by) % count) for i in range(count)]


def per_device(
    pressure_head,
    zone_ids,
    retention_alpha,
    retention_exponent,
    conductivity,
    sent_columns,
    displacement,
    stress_old,
    connectivity,
    shared_nodes,
    element_zone,
    element_slot,
    element_depth,
    cohesion,
    friction,
):
    crest, section = (lax.axis_size(axis) for axis in AXES)
    devices = crest * section
    planes, rows, depth = pressure_head.shape
    height = rows + 8
    elems = connectivity.shape[1]
    nodes = displacement.shape[1]
    shared = shared_nodes.reshape(4, 128)
    place = jnp.stack([lax.axis_index("section"), lax.axis_index("crest")])

    own = (2, WIDE, rows, depth)
    forward, backward, low, high = call(
        pack_edges,
        [HBM] * 4,
        [(2 * WIDE * planes, depth), (32, depth), own, own],
        [
            pltpu.VMEM(pressure_head.shape, jnp.float32),
            pltpu.VMEM(zone_ids.shape, jnp.int32),
            pltpu.VMEM(displacement.shape, jnp.float32),
            pltpu.VMEM(shared.shape, jnp.int32),
            pltpu.SemaphoreType.DMA((4,)),
        ],
        "pack_edges",
    )(*(in_hbm(x) for x in (pressure_head, zone_ids, displacement, shared)))
    before = lax.ppermute(forward, "section", steps(section, 1))
    after = lax.ppermute(backward, AXES, steps(devices, -1))
    west = lax.ppermute(high, "crest", steps(crest, 1))
    east = lax.ppermute(low, "crest", steps(crest, -1))

    tails = (2, 2, 8, depth)
    low_tail, high_tail = call(
        functools.partial(pack_corners, section), [SM] + [VM] * 2, [tails, tails], [], "pack_corners"
    )(place, before, after)
    west_tail = lax.ppermute(high_tail, "crest", steps(crest, 1))
    east_tail = lax.ppermute(low_tail, "crest", steps(crest, -1))

    zones = retention_alpha.shape[0]
    matrix = component_major()
    disp, stress, conn, strain_matrix_v, force_matrix, row_hot, node_hot, strength, lane, tables, index = call(
        selectors,
        [VM] + [HBM] * 14,
        [
            displacement.shape,
            (6, 8, elems),
            connectivity.shape,
            (48, 24),
            (24, 48),
            (devices * 8, elems),
            (8, 128, elems),
            (2, elems),
            (1, elems),
            (4 * zones, depth),
            (devices, 128),
        ],
        [pltpu.VMEM((8, 128), jnp.int32)] * 3
        + [pltpu.VMEM((64, devices), jnp.int32)]
        + [pltpu.SMEM((zones,), jnp.float32)] * 5
        + [pltpu.SemaphoreType.DMA((14,))],
        "selectors",
        [jnp.float32] * 2
        + [jnp.int32]
        + [jnp.float32] * 2
        + [jnp.bfloat16] * 2
        + [jnp.float32, jnp.int32, jnp.float32, jnp.int32],
    )(
        forward,
        *(
            in_hbm(x)
            for x in (
                displacement,
                stress_old.transpose(1, 0, 2),
                connectivity,
                jnp.asarray(matrix, jnp.float32),
                jnp.asarray(matrix.T * 0.125, jnp.float32),
                element_slot.reshape(8, 128),
                element_depth.reshape(8, 128),
                element_zone.reshape(8, 128),
                sent_columns[0].T,
                retention_alpha,
                retention_exponent,
                conductivity,
                cohesion,
                friction,
            )
        ),
    )
    (trial,) = call(
        trial_state,
        [VM] * 5,
        [(8, 8, elems)],
        [pltpu.VMEM((40, 128), jnp.float32), pltpu.VMEM((24, elems), jnp.float32)],
        "trial_state",
    )(strain_matrix_v, disp, after, conn, stress)

    trial, tables = lax.optimization_barrier((trial, tables))
    total = planes + 2 * WIDE
    field = pltpu.VMEM((total, height, depth), jnp.float32)
    head_out, outgoing = call(
        functools.partial(seepage, crest),
        [SM] + [VM] * 10,
        [pressure_head.shape, (devices, 8, 128)],
        [field] * 8
        + [pltpu.VMEM((planes * rows, depth), jnp.float32), pltpu.VMEM((depth, planes * rows), jnp.float32)],
        "seepage",
    )(place, tables, index, low, high, low_tail, high_tail, west, east, west_tail, east_tail)
    incoming = lax.all_to_all(outgoing, AXES, split_axis=0, concat_axis=0, tiled=True)

    stress_new, release, own, ghost = call(
        final_state,
        [VM] * 8,
        [(6, 8, elems), (8, elems), (24, 128), (12, 128)],
        [],
        "final_state",
    )(force_matrix, incoming.reshape(devices * 8, 128), row_hot, lane, node_hot, strength, trial, conn)
    returned = lax.ppermute(ghost, AXES, steps(devices, 1))
    (node_forces,) = call(add_returned, [VM] * 3, [(3, nodes)], [], "add_returned")(own, returned, shared)
    return (head_out, stress_new.transpose(1, 0, 2), release, node_forces)


def solution(mesh):
    return jax.shard_map(
        per_device,
        mesh=mesh,
        in_specs=(
            P("crest", "section", None),
            P("crest", "section", None),
            P(),
            P(),
            P(),
            P(("crest", "section"), None, None),
            P(None, ("crest", "section")),
            P(None, None, ("crest", "section")),
            P(None, ("crest", "section")),
            P(("crest", "section")),
            P(("crest", "section")),
            P(("crest", "section")),
            P(("crest", "section")),
            P(),
            P(),
        ),
        out_specs=(
            P("crest", "section", None),
            P(None, None, ("crest", "section")),
            P(None, ("crest", "section")),
            P(None, ("crest", "section")),
        ),
        check_vma=False,
    )
```

```python
import functools

import jax
import jax.numpy as jnp
import numpy as np
from jax import lax
from jax.experimental import pallas as pl
from jax.experimental.pallas import tpu as pltpu
from jax.sharding import PartitionSpec as P

BAND = 16
SWEEPS = 3
WIDE = 3

STORAGE = 0.5
THETA_GAP = 0.35
TIME_STEP = 0.05
REDUCTION = 1.4
YOUNG = 200.0
POISSON = 0.3

AXES = ("crest", "section")
VMEM_LIMIT = 32 * 1024 * 1024


def corner_signs(index):
    return (2 * (index & 1) - 1, 2 * (index >> 1 & 1) - 1, 2 * (index >> 2 & 1) - 1)


def strain_matrix():
    matrix = np.zeros((48, 24))
    inv_root = 1.0 / np.sqrt(3.0)
    for gauss_point in range(8):
        gauss = [value * inv_root for value in corner_signs(gauss_point)]
        row_start = 6 * gauss_point
        for node_corner in range(8):
            sign_x, sign_y, sign_z = corner_signs(node_corner)
            grad_x = 0.25 * sign_x * (1 + gauss[1] * sign_y) * (1 + gauss[2] * sign_z)
            grad_y = 0.25 * sign_y * (1 + gauss[0] * sign_x) * (1 + gauss[2] * sign_z)
            grad_z = 0.25 * sign_z * (1 + gauss[0] * sign_x) * (1 + gauss[1] * sign_y)
            matrix[row_start + 0, node_corner] = grad_x
            matrix[row_start + 1, 8 + node_corner] = grad_y
            matrix[row_start + 2, 16 + node_corner] = grad_z
            matrix[row_start + 3, node_corner] = grad_y
            matrix[row_start + 3, 8 + node_corner] = grad_x
            matrix[row_start + 4, 8 + node_corner] = grad_z
            matrix[row_start + 4, 16 + node_corner] = grad_y
            matrix[row_start + 5, 16 + node_corner] = grad_x
            matrix[row_start + 5, node_corner] = grad_z
    return matrix


def component_major():
    order = [6 * gauss_point + comp for comp in range(6) for gauss_point in range(8)]
    return strain_matrix()[order]


def take_lanes(row, lanes):
    return jnp.take_along_axis(jnp.broadcast_to(row, lanes.shape), lanes, axis=1, mode="promise_in_bounds")


def pick(values_ref, index, first=0):
    lane = lax.broadcasted_iota(jnp.int32, (8, 128), 1)
    table = jnp.zeros((8, 128), jnp.float32)
    for zone in range(values_ref.shape[0]):
        table = jnp.where(lane == first + zone, values_ref[zone], table)
    return table if index is None else take_lanes(table, index)


def fetch(pairs, sems):
    copies = [pltpu.make_async_copy(source, target, sems.at[i]) for i, (source, target) in enumerate(pairs)]
    for copy in copies:
        copy.start()
    for copy in copies:
        copy.wait()


def pack_section(
    head_hbm, zone_hbm, disp_hbm, shared_hbm, forward_ref, backward_ref, head_ref, zone_ref, disp_ref, shared_ref, sems
):
    fetch([(head_hbm, head_ref), (zone_hbm, zone_ref), (disp_hbm, disp_ref), (shared_hbm, shared_ref)], sems)
    planes, rows = head_ref.shape[0], head_ref.shape[1]
    for x in range(planes):
        for field in range(2):
            first, last = slice(0, WIDE), slice(rows - WIDE, rows)
            at = field * WIDE * planes + WIDE * x
            if field == 0:
                forward_ref[at : at + WIDE, :] = head_ref[x, last, :]
                backward_ref[at : at + WIDE, :] = head_ref[x, first, :]
            else:
                forward_ref[at : at + WIDE, :] = zone_ref[x, last, :].astype(jnp.float32) + 1.0
                backward_ref[at : at + WIDE, :] = zone_ref[x, first, :].astype(jnp.float32) + 1.0
    index = shared_ref[...]
    index = jnp.concatenate([index, index], axis=0)
    lanes, segment = index & 127, index >> 7
    for comp in range(3):
        found = jnp.zeros((8, 128), jnp.float32)
        for s in range(disp_ref.shape[1] // 128):
            row = disp_ref[comp : comp + 1, s * 128 : (s + 1) * 128]
            found = jnp.where(segment == s, take_lanes(row, lanes), found)
        for s in range(4):
            at = 2 * WIDE * planes + 2 * comp + s // 2
            backward_ref[at : at + 1, (s % 2) * 128 : (s % 2 + 1) * 128] = found[s : s + 1]
    backward_ref[30:32, :] = jnp.zeros((2, 256), jnp.float32)


def pack_crest(
    head_ref,
    zone_ref,
    wanted_hbm,
    alpha_hbm,
    expo_hbm,
    ks_hbm,
    low_ref,
    high_ref,
    tables_ref,
    index_ref,
    wanted_ref,
    alpha_ref,
    expo_ref,
    ks_ref,
    sems,
):
    pairs = [(wanted_hbm, wanted_ref), (alpha_hbm, alpha_ref), (expo_hbm, expo_ref), (ks_hbm, ks_ref)]
    copies = [pltpu.make_async_copy(source, target, sems.at[i]) for i, (source, target) in enumerate(pairs)]
    for copy in copies:
        copy.start()
    planes = head_ref.shape[0]
    for x in range(planes):
        own = [head_ref[x], zone_ref[x].astype(jnp.float32) + 1.0]
        for field in range(2):
            if x < WIDE:
                low_ref[field, x] = own[field]
            if x >= planes - WIDE:
                high_ref[field, x - planes + WIDE] = own[field]
    for copy in copies:
        copy.wait()
    zones, width = alpha_ref.shape[0], tables_ref.shape[1]
    for z in range(zones):
        expo = jnp.full((1, width), expo_ref[z], jnp.float32)
        expo = jnp.where(expo > 0, expo, 2.0)
        tables_ref[z : z + 1, :] = jnp.full((1, width), alpha_ref[z], jnp.float32)
        tables_ref[zones + z : zones + z + 1, :] = expo - 1.0
        tables_ref[2 * zones + z : 2 * zones + z + 1, :] = -0.25 * (1.0 - 1.0 / expo)
        tables_ref[3 * zones + z : 3 * zones + z + 1, :] = jnp.sqrt(jnp.full((1, width), ks_ref[z], jnp.float32))
    wanted = wanted_ref[...]
    index_ref[...] = jnp.concatenate([wanted, pltpu.roll(wanted, wanted.shape[1] // 2, 1)], axis=0).T


def pack_corners(sections, place_ref, before_ref, after_ref, low_ref, high_ref):
    planes = high_ref.shape[0]
    behind = jnp.where(place_ref[0] > 0, 1.0, 0.0)
    ahead = jnp.where(place_ref[0] < sections - 1, 1.0, 0.0)
    for x in range(planes):
        for field in range(2):
            at = field * WIDE * planes + WIDE * x
            tail = jnp.concatenate(
                [
                    after_ref[at : at + WIDE, :] * ahead,
                    jnp.zeros((2, after_ref.shape[1]), jnp.float32),
                    before_ref[at : at + WIDE, :] * behind,
                ],
                axis=0,
            )
            if x < 2:
                low_ref[2 * field + x] = tail
            else:
                high_ref[2 * field + x - 2] = tail
    low_ref[4] = after_ref[24:32, :]


def seepage(
    crests,
    place_ref,
    tables_ref,
    index,
    low_ref,
    high_ref,
    low_tail_ref,
    high_tail_ref,
    before_ref,
    after_ref,
    before_tail_ref,
    after_tail_ref,
    head_ref,
    out_ref,
    order_ref,
    h,
    alpha_f,
    less_f,
    m_f,
    root_f,
    gain_f,
    r_f,
    cap_f,
    table,
    deep,
):
    planes = head_ref.shape[0]
    rows = head_ref.shape[1]
    total = planes + 2 * WIDE
    height, depth = h.shape[1], h.shape[2]
    lane8 = lax.broadcasted_iota(jnp.int32, (8, 128), 1)
    zones = tables_ref.shape[0] // 4
    alpha_t, less_t, m_t, root_t = (
        [jnp.broadcast_to(tables_ref[f * zones + z : f * zones + z + 1, :], (8, depth)) for z in range(zones)]
        for f in range(4)
    )
    behind = jnp.where(place_ref[1] > 0, 1.0, 0.0)
    ahead = jnp.where(place_ref[1] < crests - 1, 1.0, 0.0)

    def fields(x, row, head, zone):
        at = slice(row, row + 8)
        h[x, at, :] = head
        zone = zone.astype(jnp.int32) - 1
        bits = [(zone & (1 << bit)) != 0 for bit in range(3)]

        def choose(values):
            for bit in bits:
                values = [jnp.where(bit, values[i + 1], values[i]) for i in range(0, len(values), 2)]
            return values[0]

        alpha, less = choose(alpha_t), choose(less_t)
        alpha_f[x, at, :] = alpha
        less_f[x, at, :] = less
        m_f[x, at, :] = choose(m_t)
        root_f[x, at, :] = jnp.where(zone >= 0, choose(root_t), 0.0)
        gain_f[x, at, :] = THETA_GAP * alpha * less

    def body_rows(x, source, plane, inside=None):
        for row in range(0, rows, 8):
            zone = source[1, plane, row : row + 8, :]
            fields(x, row, source[0, plane, row : row + 8, :], zone if inside is None else zone * inside)

    @pl.loop(0, WIDE)
    def _(x):
        body_rows(x, before_ref, x, behind)
        body_rows(WIDE + x, low_ref, x)
        body_rows(WIDE + planes + x, after_ref, x, ahead)

    body_rows(2 * WIDE, high_ref, WIDE - 1)

    @pl.loop(0, 2)
    def _(x):
        fields(1 + x, rows, before_tail_ref[x], before_tail_ref[2 + x] * behind)
        fields(3 + x, rows, low_tail_ref[x], low_tail_ref[2 + x])
        fields(5 + x, rows, high_tail_ref[x], high_tail_ref[2 + x])
        fields(7 + x, rows, after_tail_ref[x], after_tail_ref[2 + x] * ahead)

    for x in (0, total - 1):
        for field in (h, alpha_f, less_f, m_f, root_f, gain_f):
            field[x, rows:height, :] = jnp.zeros((height - rows, depth), jnp.float32)

    def base(x):
        scaled = alpha_f[x] * jnp.maximum(-h[x], 0.0)
        power = jnp.exp(less_f[x] * jnp.log(jnp.maximum(scaled, 1e-30)))
        plus = 1.0 + power * scaled
        return power, plus, jnp.log(plus)

    def retention(x):
        power, plus, log_plus = base(x)
        fourth = jnp.exp(m_f[x] * log_plus)
        square = fourth * fourth
        part = power * (square * square)
        r_f[x] = root_f[x] * fourth * (1.0 - part)
        cap_f[x] = TIME_STEP * plus / (STORAGE * plus + gain_f[x] * part)

    inner_z = lax.broadcasted_iota(jnp.int32, (height, depth), 1) < depth - 1

    def face(x):
        return r_f[x] * r_f[x + 1] * (h[x + 1] - h[x])

    for sweep in range(SWEEPS):

        @pl.loop(sweep, total - sweep)
        def _(x):
            retention(x)

        def update(x, came):
            here, r = h[x], r_f[x]
            goes = face(x)
            flux_y = r * pltpu.roll(r, height - 1, 0) * (pltpu.roll(here, height - 1, 0) - here)
            flux_z = r * pltpu.roll(r, depth - 1, 1) * (pltpu.roll(here, depth - 1, 1) - here + 1.0)
            flux_z = jnp.where(inner_z, flux_z, 0.0)
            inflow = goes - came + (flux_y - pltpu.roll(flux_y, 1, 0)) + (flux_z - pltpu.roll(flux_z, 1, 1))
            h[x] = here + cap_f[x] * inflow
            return goes

        lax.fori_loop(sweep + 1, total - sweep - 1, update, face(sweep))

    for x in range(planes):
        _, _, log_plus = base(WIDE + x)
        here = h[WIDE + x][0:rows]
        head_ref[x] = here
        table[x * rows : (x + 1) * rows, :] = jnp.exp(4.0 * m_f[WIDE + x] * log_plus)[0:rows] * here
    deep[...] = table[...].T
    bands = depth // BAND

    order_ref[...] = deep[0:8, :]
    half = out_ref.shape[0] // 2

    @pl.loop(0, bands)
    def _(b):
        upper = deep[pl.ds(pl.multiple_of(b * BAND, 8), 8), :]
        lower = deep[pl.ds(pl.multiple_of(b * BAND + 8, 8), 8), :]
        for group in range(half // bands):
            d = group * bands + b
            columns = jnp.broadcast_to(index[pl.ds(d, 1), :], (8, 128))
            first, second = take_lanes(upper, columns), pltpu.roll(take_lanes(lower, columns), 64, 1)
            out_ref[d] = jnp.where(lane8 < 64, first, second)
            out_ref[half + d] = jnp.where(lane8 < 64, second, first)


def element_rows(value):
    return jnp.concatenate([value[r : r + 1] for r in range(8)], axis=1)


def selectors(
    partitions,
    place_ref,
    order_ref,
    disp_hbm,
    stress_hbm,
    conn_hbm,
    strain_hbm,
    force_hbm,
    slot_hbm,
    depth_hbm,
    zone_hbm,
    cohesion_hbm,
    friction_hbm,
    disp_ref,
    stress_ref,
    conn_ref,
    strain_ref,
    force_ref,
    strength_ref,
    at_ref,
    slot_ref,
    depth_ref,
    zone_ref,
    cohesion_ref,
    friction_ref,
    sems,
):
    del order_ref
    fetch(
        [
            (conn_hbm, conn_ref),
            (slot_hbm, slot_ref),
            (depth_hbm, depth_ref),
            (zone_hbm, zone_ref),
            (cohesion_hbm, cohesion_ref),
            (friction_hbm, friction_ref),
            (disp_hbm, disp_ref),
            (stress_hbm, stress_ref),
            (strain_hbm, strain_ref),
            (force_hbm, force_ref),
        ],
        sems,
    )
    elems = conn_ref.shape[1]
    slot, depth = slot_ref[...], depth_ref[...]
    swap = jnp.where(place_ref[2] >= partitions // 2, 1, 0)
    at_ref[0:1, :] = element_rows((slot >> 6) * 8 + (depth & 7))
    at_ref[1:2, :] = element_rows(((depth >> 3) ^ swap) * 64 + (slot & 63))
    zone = zone_ref[...]
    tan_red = pick(friction_ref, zone) * (1.0 / REDUCTION)
    cos_red = 1.0 / jnp.sqrt(1.0 + tan_red * tan_red)
    sin_red = tan_red * cos_red
    common = 6.0 / (np.sqrt(3.0).astype(np.float32) * (3.0 - sin_red))
    strength_ref[0:1, :] = element_rows(common * (pick(cohesion_ref, zone) * (1.0 / REDUCTION)) * cos_red)
    strength_ref[1:2, :] = element_rows(common * sin_red)


def trial_state(
    sections, place_ref, matrix_ref, disp_ref, after_ref, tail_ref, conn_ref, stress_ref, trial_ref, nodes, corners
):
    ghost = jnp.where(place_ref[0] < sections - 1, after_ref[24:32, :], tail_ref[4])
    for comp in range(3):
        for s in range(8):
            nodes[comp * 12 + s : comp * 12 + s + 1, :] = disp_ref[comp : comp + 1, s * 128 : (s + 1) * 128]
        for s in range(4):
            at = 2 * comp + s // 2
            nodes[comp * 12 + 8 + s : comp * 12 + 9 + s, :] = ghost[at : at + 1, (s % 2) * 128 : (s % 2 + 1) * 128]
    elems = conn_ref.shape[1]

    @pl.loop(0, elems, step=128)
    def _(e):
        e = pl.multiple_of(e, 128)
        index = conn_ref[:, pl.ds(e, 128)]
        lanes, segment = index & 127, index >> 7
        found = [jnp.zeros((8, 128), jnp.float32) for _ in range(3)]
        for s in range(12):
            here = segment == s
            for comp in range(3):
                row = nodes[comp * 12 + s : comp * 12 + s + 1, :]
                found[comp] = jnp.where(here, take_lanes(row, lanes), found[comp])
        for comp in range(3):
            corners[comp * 8 : comp * 8 + 8, pl.ds(e, 128)] = found[comp]

    strain = jnp.dot(
        matrix_ref[...], corners[...], precision=lax.Precision.HIGHEST, preferred_element_type=jnp.float32
    )
    lame_first = YOUNG * POISSON / ((1.0 + POISSON) * (1.0 - 2.0 * POISSON))
    modulus = YOUNG / (2.0 * (1.0 + POISSON))
    part = [strain[8 * i : 8 * i + 8] for i in range(6)]
    volume = lame_first * (part[0] + part[1] + part[2])
    normals = [stress_ref[i] + volume + 2.0 * modulus * part[i] for i in range(3)]
    shears = [stress_ref[i] + modulus * part[i] for i in range(3, 6)]
    mean = (normals[0] + normals[1] + normals[2]) * (1.0 / 3.0)
    devs = [value - mean for value in normals]
    trial_ref[6] = mean
    trial_ref[7] = jnp.sqrt(
        0.5 * (devs[0] ** 2 + devs[1] ** 2 + devs[2] ** 2) + shears[0] ** 2 + shears[1] ** 2 + shears[2] ** 2
    )
    for i in range(3):
        trial_ref[i] = devs[i]
        trial_ref[3 + i] = shears[i]


def halves(value):
    high = value.astype(jnp.bfloat16).astype(jnp.float32)
    return high, value - high


def final_state(
    matrix_ref, band_ref, at_ref, strength_ref, trial_ref, conn_ref, stress_ref, release_ref, own_ref, ghost_ref
):
    elems = conn_ref.shape[1]
    high, low = halves(band_ref[...])
    in_row = lax.broadcasted_iota(jnp.int32, (band_ref.shape[0], elems), 0) == at_ref[0:1, :]
    found = lax.dot_general(
        jnp.concatenate([high, low], axis=1).astype(jnp.bfloat16),
        jnp.where(in_row, 1.0, 0.0).astype(jnp.bfloat16),
        (((0,), (0,)), ((), ())),
        preferred_element_type=jnp.float32,
    )
    found = found[0:128] + found[128:256]
    in_lane = lax.broadcasted_iota(jnp.int32, (128, elems), 0)
    pore = jnp.sum(jnp.where(in_lane == at_ref[1:2, :], found, 0.0), axis=0, keepdims=True)
    allow = jnp.maximum(strength_ref[0:1, :] - strength_ref[1:2, :] * (trial_ref[6] + pore), 0.0)
    deviator = trial_ref[7]
    yielded = deviator > allow
    scale = jnp.where(yielded, allow / jnp.where(yielded, deviator, 1.0), 1.0)
    release_ref[...] = (1.0 - scale) * deviator
    mean = trial_ref[6]
    parts = [mean + scale * trial_ref[i] for i in range(3)] + [scale * trial_ref[3 + i] for i in range(3)]
    for i in range(6):
        stress_ref[i] = parts[i]
    force = jnp.dot(
        matrix_ref[...],
        jnp.concatenate(parts, axis=0),
        precision=lax.Precision.HIGHEST,
        preferred_element_type=jnp.float32,
    )
    in_segment = lax.broadcasted_iota(jnp.int32, (16, elems), 0)
    high, low = halves(force)
    total = jnp.zeros((96, 128), jnp.float32)
    for corner in range(8):
        node = conn_ref[corner : corner + 1, :]
        here = jnp.broadcast_to(node >> 7, in_segment.shape) == in_segment
        rows = []
        for source in (high, low):
            for comp in range(3):
                value = source[comp * 8 + corner : comp * 8 + corner + 1, :]
                rows.append(jnp.where(here, jnp.broadcast_to(value, in_segment.shape), 0.0))
        left = jnp.concatenate(rows, axis=0).astype(jnp.bfloat16)
        right = jnp.where(jnp.broadcast_to(node & 127, in_lane.shape) == in_lane, 1.0, 0.0).astype(jnp.bfloat16)
        total += lax.dot_general(left, right, (((1,), (1,)), ((), ())), preferred_element_type=jnp.float32)
    total = total[0:48] + total[48:96]
    for comp in range(3):
        own_ref[comp * 8 : comp * 8 + 8, :] = total[comp * 16 : comp * 16 + 8]
        ghost_ref[comp * 4 : comp * 4 + 4, :] = total[comp * 16 + 8 : comp * 16 + 12]


def add_returned(own_ref, ghost_ref, shared_ref, out_ref):
    shared = shared_ref[...]
    in_lane = lax.broadcasted_iota(jnp.int32, (128, 128), 0)
    in_segment = lax.broadcasted_iota(jnp.int32, (8, 128), 0)
    lefts, rights = [], []
    for s in range(4):
        node = shared[s : s + 1]
        rights.append(jnp.where(jnp.broadcast_to(node & 127, in_lane.shape) == in_lane, 1.0, 0.0))
        here = jnp.broadcast_to(node >> 7, in_segment.shape) == in_segment
        rows = []
        for comp in range(3):
            value = ghost_ref[comp * 4 + s : comp * 4 + s + 1, :]
            high, low = halves(value)
            for piece in (high, low):
                rows.append(jnp.where(here, jnp.broadcast_to(piece, in_segment.shape), 0.0))
        lefts.append(jnp.concatenate(rows, axis=0))
    left = jnp.concatenate(lefts, axis=1).astype(jnp.bfloat16)
    right = jnp.concatenate(rights, axis=1).astype(jnp.bfloat16)
    added = lax.dot_general(left, right, (((1,), (1,)), ((), ())), preferred_element_type=jnp.float32)
    for comp in range(3):
        total = own_ref[comp * 8 : comp * 8 + 8, :] + added[comp * 16 : comp * 16 + 8] + added[comp * 16 + 8 : comp * 16 + 16]
        for s in range(8):
            out_ref[comp : comp + 1, s * 128 : (s + 1) * 128] = total[s : s + 1]


VM = pl.BlockSpec(memory_space=pltpu.VMEM)
SM = pl.BlockSpec(memory_space=pltpu.SMEM)


HBM = pl.BlockSpec(memory_space=pltpu.HBM)


def call(body, specs, outs, scratch, name, types=None):
    types = types or [jnp.float32] * len(outs)
    return pl.pallas_call(
        body,
        in_specs=specs,
        out_specs=tuple(VM for _ in outs),
        out_shape=tuple(jax.ShapeDtypeStruct(shape, kind) for shape, kind in zip(outs, types)),
        scratch_shapes=scratch,
        compiler_params=pltpu.CompilerParams(vmem_limit_bytes=VMEM_LIMIT),
        name=name,
    )


def in_hbm(value):
    return pltpu.with_memory_space_constraint(value, pltpu.HBM)


def steps(count, by):
    return [(i, (i + by) % count) for i in range(count)]


def per_device(
    pressure_head,
    zone_ids,
    retention_alpha,
    retention_exponent,
    conductivity,
    sent_columns,
    displacement,
    stress_old,
    connectivity,
    shared_nodes,
    element_zone,
    element_slot,
    element_depth,
    cohesion,
    friction,
):
    crest, section = (lax.axis_size(axis) for axis in AXES)
    devices = crest * section
    planes, rows, depth = pressure_head.shape
    height = rows + 8
    elems = connectivity.shape[1]
    nodes = displacement.shape[1]
    shared = shared_nodes.reshape(4, 128)
    zones = retention_alpha.shape[0]
    place = jnp.stack([lax.axis_index("section"), lax.axis_index("crest"), lax.axis_index(AXES)])
    i32, f32 = jnp.int32, jnp.float32

    forward, backward, head, zone = call(
        pack_section,
        [HBM] * 4,
        [(2 * WIDE * planes, depth), (32, depth), pressure_head.shape, zone_ids.shape],
        [pltpu.VMEM(displacement.shape, f32), pltpu.VMEM(shared.shape, i32), pltpu.SemaphoreType.DMA((4,))],
        "pack_section",
        [f32, f32, f32, i32],
    )(*(in_hbm(x) for x in (pressure_head, zone_ids, displacement, shared)))
    before = lax.ppermute(forward, "section", steps(section, 1))
    after = lax.ppermute(backward, "section", steps(section, -1))

    own = (2, WIDE, rows, depth)
    low, high, tables, index = call(
        pack_crest,
        [VM] * 2 + [HBM] * 4,
        [own, own, (4 * zones, depth), (devices, 128)],
        [pltpu.VMEM((64, devices), i32)] + [pltpu.SMEM((zones,), f32)] * 3 + [pltpu.SemaphoreType.DMA((4,))],
        "pack_crest",
        [f32, f32, f32, i32],
    )(head, zone, *(in_hbm(x) for x in (sent_columns[0].T, retention_alpha, retention_exponent, conductivity)))
    west = lax.ppermute(high, "crest", steps(crest, 1))
    east = lax.ppermute(low, "crest", steps(crest, -1))

    low_tail, high_tail = call(
        functools.partial(pack_corners, section), [SM] + [VM] * 2, [(5, 8, depth), (4, 8, depth)], [], "pack_corners"
    )(place, before, after)
    west_tail = lax.ppermute(high_tail, "crest", steps(crest, 1))
    east_tail = lax.ppermute(low_tail, "crest", steps(crest, -1))

    total = planes + 2 * WIDE
    field = pltpu.VMEM((total, height, depth), f32)
    head_out, outgoing, order = call(
        functools.partial(seepage, crest),
        [SM] + [VM] * 10,
        [pressure_head.shape, (devices, 8, 128), (8, 128)],
        [field] * 8 + [pltpu.VMEM((planes * rows, depth), f32), pltpu.VMEM((depth, planes * rows), f32)],
        "seepage",
    )(place, tables, index, low, high, low_tail, high_tail, west, east, west_tail, east_tail)

    matrix = component_major()
    disp, stress, conn, strain_rows, force_rows, strength, places = call(
        functools.partial(selectors, devices),
        [SM, VM] + [HBM] * 10,
        [
            displacement.shape,
            (6, 8, elems),
            connectivity.shape,
            (48, 24),
            (24, 48),
            (2, elems),
            (2, elems),
        ],
        [pltpu.VMEM((8, 128), i32)] * 3 + [pltpu.SMEM((zones,), f32)] * 2 + [pltpu.SemaphoreType.DMA((10,))],
        "selectors",
        [f32, f32, i32, f32, f32, f32, i32],
    )(
        place,
        order,
        *(
            in_hbm(x)
            for x in (
                displacement,
                stress_old.transpose(1, 0, 2),
                connectivity,
                jnp.asarray(matrix, f32),
                jnp.asarray(matrix.T * 0.125, f32),
                element_slot.reshape(8, 128),
                element_depth.reshape(8, 128),
                element_zone.reshape(8, 128),
                cohesion,
                friction,
            )
        ),
    )
    (trial,) = call(
        functools.partial(trial_state, section),
        [SM] + [VM] * 6,
        [(8, 8, elems)],
        [pltpu.VMEM((40, 128), f32), pltpu.VMEM((24, elems), f32)],
        "trial_state",
    )(place, strain_rows, disp, after, east_tail, conn, stress)
    incoming = lax.all_to_all(outgoing, AXES, split_axis=0, concat_axis=0, tiled=True)

    stress_new, release, own, ghost = call(
        final_state,
        [VM] * 6,
        [(6, 8, elems), (8, elems), (24, 128), (12, 128)],
        [],
        "final_state",
    )(force_rows, incoming.reshape(devices * 8, 128), places, strength, trial, conn)
    returned = lax.ppermute(ghost, AXES, steps(devices, 1))
    (node_forces,) = call(add_returned, [VM] * 3, [(3, nodes)], [], "add_returned")(own, returned, shared)
    return (head_out, stress_new.transpose(1, 0, 2), release, node_forces)


def solution(mesh):
    return jax.shard_map(
        per_device,
        mesh=mesh,
        in_specs=(
            P("crest", "section", None),
            P("crest", "section", None),
            P(),
            P(),
            P(),
            P(("crest", "section"), None, None),
            P(None, ("crest", "section")),
            P(None, None, ("crest", "section")),
            P(None, ("crest", "section")),
            P(("crest", "section")),
            P(("crest", "section")),
            P(("crest", "section")),
            P(("crest", "section")),
            P(),
            P(),
        ),
        out_specs=(
            P("crest", "section", None),
            P(None, None, ("crest", "section")),
            P(None, ("crest", "section")),
            P(None, ("crest", "section")),
        ),
        check_vma=False,
    )
```

```python
import functools

import jax
import jax.numpy as jnp
import numpy as np
from jax import lax
from jax.experimental import pallas as pl
from jax.experimental.pallas import tpu as pltpu
from jax.sharding import PartitionSpec as P

BAND = 16
SWEEPS = 3
WIDE = 3

STORAGE = 0.5
THETA_GAP = 0.35
TIME_STEP = 0.05
REDUCTION = 1.4
YOUNG = 200.0
POISSON = 0.3

AXES = ("crest", "section")
VMEM_LIMIT = 32 * 1024 * 1024


def corner_signs(index):
    return (2 * (index & 1) - 1, 2 * (index >> 1 & 1) - 1, 2 * (index >> 2 & 1) - 1)


def strain_matrix():
    matrix = np.zeros((48, 24))
    inv_root = 1.0 / np.sqrt(3.0)
    for gauss_point in range(8):
        gauss = [value * inv_root for value in corner_signs(gauss_point)]
        row_start = 6 * gauss_point
        for node_corner in range(8):
            sign_x, sign_y, sign_z = corner_signs(node_corner)
            grad_x = 0.25 * sign_x * (1 + gauss[1] * sign_y) * (1 + gauss[2] * sign_z)
            grad_y = 0.25 * sign_y * (1 + gauss[0] * sign_x) * (1 + gauss[2] * sign_z)
            grad_z = 0.25 * sign_z * (1 + gauss[0] * sign_x) * (1 + gauss[1] * sign_y)
            matrix[row_start + 0, node_corner] = grad_x
            matrix[row_start + 1, 8 + node_corner] = grad_y
            matrix[row_start + 2, 16 + node_corner] = grad_z
            matrix[row_start + 3, node_corner] = grad_y
            matrix[row_start + 3, 8 + node_corner] = grad_x
            matrix[row_start + 4, 8 + node_corner] = grad_z
            matrix[row_start + 4, 16 + node_corner] = grad_y
            matrix[row_start + 5, 16 + node_corner] = grad_x
            matrix[row_start + 5, node_corner] = grad_z
    return matrix


def component_major():
    order = [6 * gauss_point + comp for comp in range(6) for gauss_point in range(8)]
    return strain_matrix()[order]


def take_lanes(row, lanes):
    return jnp.take_along_axis(jnp.broadcast_to(row, lanes.shape), lanes, axis=1, mode="promise_in_bounds")


def pick(values_ref, index, first=0):
    lane = lax.broadcasted_iota(jnp.int32, (8, 128), 1)
    table = jnp.zeros((8, 128), jnp.float32)
    for zone in range(values_ref.shape[0]):
        table = jnp.where(lane == first + zone, values_ref[zone], table)
    return table if index is None else take_lanes(table, index)


def fetch(pairs, sems):
    copies = [pltpu.make_async_copy(source, target, sems.at[i]) for i, (source, target) in enumerate(pairs)]
    for copy in copies:
        copy.start()
    for copy in copies:
        copy.wait()


def pack_section(
    head_hbm, zone_hbm, disp_hbm, shared_hbm, forward_ref, backward_ref, head_ref, zone_ref, disp_ref, shared_ref, sems
):
    fetch([(head_hbm, head_ref), (zone_hbm, zone_ref), (disp_hbm, disp_ref), (shared_hbm, shared_ref)], sems)
    planes, rows = head_ref.shape[0], head_ref.shape[1]
    for x in range(planes):
        for field in range(2):
            first, last = slice(0, WIDE), slice(rows - WIDE, rows)
            at = field * WIDE * planes + WIDE * x
            if field == 0:
                forward_ref[at : at + WIDE, :] = head_ref[x, last, :]
                backward_ref[at : at + WIDE, :] = head_ref[x, first, :]
            else:
                forward_ref[at : at + WIDE, :] = zone_ref[x, last, :].astype(jnp.float32) + 1.0
                backward_ref[at : at + WIDE, :] = zone_ref[x, first, :].astype(jnp.float32) + 1.0
    index = shared_ref[...]
    index = jnp.concatenate([index, index], axis=0)
    lanes, segment = index & 127, index >> 7
    for comp in range(3):
        found = jnp.zeros((8, 128), jnp.float32)
        for s in range(disp_ref.shape[1] // 128):
            row = disp_ref[comp : comp + 1, s * 128 : (s + 1) * 128]
            found = jnp.where(segment == s, take_lanes(row, lanes), found)
        for s in range(4):
            at = 2 * WIDE * planes + 2 * comp + s // 2
            backward_ref[at : at + 1, (s % 2) * 128 : (s % 2 + 1) * 128] = found[s : s + 1]
    backward_ref[30:32, :] = jnp.zeros((2, 256), jnp.float32)


def pack_crest(
    head_ref,
    zone_ref,
    wanted_hbm,
    alpha_hbm,
    expo_hbm,
    ks_hbm,
    low_ref,
    high_ref,
    tables_ref,
    index_ref,
    wanted_ref,
    alpha_ref,
    expo_ref,
    ks_ref,
    sems,
):
    pairs = [(wanted_hbm, wanted_ref), (alpha_hbm, alpha_ref), (expo_hbm, expo_ref), (ks_hbm, ks_ref)]
    copies = [pltpu.make_async_copy(source, target, sems.at[i]) for i, (source, target) in enumerate(pairs)]
    for copy in copies:
        copy.start()
    planes = head_ref.shape[0]
    for x in range(planes):
        own = [head_ref[x], zone_ref[x].astype(jnp.float32) + 1.0]
        for field in range(2):
            if x < WIDE:
                low_ref[field, x] = own[field]
            if x >= planes - WIDE:
                high_ref[field, x - planes + WIDE] = own[field]
    for copy in copies:
        copy.wait()
    zones, width = alpha_ref.shape[0], tables_ref.shape[1]
    for z in range(zones):
        expo = jnp.full((1, width), expo_ref[z], jnp.float32)
        expo = jnp.where(expo > 0, expo, 2.0)
        tables_ref[z : z + 1, :] = jnp.full((1, width), alpha_ref[z], jnp.float32)
        tables_ref[zones + z : zones + z + 1, :] = expo - 1.0
        tables_ref[2 * zones + z : 2 * zones + z + 1, :] = -0.25 * (1.0 - 1.0 / expo)
        tables_ref[3 * zones + z : 3 * zones + z + 1, :] = jnp.sqrt(jnp.full((1, width), ks_ref[z], jnp.float32))
    wanted = wanted_ref[...]
    index_ref[...] = jnp.concatenate([wanted, pltpu.roll(wanted, wanted.shape[1] // 2, 1)], axis=0).T


def pack_corners(sections, place_ref, before_ref, after_ref, low_ref, high_ref):
    planes = high_ref.shape[0]
    behind = jnp.where(place_ref[0] > 0, 1.0, 0.0)
    ahead = jnp.where(place_ref[0] < sections - 1, 1.0, 0.0)
    for x in range(planes):
        for field in range(2):
            at = field * WIDE * planes + WIDE * x
            tail = jnp.concatenate(
                [
                    after_ref[at : at + WIDE, :] * ahead,
                    jnp.zeros((2, after_ref.shape[1]), jnp.float32),
                    before_ref[at : at + WIDE, :] * behind,
                ],
                axis=0,
            )
            if x < 2:
                low_ref[2 * field + x] = tail
            else:
                high_ref[2 * field + x - 2] = tail
    low_ref[4] = after_ref[24:32, :]


def seepage(
    crests,
    place_ref,
    tables_ref,
    index,
    low_ref,
    high_ref,
    low_tail_ref,
    high_tail_ref,
    before_ref,
    after_ref,
    before_tail_ref,
    after_tail_ref,
    head_ref,
    out_ref,
    order_ref,
    h,
    alpha_f,
    less_f,
    m_f,
    root_f,
    gain_f,
    r_f,
    cap_f,
    table,
    deep,
):
    planes = head_ref.shape[0]
    rows = head_ref.shape[1]
    total = planes + 2 * WIDE
    height, depth = h.shape[1], h.shape[2]
    lane8 = lax.broadcasted_iota(jnp.int32, (8, 128), 1)
    zones = tables_ref.shape[0] // 4
    alpha_t, less_t, m_t, root_t = (
        [jnp.broadcast_to(tables_ref[f * zones + z : f * zones + z + 1, :], (8, depth)) for z in range(zones)]
        for f in range(4)
    )
    behind = jnp.where(place_ref[1] > 0, 1.0, 0.0)
    ahead = jnp.where(place_ref[1] < crests - 1, 1.0, 0.0)

    def fields(x, row, head, zone):
        at = slice(row, row + 8)
        h[x, at, :] = head
        zone = zone.astype(jnp.int32) - 1
        bits = [(zone & (1 << bit)) != 0 for bit in range(3)]

        def choose(values):
            for bit in bits:
                values = [jnp.where(bit, values[i + 1], values[i]) for i in range(0, len(values), 2)]
            return values[0]

        alpha, less = choose(alpha_t), choose(less_t)
        alpha_f[x, at, :] = alpha
        less_f[x, at, :] = less
        m_f[x, at, :] = choose(m_t)
        root_f[x, at, :] = jnp.where(zone >= 0, choose(root_t), 0.0)
        gain_f[x, at, :] = THETA_GAP * alpha * less

    def body_rows(x, source, plane, inside=None):
        for row in range(0, rows, 8):
            zone = source[1, plane, row : row + 8, :]
            fields(x, row, source[0, plane, row : row + 8, :], zone if inside is None else zone * inside)

    for x in range(WIDE):
        body_rows(x, before_ref, x, behind)
        body_rows(WIDE + x, low_ref, x)
        body_rows(WIDE + planes + x, after_ref, x, ahead)

    body_rows(2 * WIDE, high_ref, WIDE - 1)

    for x in range(2):
        fields(1 + x, rows, before_tail_ref[x], before_tail_ref[2 + x] * behind)
        fields(3 + x, rows, low_tail_ref[x], low_tail_ref[2 + x])
        fields(5 + x, rows, high_tail_ref[x], high_tail_ref[2 + x])
        fields(7 + x, rows, after_tail_ref[x], after_tail_ref[2 + x] * ahead)

    for x in (0, total - 1):
        for field in (h, alpha_f, less_f, m_f, root_f, gain_f):
            field[x, rows:height, :] = jnp.zeros((height - rows, depth), jnp.float32)

    def base(x):
        scaled = alpha_f[x] * jnp.maximum(-h[x], 0.0)
        power = jnp.exp(less_f[x] * jnp.log(jnp.maximum(scaled, 1e-30)))
        plus = 1.0 + power * scaled
        return power, plus, jnp.log(plus)

    def retention(x):
        power, plus, log_plus = base(x)
        fourth = jnp.exp(m_f[x] * log_plus)
        square = fourth * fourth
        part = power * (square * square)
        r_f[x] = root_f[x] * fourth * (1.0 - part)
        cap_f[x] = TIME_STEP * plus / (STORAGE * plus + gain_f[x] * part)

    inner_z = lax.broadcasted_iota(jnp.int32, (height, depth), 1) < depth - 1

    def face(x):
        return r_f[x] * r_f[x + 1] * (h[x + 1] - h[x])

    for sweep in range(SWEEPS):

        for x in range(sweep, total - sweep):
            retention(x)

        def update(x, came):
            here, r = h[x], r_f[x]
            goes = face(x)
            flux_y = r * pltpu.roll(r, height - 1, 0) * (pltpu.roll(here, height - 1, 0) - here)
            flux_z = r * pltpu.roll(r, depth - 1, 1) * (pltpu.roll(here, depth - 1, 1) - here + 1.0)
            flux_z = jnp.where(inner_z, flux_z, 0.0)
            inflow = goes - came + (flux_y - pltpu.roll(flux_y, 1, 0)) + (flux_z - pltpu.roll(flux_z, 1, 1))
            h[x] = here + cap_f[x] * inflow
            return goes

        came = face(sweep)
        for x in range(sweep + 1, total - sweep - 1):
            came = update(x, came)

    for x in range(planes):
        _, _, log_plus = base(WIDE + x)
        here = h[WIDE + x][0:rows]
        head_ref[x] = here
        table[x * rows : (x + 1) * rows, :] = jnp.exp(4.0 * m_f[WIDE + x] * log_plus)[0:rows] * here
    deep[...] = table[...].T
    bands = depth // BAND

    order_ref[...] = deep[0:8, :]
    half = out_ref.shape[0] // 2

    for b in range(bands):
        upper = deep[b * BAND : b * BAND + 8, :]
        lower = deep[b * BAND + 8 : b * BAND + 16, :]
        for d in range(b, half, bands):
            columns = jnp.broadcast_to(index[d : d + 1, :], (8, 128))
            first, second = take_lanes(upper, columns), pltpu.roll(take_lanes(lower, columns), 64, 1)
            out_ref[d] = jnp.where(lane8 < 64, first, second)
            out_ref[half + d] = jnp.where(lane8 < 64, second, first)


def element_rows(value):
    return jnp.concatenate([value[r : r + 1] for r in range(8)], axis=1)


def selectors(
    partitions,
    place_ref,
    order_ref,
    disp_hbm,
    stress_hbm,
    conn_hbm,
    strain_hbm,
    force_hbm,
    slot_hbm,
    depth_hbm,
    zone_hbm,
    cohesion_hbm,
    friction_hbm,
    disp_ref,
    stress_ref,
    conn_ref,
    strain_ref,
    force_ref,
    strength_ref,
    at_ref,
    slot_ref,
    depth_ref,
    zone_ref,
    cohesion_ref,
    friction_ref,
    sems,
):
    del order_ref
    fetch(
        [
            (conn_hbm, conn_ref),
            (slot_hbm, slot_ref),
            (depth_hbm, depth_ref),
            (zone_hbm, zone_ref),
            (cohesion_hbm, cohesion_ref),
            (friction_hbm, friction_ref),
            (disp_hbm, disp_ref),
            (stress_hbm, stress_ref),
            (strain_hbm, strain_ref),
            (force_hbm, force_ref),
        ],
        sems,
    )
    elems = conn_ref.shape[1]
    slot, depth = slot_ref[...], depth_ref[...]
    swap = jnp.where(place_ref[2] >= partitions // 2, 1, 0)
    at_ref[0:1, :] = element_rows((slot >> 6) * 8 + (depth & 7))
    at_ref[1:2, :] = element_rows(((depth >> 3) ^ swap) * 64 + (slot & 63))
    zone = zone_ref[...]
    tan_red = pick(friction_ref, zone) * (1.0 / REDUCTION)
    cos_red = 1.0 / jnp.sqrt(1.0 + tan_red * tan_red)
    sin_red = tan_red * cos_red
    common = 6.0 / (np.sqrt(3.0).astype(np.float32) * (3.0 - sin_red))
    strength_ref[0:1, :] = element_rows(common * (pick(cohesion_ref, zone) * (1.0 / REDUCTION)) * cos_red)
    strength_ref[1:2, :] = element_rows(common * sin_red)


def trial_state(
    sections, place_ref, matrix_ref, disp_ref, after_ref, tail_ref, conn_ref, stress_ref, trial_ref, nodes, corners
):
    ghost = jnp.where(place_ref[0] < sections - 1, after_ref[24:32, :], tail_ref[4])
    for comp in range(3):
        for s in range(8):
            nodes[comp * 12 + s : comp * 12 + s + 1, :] = disp_ref[comp : comp + 1, s * 128 : (s + 1) * 128]
        for s in range(4):
            at = 2 * comp + s // 2
            nodes[comp * 12 + 8 + s : comp * 12 + 9 + s, :] = ghost[at : at + 1, (s % 2) * 128 : (s % 2 + 1) * 128]
    elems = conn_ref.shape[1]

    @pl.loop(0, elems, step=128)
    def _(e):
        e = pl.multiple_of(e, 128)
        index = conn_ref[:, pl.ds(e, 128)]
        lanes, segment = index & 127, index >> 7
        found = [jnp.zeros((8, 128), jnp.float32) for _ in range(3)]
        for s in range(12):
            here = segment == s
            for comp in range(3):
                row = nodes[comp * 12 + s : comp * 12 + s + 1, :]
                found[comp] = jnp.where(here, take_lanes(row, lanes), found[comp])
        for comp in range(3):
            corners[comp * 8 : comp * 8 + 8, pl.ds(e, 128)] = found[comp]

    strain = jnp.dot(
        matrix_ref[...], corners[...], precision=lax.Precision.HIGHEST, preferred_element_type=jnp.float32
    )
    lame_first = YOUNG * POISSON / ((1.0 + POISSON) * (1.0 - 2.0 * POISSON))
    modulus = YOUNG / (2.0 * (1.0 + POISSON))
    part = [strain[8 * i : 8 * i + 8] for i in range(6)]
    volume = lame_first * (part[0] + part[1] + part[2])
    normals = [stress_ref[i] + volume + 2.0 * modulus * part[i] for i in range(3)]
    shears = [stress_ref[i] + modulus * part[i] for i in range(3, 6)]
    mean = (normals[0] + normals[1] + normals[2]) * (1.0 / 3.0)
    devs = [value - mean for value in normals]
    trial_ref[6] = mean
    trial_ref[7] = jnp.sqrt(
        0.5 * (devs[0] ** 2 + devs[1] ** 2 + devs[2] ** 2) + shears[0] ** 2 + shears[1] ** 2 + shears[2] ** 2
    )
    for i in range(3):
        trial_ref[i] = devs[i]
        trial_ref[3 + i] = shears[i]


def halves(value):
    high = value.astype(jnp.bfloat16).astype(jnp.float32)
    return high, value - high


def final_state(
    matrix_ref, band_ref, at_ref, strength_ref, trial_ref, conn_ref, stress_ref, release_ref, own_ref, ghost_ref
):
    elems = conn_ref.shape[1]
    high, low = halves(band_ref[...])
    in_row = lax.broadcasted_iota(jnp.int32, (band_ref.shape[0], elems), 0) == at_ref[0:1, :]
    found = lax.dot_general(
        jnp.concatenate([high, low], axis=1).astype(jnp.bfloat16),
        jnp.where(in_row, 1.0, 0.0).astype(jnp.bfloat16),
        (((0,), (0,)), ((), ())),
        preferred_element_type=jnp.float32,
    )
    found = found[0:128] + found[128:256]
    in_lane = lax.broadcasted_iota(jnp.int32, (128, elems), 0)
    pore = jnp.sum(jnp.where(in_lane == at_ref[1:2, :], found, 0.0), axis=0, keepdims=True)
    allow = jnp.maximum(strength_ref[0:1, :] - strength_ref[1:2, :] * (trial_ref[6] + pore), 0.0)
    deviator = trial_ref[7]
    yielded = deviator > allow
    scale = jnp.where(yielded, allow / jnp.where(yielded, deviator, 1.0), 1.0)
    release_ref[...] = (1.0 - scale) * deviator
    mean = trial_ref[6]
    parts = [mean + scale * trial_ref[i] for i in range(3)] + [scale * trial_ref[3 + i] for i in range(3)]
    for i in range(6):
        stress_ref[i] = parts[i]
    force = jnp.dot(
        matrix_ref[...],
        jnp.concatenate(parts, axis=0),
        precision=lax.Precision.HIGHEST,
        preferred_element_type=jnp.float32,
    )
    in_segment = lax.broadcasted_iota(jnp.int32, (16, elems), 0)
    high, low = halves(force)
    total = jnp.zeros((96, 128), jnp.float32)
    for corner in range(8):
        node = conn_ref[corner : corner + 1, :]
        here = jnp.broadcast_to(node >> 7, in_segment.shape) == in_segment
        rows = []
        for source in (high, low):
            for comp in range(3):
                value = source[comp * 8 + corner : comp * 8 + corner + 1, :]
                rows.append(jnp.where(here, jnp.broadcast_to(value, in_segment.shape), 0.0))
        left = jnp.concatenate(rows, axis=0).astype(jnp.bfloat16)
        right = jnp.where(jnp.broadcast_to(node & 127, in_lane.shape) == in_lane, 1.0, 0.0).astype(jnp.bfloat16)
        total += lax.dot_general(left, right, (((1,), (1,)), ((), ())), preferred_element_type=jnp.float32)
    total = total[0:48] + total[48:96]
    for comp in range(3):
        own_ref[comp * 8 : comp * 8 + 8, :] = total[comp * 16 : comp * 16 + 8]
        ghost_ref[comp * 4 : comp * 4 + 4, :] = total[comp * 16 + 8 : comp * 16 + 12]


def add_returned(own_ref, ghost_ref, shared_ref, out_ref):
    shared = shared_ref[...]
    in_lane = lax.broadcasted_iota(jnp.int32, (128, 128), 0)
    in_segment = lax.broadcasted_iota(jnp.int32, (8, 128), 0)
    lefts, rights = [], []
    for s in range(4):
        node = shared[s : s + 1]
        rights.append(jnp.where(jnp.broadcast_to(node & 127, in_lane.shape) == in_lane, 1.0, 0.0))
        here = jnp.broadcast_to(node >> 7, in_segment.shape) == in_segment
        rows = []
        for comp in range(3):
            value = ghost_ref[comp * 4 + s : comp * 4 + s + 1, :]
            high, low = halves(value)
            for piece in (high, low):
                rows.append(jnp.where(here, jnp.broadcast_to(piece, in_segment.shape), 0.0))
        lefts.append(jnp.concatenate(rows, axis=0))
    left = jnp.concatenate(lefts, axis=1).astype(jnp.bfloat16)
    right = jnp.concatenate(rights, axis=1).astype(jnp.bfloat16)
    added = lax.dot_general(left, right, (((1,), (1,)), ((), ())), preferred_element_type=jnp.float32)
    for comp in range(3):
        total = own_ref[comp * 8 : comp * 8 + 8, :] + added[comp * 16 : comp * 16 + 8] + added[comp * 16 + 8 : comp * 16 + 16]
        for s in range(8):
            out_ref[comp : comp + 1, s * 128 : (s + 1) * 128] = total[s : s + 1]


VM = pl.BlockSpec(memory_space=pltpu.VMEM)
SM = pl.BlockSpec(memory_space=pltpu.SMEM)


HBM = pl.BlockSpec(memory_space=pltpu.HBM)


def call(body, specs, outs, scratch, name, types=None):
    types = types or [jnp.float32] * len(outs)
    return pl.pallas_call(
        body,
        in_specs=specs,
        out_specs=tuple(VM for _ in outs),
        out_shape=tuple(jax.ShapeDtypeStruct(shape, kind) for shape, kind in zip(outs, types)),
        scratch_shapes=scratch,
        compiler_params=pltpu.CompilerParams(vmem_limit_bytes=VMEM_LIMIT),
        name=name,
    )


def in_hbm(value):
    return pltpu.with_memory_space_constraint(value, pltpu.HBM)


def steps(count, by):
    return [(i, (i + by) % count) for i in range(count)]


def per_device(
    pressure_head,
    zone_ids,
    retention_alpha,
    retention_exponent,
    conductivity,
    sent_columns,
    displacement,
    stress_old,
    connectivity,
    shared_nodes,
    element_zone,
    element_slot,
    element_depth,
    cohesion,
    friction,
):
    crest, section = (lax.axis_size(axis) for axis in AXES)
    devices = crest * section
    planes, rows, depth = pressure_head.shape
    height = rows + 8
    elems = connectivity.shape[1]
    nodes = displacement.shape[1]
    shared = shared_nodes.reshape(4, 128)
    zones = retention_alpha.shape[0]
    place = jnp.stack([lax.axis_index("section"), lax.axis_index("crest"), lax.axis_index(AXES)])
    i32, f32 = jnp.int32, jnp.float32

    forward, backward, head, zone = call(
        pack_section,
        [HBM] * 4,
        [(2 * WIDE * planes, depth), (32, depth), pressure_head.shape, zone_ids.shape],
        [pltpu.VMEM(displacement.shape, f32), pltpu.VMEM(shared.shape, i32), pltpu.SemaphoreType.DMA((4,))],
        "pack_section",
        [f32, f32, f32, i32],
    )(*(in_hbm(x) for x in (pressure_head, zone_ids, displacement, shared)))
    before = lax.ppermute(forward, "section", steps(section, 1))
    after = lax.ppermute(backward, "section", steps(section, -1))

    own = (2, WIDE, rows, depth)
    low, high, tables, index = call(
        pack_crest,
        [VM] * 2 + [HBM] * 4,
        [own, own, (4 * zones, depth), (devices, 128)],
        [pltpu.VMEM((64, devices), i32)] + [pltpu.SMEM((zones,), f32)] * 3 + [pltpu.SemaphoreType.DMA((4,))],
        "pack_crest",
        [f32, f32, f32, i32],
    )(head, zone, *(in_hbm(x) for x in (sent_columns[0].T, retention_alpha, retention_exponent, conductivity)))
    west = lax.ppermute(high, "crest", steps(crest, 1))
    east = lax.ppermute(low, "crest", steps(crest, -1))

    low_tail, high_tail = call(
        functools.partial(pack_corners, section), [SM] + [VM] * 2, [(5, 8, depth), (4, 8, depth)], [], "pack_corners"
    )(place, before, after)
    west_tail = lax.ppermute(high_tail, "crest", steps(crest, 1))
    east_tail = lax.ppermute(low_tail, "crest", steps(crest, -1))

    total = planes + 2 * WIDE
    field = pltpu.VMEM((total, height, depth), f32)
    head_out, outgoing, order = call(
        functools.partial(seepage, crest),
        [SM] + [VM] * 10,
        [pressure_head.shape, (devices, 8, 128), (8, 128)],
        [field] * 8 + [pltpu.VMEM((planes * rows, depth), f32), pltpu.VMEM((depth, planes * rows), f32)],
        "seepage",
    )(place, tables, index, low, high, low_tail, high_tail, west, east, west_tail, east_tail)

    matrix = component_major()
    disp, stress, conn, strain_rows, force_rows, strength, places = call(
        functools.partial(selectors, devices),
        [SM, VM] + [HBM] * 10,
        [
            displacement.shape,
            (6, 8, elems),
            connectivity.shape,
            (48, 24),
            (24, 48),
            (2, elems),
            (2, elems),
        ],
        [pltpu.VMEM((8, 128), i32)] * 3 + [pltpu.SMEM((zones,), f32)] * 2 + [pltpu.SemaphoreType.DMA((10,))],
        "selectors",
        [f32, f32, i32, f32, f32, f32, i32],
    )(
        place,
        order,
        *(
            in_hbm(x)
            for x in (
                displacement,
                stress_old.transpose(1, 0, 2),
                connectivity,
                jnp.asarray(matrix, f32),
                jnp.asarray(matrix.T * 0.125, f32),
                element_slot.reshape(8, 128),
                element_depth.reshape(8, 128),
                element_zone.reshape(8, 128),
                cohesion,
                friction,
            )
        ),
    )
    (trial,) = call(
        functools.partial(trial_state, section),
        [SM] + [VM] * 6,
        [(8, 8, elems)],
        [pltpu.VMEM((40, 128), f32), pltpu.VMEM((24, elems), f32)],
        "trial_state",
    )(place, strain_rows, disp, after, east_tail, conn, stress)
    incoming = lax.all_to_all(outgoing, AXES, split_axis=0, concat_axis=0, tiled=True)

    stress_new, release, own, ghost = call(
        final_state,
        [VM] * 6,
        [(6, 8, elems), (8, elems), (24, 128), (12, 128)],
        [],
        "final_state",
    )(force_rows, incoming.reshape(devices * 8, 128), places, strength, trial, conn)
    returned = lax.ppermute(ghost, AXES, steps(devices, 1))
    (node_forces,) = call(add_returned, [VM] * 3, [(3, nodes)], [], "add_returned")(own, returned, shared)
    return (head_out, stress_new.transpose(1, 0, 2), release, node_forces)


def solution(mesh):
    return jax.shard_map(
        per_device,
        mesh=mesh,
        in_specs=(
            P("crest", "section", None),
            P("crest", "section", None),
            P(),
            P(),
            P(),
            P(("crest", "section"), None, None),
            P(None, ("crest", "section")),
            P(None, None, ("crest", "section")),
            P(None, ("crest", "section")),
            P(("crest", "section")),
            P(("crest", "section")),
            P(("crest", "section")),
            P(("crest", "section")),
            P(),
            P(),
        ),
        out_specs=(
            P("crest", "section", None),
            P(None, None, ("crest", "section")),
            P(None, ("crest", "section")),
            P(None, ("crest", "section")),
        ),
        check_vma=False,
    )
```

```python
import functools

import jax
import jax.numpy as jnp
import numpy as np
from jax import lax
from jax.experimental import pallas as pl
from jax.experimental.pallas import tpu as pltpu
from jax.sharding import PartitionSpec as P

BAND = 16
SWEEPS = 3
WIDE = 3

STORAGE = 0.5
THETA_GAP = 0.35
TIME_STEP = 0.05
REDUCTION = 1.4
YOUNG = 200.0
POISSON = 0.3

AXES = ("crest", "section")
VMEM_LIMIT = 32 * 1024 * 1024


def corner_signs(index):
    return (2 * (index & 1) - 1, 2 * (index >> 1 & 1) - 1, 2 * (index >> 2 & 1) - 1)


def strain_matrix():
    matrix = np.zeros((48, 24))
    inv_root = 1.0 / np.sqrt(3.0)
    for gauss_point in range(8):
        gauss = [value * inv_root for value in corner_signs(gauss_point)]
        row_start = 6 * gauss_point
        for node_corner in range(8):
            sign_x, sign_y, sign_z = corner_signs(node_corner)
            grad_x = 0.25 * sign_x * (1 + gauss[1] * sign_y) * (1 + gauss[2] * sign_z)
            grad_y = 0.25 * sign_y * (1 + gauss[0] * sign_x) * (1 + gauss[2] * sign_z)
            grad_z = 0.25 * sign_z * (1 + gauss[0] * sign_x) * (1 + gauss[1] * sign_y)
            matrix[row_start + 0, node_corner] = grad_x
            matrix[row_start + 1, 8 + node_corner] = grad_y
            matrix[row_start + 2, 16 + node_corner] = grad_z
            matrix[row_start + 3, node_corner] = grad_y
            matrix[row_start + 3, 8 + node_corner] = grad_x
            matrix[row_start + 4, 8 + node_corner] = grad_z
            matrix[row_start + 4, 16 + node_corner] = grad_y
            matrix[row_start + 5, 16 + node_corner] = grad_x
            matrix[row_start + 5, node_corner] = grad_z
    return matrix


def component_major():
    order = [6 * gauss_point + comp for comp in range(6) for gauss_point in range(8)]
    return strain_matrix()[order]


def take_lanes(row, lanes):
    return jnp.take_along_axis(jnp.broadcast_to(row, lanes.shape), lanes, axis=1, mode="promise_in_bounds")


def pick(values_ref, index, first=0):
    lane = lax.broadcasted_iota(jnp.int32, (8, 128), 1)
    table = jnp.zeros((8, 128), jnp.float32)
    for zone in range(values_ref.shape[0]):
        table = jnp.where(lane == first + zone, values_ref[zone], table)
    return table if index is None else take_lanes(table, index)


def fetch(pairs, sems):
    copies = [pltpu.make_async_copy(source, target, sems.at[i]) for i, (source, target) in enumerate(pairs)]
    for copy in copies:
        copy.start()
    for copy in copies:
        copy.wait()


def pack_section(
    head_hbm, zone_hbm, disp_hbm, shared_hbm, forward_ref, backward_ref, head_ref, zone_ref, disp_ref, shared_ref, sems
):
    fetch([(head_hbm, head_ref), (zone_hbm, zone_ref), (disp_hbm, disp_ref), (shared_hbm, shared_ref)], sems)
    planes, rows = head_ref.shape[0], head_ref.shape[1]
    for x in range(planes):
        for field in range(2):
            first, last = slice(0, WIDE), slice(rows - WIDE, rows)
            at = field * WIDE * planes + WIDE * x
            if field == 0:
                forward_ref[at : at + WIDE, :] = head_ref[x, last, :]
                backward_ref[at : at + WIDE, :] = head_ref[x, first, :]
            else:
                forward_ref[at : at + WIDE, :] = zone_ref[x, last, :].astype(jnp.float32) + 1.0
                backward_ref[at : at + WIDE, :] = zone_ref[x, first, :].astype(jnp.float32) + 1.0
    index = shared_ref[...]
    index = jnp.concatenate([index, index], axis=0)
    lanes, segment = index & 127, index >> 7
    for comp in range(3):
        found = jnp.zeros((8, 128), jnp.float32)
        for s in range(disp_ref.shape[1] // 128):
            row = disp_ref[comp : comp + 1, s * 128 : (s + 1) * 128]
            found = jnp.where(segment == s, take_lanes(row, lanes), found)
        for s in range(4):
            at = 2 * WIDE * planes + 2 * comp + s // 2
            backward_ref[at : at + 1, (s % 2) * 128 : (s % 2 + 1) * 128] = found[s : s + 1]
    backward_ref[30:32, :] = jnp.zeros((2, 256), jnp.float32)


def pack_crest(sections, place_ref, head_ref, zone_ref, before_ref, after_ref, low_ref, high_ref):
    planes, rows = head_ref.shape[0], head_ref.shape[1]
    groups = rows // 8
    behind = jnp.where(place_ref[0] > 0, 1.0, 0.0)
    ahead = jnp.where(place_ref[0] < sections - 1, 1.0, 0.0)
    for field in range(2):
        first = field * (WIDE * groups + 2)
        for x in range(planes):
            for group in range(groups):
                at = slice(8 * group, 8 * group + 8)
                own = head_ref[x, at, :] if field == 0 else zone_ref[x, at, :].astype(jnp.float32) + 1.0
                if x < WIDE:
                    low_ref[first + x * groups + group] = own
                if x >= planes - WIDE:
                    high_ref[first + (x - planes + WIDE) * groups + group] = own
            at = field * WIDE * planes + WIDE * x
            tail = jnp.concatenate(
                [
                    after_ref[at : at + WIDE, :] * ahead,
                    jnp.zeros((2, after_ref.shape[1]), jnp.float32),
                    before_ref[at : at + WIDE, :] * behind,
                ],
                axis=0,
            )
            if x < 2:
                low_ref[first + WIDE * groups + x] = tail
            else:
                high_ref[first + WIDE * groups + x - 2] = tail
    low_ref[2 * (WIDE * groups + 2)] = after_ref[24:32, :]


def choose(values, bits):
    for bit in bits:
        values = [jnp.where(bit, values[i + 1], values[i]) for i in range(0, len(values), 2)]
    return values[0]


def fields(tables_ref, out, x, row, head, zone):
    zones = tables_ref.shape[0] // 4
    tables = [
        [jnp.broadcast_to(tables_ref[f * zones + z : f * zones + z + 1, :], head.shape) for z in range(zones)]
        for f in range(4)
    ]
    zone = zone.astype(jnp.int32) - 1
    bits = [(zone & (1 << bit)) != 0 for bit in range(3)]
    alpha, less, m, root = (choose(table, bits) for table in tables)
    values = (head, alpha, less, m, jnp.where(zone >= 0, root, 0.0), THETA_GAP * alpha * less)
    for ref, value in zip(out, values):
        ref[x, row : row + 8, :] = value


def base(alpha, less, h):
    scaled = alpha * jnp.maximum(-h, 0.0)
    power = jnp.exp(less * jnp.log(jnp.maximum(scaled, 1e-30)))
    plus = 1.0 + power * scaled
    return power, plus, jnp.log(plus)


def retention(h, alpha, less, m, root, gain):
    power, plus, log_plus = base(alpha, less, h)
    fourth = jnp.exp(m * log_plus)
    square = fourth * fourth
    part = power * (square * square)
    return root * fourth * (1.0 - part), TIME_STEP * plus / (STORAGE * plus + gain * part)


def prepare(
    low_ref,
    high_ref,
    wanted_hbm,
    alpha_hbm,
    expo_hbm,
    ks_hbm,
    tables_ref,
    index_ref,
    h,
    alpha_f,
    less_f,
    m_f,
    root_f,
    gain_f,
    r_f,
    cap_f,
    wanted_ref,
    alpha_ref,
    expo_ref,
    ks_ref,
    sems,
):
    fetch([(wanted_hbm, wanted_ref), (alpha_hbm, alpha_ref), (expo_hbm, expo_ref), (ks_hbm, ks_ref)], sems)
    zones, width = alpha_ref.shape[0], tables_ref.shape[1]
    for z in range(zones):
        expo = jnp.full((1, width), expo_ref[z], jnp.float32)
        expo = jnp.where(expo > 0, expo, 2.0)
        tables_ref[z : z + 1, :] = jnp.full((1, width), alpha_ref[z], jnp.float32)
        tables_ref[zones + z : zones + z + 1, :] = expo - 1.0
        tables_ref[2 * zones + z : 2 * zones + z + 1, :] = -0.25 * (1.0 - 1.0 / expo)
        tables_ref[3 * zones + z : 3 * zones + z + 1, :] = jnp.sqrt(jnp.full((1, width), ks_ref[z], jnp.float32))
    wanted = wanted_ref[...]
    index_ref[...] = jnp.concatenate([wanted, pltpu.roll(wanted, wanted.shape[1] // 2, 1)], axis=0).T
    planes, groups = h.shape[0], h.shape[1] // 8 - 1
    out = (h, alpha_f, less_f, m_f, root_f, gain_f)
    for x in range(planes):
        source, plane, tail = (low_ref, x, x) if x < 2 else (high_ref, x - planes + WIDE, x - 2)
        zone_at = WIDE * groups + 2
        for group in range(groups):
            at = plane * groups + group
            fields(tables_ref, out, x, 8 * group, source[at], source[zone_at + at])
        at = WIDE * groups + tail
        fields(tables_ref, out, x, 8 * groups, source[at], source[zone_at + at])
        r_f[x], cap_f[x] = retention(*(ref[x] for ref in out))


def seepage(
    crests,
    place_ref,
    tables_ref,
    index,
    own_h,
    own_alpha,
    own_less,
    own_m,
    own_root,
    own_gain,
    own_r,
    own_cap,
    before_ref,
    after_ref,
    head_ref,
    out_ref,
    order_ref,
    h,
    alpha_f,
    less_f,
    m_f,
    root_f,
    gain_f,
    r_f,
    cap_f,
    table,
    deep,
):
    planes = head_ref.shape[0]
    rows = head_ref.shape[1]
    total = planes + 2 * WIDE
    height, depth = h.shape[1], h.shape[2]
    groups = rows // 8
    zone_at = WIDE * groups + 2
    lane8 = lax.broadcasted_iota(jnp.int32, (8, 128), 1)
    behind = jnp.where(place_ref[1] > 0, 1.0, 0.0)
    ahead = jnp.where(place_ref[1] < crests - 1, 1.0, 0.0)
    out = (h, alpha_f, less_f, m_f, root_f, gain_f)

    for source, first, tail, inside in ((before_ref, 0, 1, behind), (after_ref, WIDE + planes, 0, ahead)):
        for plane in range(WIDE):
            for group in range(groups):
                at = plane * groups + group
                fields(tables_ref, out, first + plane, 8 * group, source[at], source[zone_at + at] * inside)
        for plane in range(2):
            at = WIDE * groups + plane
            fields(tables_ref, out, first + tail + plane, rows, source[at], source[zone_at + at] * inside)
    for x in (0, total - 1):
        for ref in out:
            ref[x, rows:height, :] = jnp.zeros((height - rows, depth), jnp.float32)
    for x in range(planes):
        h[WIDE + x] = own_h[x]

    own = dict(zip(map(id, (alpha_f, less_f, m_f, root_f, gain_f)), (own_alpha, own_less, own_m, own_root, own_gain)))

    def param(ref, x):
        return own[id(ref)][x - WIDE] if WIDE <= x < WIDE + planes else ref[x]

    inner_z = lax.broadcasted_iota(jnp.int32, (height, depth), 1) < depth - 1

    for sweep in range(SWEEPS):
        held = {}
        for x in range(sweep, total - sweep):
            if sweep == 0 and WIDE <= x < WIDE + planes:
                held[x] = (own_r, own_cap, x - WIDE)
            else:
                values = (param(ref, x) for ref in (alpha_f, less_f, m_f, root_f, gain_f))
                r_f[x], cap_f[x] = retention(h[x], *values)
                held[x] = (r_f, cap_f, x)

        def r_of(x):
            return held[x][0][held[x][2]]

        def face(x):
            return r_of(x) * r_of(x + 1) * (h[x + 1] - h[x])

        came = face(sweep)
        for x in range(sweep + 1, total - sweep - 1):
            here, r = h[x], r_of(x)
            goes = face(x)
            flux_y = r * pltpu.roll(r, height - 1, 0) * (pltpu.roll(here, height - 1, 0) - here)
            flux_z = r * pltpu.roll(r, depth - 1, 1) * (pltpu.roll(here, depth - 1, 1) - here + 1.0)
            flux_z = jnp.where(inner_z, flux_z, 0.0)
            inflow = goes - came + (flux_y - pltpu.roll(flux_y, 1, 0)) + (flux_z - pltpu.roll(flux_z, 1, 1))
            h[x] = here + held[x][1][held[x][2]] * inflow
            came = goes

    for x in range(planes):
        here = h[WIDE + x]
        _, _, log_plus = base(own_alpha[x], own_less[x], here)
        head_ref[x] = here[0:rows]
        table[x * rows : (x + 1) * rows, :] = (jnp.exp(4.0 * own_m[x] * log_plus) * here)[0:rows]
    deep[...] = table[...].T
    order_ref[...] = deep[0:8, :]
    bands = depth // BAND
    half = out_ref.shape[0] // 2

    for b in range(bands):
        upper = deep[b * BAND : b * BAND + 8, :]
        lower = deep[b * BAND + 8 : b * BAND + 16, :]
        for d in range(b, half, bands):
            columns = jnp.broadcast_to(index[d : d + 1, :], (8, 128))
            first, second = take_lanes(upper, columns), pltpu.roll(take_lanes(lower, columns), 64, 1)
            out_ref[d] = jnp.where(lane8 < 64, first, second)
            out_ref[half + d] = jnp.where(lane8 < 64, second, first)


def element_rows(value):
    return jnp.concatenate([value[r : r + 1] for r in range(8)], axis=1)


def selectors(
    partitions,
    place_ref,
    order_ref,
    disp_hbm,
    stress_hbm,
    conn_hbm,
    strain_hbm,
    force_hbm,
    slot_hbm,
    depth_hbm,
    zone_hbm,
    cohesion_hbm,
    friction_hbm,
    disp_ref,
    stress_ref,
    conn_ref,
    strain_ref,
    force_ref,
    strength_ref,
    at_ref,
    slot_ref,
    depth_ref,
    zone_ref,
    cohesion_ref,
    friction_ref,
    sems,
):
    del order_ref
    fetch(
        [
            (conn_hbm, conn_ref),
            (slot_hbm, slot_ref),
            (depth_hbm, depth_ref),
            (zone_hbm, zone_ref),
            (cohesion_hbm, cohesion_ref),
            (friction_hbm, friction_ref),
            (disp_hbm, disp_ref),
            (stress_hbm, stress_ref),
            (strain_hbm, strain_ref),
            (force_hbm, force_ref),
        ],
        sems,
    )
    elems = conn_ref.shape[1]
    slot, depth = slot_ref[...], depth_ref[...]
    swap = jnp.where(place_ref[2] >= partitions // 2, 1, 0)
    at_ref[0:1, :] = element_rows((slot >> 6) * 8 + (depth & 7))
    at_ref[1:2, :] = element_rows(((depth >> 3) ^ swap) * 64 + (slot & 63))
    zone = zone_ref[...]
    tan_red = pick(friction_ref, zone) * (1.0 / REDUCTION)
    cos_red = 1.0 / jnp.sqrt(1.0 + tan_red * tan_red)
    sin_red = tan_red * cos_red
    common = 6.0 / (np.sqrt(3.0).astype(np.float32) * (3.0 - sin_red))
    strength_ref[0:1, :] = element_rows(common * (pick(cohesion_ref, zone) * (1.0 / REDUCTION)) * cos_red)
    strength_ref[1:2, :] = element_rows(common * sin_red)


def trial_state(
    sections, place_ref, matrix_ref, disp_ref, after_ref, tail_ref, conn_ref, stress_ref, trial_ref, nodes, corners
):
    ghost = jnp.where(place_ref[0] < sections - 1, after_ref[24:32, :], tail_ref[tail_ref.shape[0] - 1])
    for comp in range(3):
        for s in range(8):
            nodes[comp * 12 + s : comp * 12 + s + 1, :] = disp_ref[comp : comp + 1, s * 128 : (s + 1) * 128]
        for s in range(4):
            at = 2 * comp + s // 2
            nodes[comp * 12 + 8 + s : comp * 12 + 9 + s, :] = ghost[at : at + 1, (s % 2) * 128 : (s % 2 + 1) * 128]
    elems = conn_ref.shape[1]

    @pl.loop(0, elems, step=128)
    def _(e):
        e = pl.multiple_of(e, 128)
        index = conn_ref[:, pl.ds(e, 128)]
        lanes, segment = index & 127, index >> 7
        found = [jnp.zeros((8, 128), jnp.float32) for _ in range(3)]
        for s in range(12):
            here = segment == s
            for comp in range(3):
                row = nodes[comp * 12 + s : comp * 12 + s + 1, :]
                found[comp] = jnp.where(here, take_lanes(row, lanes), found[comp])
        for comp in range(3):
            corners[comp * 8 : comp * 8 + 8, pl.ds(e, 128)] = found[comp]

    strain = jnp.dot(
        matrix_ref[...], corners[...], precision=lax.Precision.HIGHEST, preferred_element_type=jnp.float32
    )
    lame_first = YOUNG * POISSON / ((1.0 + POISSON) * (1.0 - 2.0 * POISSON))
    modulus = YOUNG / (2.0 * (1.0 + POISSON))
    part = [strain[8 * i : 8 * i + 8] for i in range(6)]
    volume = lame_first * (part[0] + part[1] + part[2])
    normals = [stress_ref[i] + volume + 2.0 * modulus * part[i] for i in range(3)]
    shears = [stress_ref[i] + modulus * part[i] for i in range(3, 6)]
    mean = (normals[0] + normals[1] + normals[2]) * (1.0 / 3.0)
    devs = [value - mean for value in normals]
    trial_ref[6] = mean
    trial_ref[7] = jnp.sqrt(
        0.5 * (devs[0] ** 2 + devs[1] ** 2 + devs[2] ** 2) + shears[0] ** 2 + shears[1] ** 2 + shears[2] ** 2
    )
    for i in range(3):
        trial_ref[i] = devs[i]
        trial_ref[3 + i] = shears[i]


def halves(value):
    high = value.astype(jnp.bfloat16).astype(jnp.float32)
    return high, value - high


def final_state(
    matrix_ref, band_ref, at_ref, strength_ref, trial_ref, conn_ref, stress_ref, release_ref, own_ref, ghost_ref
):
    elems = conn_ref.shape[1]
    high, low = halves(band_ref[...])
    in_row = lax.broadcasted_iota(jnp.int32, (band_ref.shape[0], elems), 0) == at_ref[0:1, :]
    found = lax.dot_general(
        jnp.concatenate([high, low], axis=1).astype(jnp.bfloat16),
        jnp.where(in_row, 1.0, 0.0).astype(jnp.bfloat16),
        (((0,), (0,)), ((), ())),
        preferred_element_type=jnp.float32,
    )
    found = found[0:128] + found[128:256]
    in_lane = lax.broadcasted_iota(jnp.int32, (128, elems), 0)
    pore = jnp.sum(jnp.where(in_lane == at_ref[1:2, :], found, 0.0), axis=0, keepdims=True)
    allow = jnp.maximum(strength_ref[0:1, :] - strength_ref[1:2, :] * (trial_ref[6] + pore), 0.0)
    deviator = trial_ref[7]
    yielded = deviator > allow
    scale = jnp.where(yielded, allow / jnp.where(yielded, deviator, 1.0), 1.0)
    release_ref[...] = (1.0 - scale) * deviator
    mean = trial_ref[6]
    parts = [mean + scale * trial_ref[i] for i in range(3)] + [scale * trial_ref[3 + i] for i in range(3)]
    for i in range(6):
        stress_ref[i] = parts[i]
    force = jnp.dot(
        matrix_ref[...],
        jnp.concatenate(parts, axis=0),
        precision=lax.Precision.HIGHEST,
        preferred_element_type=jnp.float32,
    )
    in_segment = lax.broadcasted_iota(jnp.int32, (16, elems), 0)
    high, low = halves(force)
    total = jnp.zeros((96, 128), jnp.float32)
    for corner in range(8):
        node = conn_ref[corner : corner + 1, :]
        here = jnp.broadcast_to(node >> 7, in_segment.shape) == in_segment
        rows = []
        for source in (high, low):
            for comp in range(3):
                value = source[comp * 8 + corner : comp * 8 + corner + 1, :]
                rows.append(jnp.where(here, jnp.broadcast_to(value, in_segment.shape), 0.0))
        left = jnp.concatenate(rows, axis=0).astype(jnp.bfloat16)
        right = jnp.where(jnp.broadcast_to(node & 127, in_lane.shape) == in_lane, 1.0, 0.0).astype(jnp.bfloat16)
        total += lax.dot_general(left, right, (((1,), (1,)), ((), ())), preferred_element_type=jnp.float32)
    total = total[0:48] + total[48:96]
    for comp in range(3):
        own_ref[comp * 8 : comp * 8 + 8, :] = total[comp * 16 : comp * 16 + 8]
        ghost_ref[comp * 4 : comp * 4 + 4, :] = total[comp * 16 + 8 : comp * 16 + 12]


def add_returned(own_ref, ghost_ref, shared_ref, out_ref):
    shared = shared_ref[...]
    in_lane = lax.broadcasted_iota(jnp.int32, (128, 128), 0)
    in_segment = lax.broadcasted_iota(jnp.int32, (8, 128), 0)
    lefts, rights = [], []
    for s in range(4):
        node = shared[s : s + 1]
        rights.append(jnp.where(jnp.broadcast_to(node & 127, in_lane.shape) == in_lane, 1.0, 0.0))
        here = jnp.broadcast_to(node >> 7, in_segment.shape) == in_segment
        rows = []
        for comp in range(3):
            value = ghost_ref[comp * 4 + s : comp * 4 + s + 1, :]
            high, low = halves(value)
            for piece in (high, low):
                rows.append(jnp.where(here, jnp.broadcast_to(piece, in_segment.shape), 0.0))
        lefts.append(jnp.concatenate(rows, axis=0))
    left = jnp.concatenate(lefts, axis=1).astype(jnp.bfloat16)
    right = jnp.concatenate(rights, axis=1).astype(jnp.bfloat16)
    added = lax.dot_general(left, right, (((1,), (1,)), ((), ())), preferred_element_type=jnp.float32)
    for comp in range(3):
        total = own_ref[comp * 8 : comp * 8 + 8, :] + added[comp * 16 : comp * 16 + 8] + added[comp * 16 + 8 : comp * 16 + 16]
        for s in range(8):
            out_ref[comp : comp + 1, s * 128 : (s + 1) * 128] = total[s : s + 1]


VM = pl.BlockSpec(memory_space=pltpu.VMEM)
SM = pl.BlockSpec(memory_space=pltpu.SMEM)


HBM = pl.BlockSpec(memory_space=pltpu.HBM)


def call(body, specs, outs, scratch, name, types=None):
    types = types or [jnp.float32] * len(outs)
    return pl.pallas_call(
        body,
        in_specs=specs,
        out_specs=tuple(VM for _ in outs),
        out_shape=tuple(jax.ShapeDtypeStruct(shape, kind) for shape, kind in zip(outs, types)),
        scratch_shapes=scratch,
        compiler_params=pltpu.CompilerParams(vmem_limit_bytes=VMEM_LIMIT),
        name=name,
    )


def in_hbm(value):
    return pltpu.with_memory_space_constraint(value, pltpu.HBM)


def steps(count, by):
    return [(i, (i + by) % count) for i in range(count)]


def per_device(
    pressure_head,
    zone_ids,
    retention_alpha,
    retention_exponent,
    conductivity,
    sent_columns,
    displacement,
    stress_old,
    connectivity,
    shared_nodes,
    element_zone,
    element_slot,
    element_depth,
    cohesion,
    friction,
):
    crest, section = (lax.axis_size(axis) for axis in AXES)
    devices = crest * section
    planes, rows, depth = pressure_head.shape
    height = rows + 8
    elems = connectivity.shape[1]
    nodes = displacement.shape[1]
    shared = shared_nodes.reshape(4, 128)
    zones = retention_alpha.shape[0]
    place = jnp.stack([lax.axis_index("section"), lax.axis_index("crest"), lax.axis_index(AXES)])
    i32, f32 = jnp.int32, jnp.float32

    forward, backward, head, zone = call(
        pack_section,
        [HBM] * 4,
        [(2 * WIDE * planes, depth), (32, depth), pressure_head.shape, zone_ids.shape],
        [pltpu.VMEM(displacement.shape, f32), pltpu.VMEM(shared.shape, i32), pltpu.SemaphoreType.DMA((4,))],
        "pack_section",
        [f32, f32, f32, i32],
    )(*(in_hbm(x) for x in (pressure_head, zone_ids, displacement, shared)))
    before = lax.ppermute(forward, "section", steps(section, 1))
    after = lax.ppermute(backward, "section", steps(section, -1))

    groups = rows // 8
    edge = (2 * (WIDE * groups + 2), 8, depth)
    low, high = call(
        functools.partial(pack_crest, section),
        [SM] + [VM] * 4,
        [(edge[0] + 1, 8, depth), edge],
        [],
        "pack_crest",
    )(place, head, zone, before, after)
    west = lax.ppermute(high, "crest", steps(crest, 1))
    east = lax.ppermute(low, "crest", steps(crest, -1))

    tables, index, *own = call(
        prepare,
        [VM] * 2 + [HBM] * 4,
        [(4 * zones, depth), (devices, 128)] + [(planes, height, depth)] * 8,
        [pltpu.VMEM((64, devices), i32)] + [pltpu.SMEM((zones,), f32)] * 3 + [pltpu.SemaphoreType.DMA((4,))],
        "prepare",
        [f32, i32] + [f32] * 8,
    )(low, high, *(in_hbm(x) for x in (sent_columns[0].T, retention_alpha, retention_exponent, conductivity)))

    field = pltpu.VMEM((planes + 2 * WIDE, height, depth), f32)
    head_out, outgoing, order = call(
        functools.partial(seepage, crest),
        [SM] + [VM] * 12,
        [pressure_head.shape, (devices, 8, 128), (8, 128)],
        [field] * 8 + [pltpu.VMEM((planes * rows, depth), f32), pltpu.VMEM((depth, planes * rows), f32)],
        "seepage",
    )(place, tables, index, *own, west, east)

    matrix = component_major()
    disp, stress, conn, strain_rows, force_rows, strength, places = call(
        functools.partial(selectors, devices),
        [SM, VM] + [HBM] * 10,
        [
            displacement.shape,
            (6, 8, elems),
            connectivity.shape,
            (48, 24),
            (24, 48),
            (2, elems),
            (2, elems),
        ],
        [pltpu.VMEM((8, 128), i32)] * 3 + [pltpu.SMEM((zones,), f32)] * 2 + [pltpu.SemaphoreType.DMA((10,))],
        "selectors",
        [f32, f32, i32, f32, f32, f32, i32],
    )(
        place,
        order,
        *(
            in_hbm(x)
            for x in (
                displacement,
                stress_old.transpose(1, 0, 2),
                connectivity,
                jnp.asarray(matrix, f32),
                jnp.asarray(matrix.T * 0.125, f32),
                element_slot.reshape(8, 128),
                element_depth.reshape(8, 128),
                element_zone.reshape(8, 128),
                cohesion,
                friction,
            )
        ),
    )
    (trial,) = call(
        functools.partial(trial_state, section),
        [SM] + [VM] * 6,
        [(8, 8, elems)],
        [pltpu.VMEM((40, 128), f32), pltpu.VMEM((24, elems), f32)],
        "trial_state",
    )(place, strain_rows, disp, after, east, conn, stress)
    incoming = lax.all_to_all(outgoing, AXES, split_axis=0, concat_axis=0, tiled=True)

    stress_new, release, own, ghost = call(
        final_state,
        [VM] * 6,
        [(6, 8, elems), (8, elems), (24, 128), (12, 128)],
        [],
        "final_state",
    )(force_rows, incoming.reshape(devices * 8, 128), places, strength, trial, conn)
    returned = lax.ppermute(ghost, AXES, steps(devices, 1))
    (node_forces,) = call(add_returned, [VM] * 3, [(3, nodes)], [], "add_returned")(own, returned, shared)
    return (head_out, stress_new.transpose(1, 0, 2), release, node_forces)


def solution(mesh):
    return jax.shard_map(
        per_device,
        mesh=mesh,
        in_specs=(
            P("crest", "section", None),
            P("crest", "section", None),
            P(),
            P(),
            P(),
            P(("crest", "section"), None, None),
            P(None, ("crest", "section")),
            P(None, None, ("crest", "section")),
            P(None, ("crest", "section")),
            P(("crest", "section")),
            P(("crest", "section")),
            P(("crest", "section")),
            P(("crest", "section")),
            P(),
            P(),
        ),
        out_specs=(
            P("crest", "section", None),
            P(None, None, ("crest", "section")),
            P(None, ("crest", "section")),
            P(None, ("crest", "section")),
        ),
        check_vma=False,
    )
```

```python
import functools

import jax
import jax.numpy as jnp
import numpy as np
from jax import lax
from jax.experimental import pallas as pl
from jax.experimental.pallas import tpu as pltpu
from jax.sharding import PartitionSpec as P

BAND = 16
SWEEPS = 3
WIDE = 3

STORAGE = 0.5
THETA_GAP = 0.35
TIME_STEP = 0.05
REDUCTION = 1.4
YOUNG = 200.0
POISSON = 0.3

AXES = ("crest", "section")
VMEM_LIMIT = 32 * 1024 * 1024


def corner_signs(index):
    return (2 * (index & 1) - 1, 2 * (index >> 1 & 1) - 1, 2 * (index >> 2 & 1) - 1)


def strain_matrix():
    matrix = np.zeros((48, 24))
    inv_root = 1.0 / np.sqrt(3.0)
    for gauss_point in range(8):
        gauss = [value * inv_root for value in corner_signs(gauss_point)]
        row_start = 6 * gauss_point
        for node_corner in range(8):
            sign_x, sign_y, sign_z = corner_signs(node_corner)
            grad_x = 0.25 * sign_x * (1 + gauss[1] * sign_y) * (1 + gauss[2] * sign_z)
            grad_y = 0.25 * sign_y * (1 + gauss[0] * sign_x) * (1 + gauss[2] * sign_z)
            grad_z = 0.25 * sign_z * (1 + gauss[0] * sign_x) * (1 + gauss[1] * sign_y)
            matrix[row_start + 0, node_corner] = grad_x
            matrix[row_start + 1, 8 + node_corner] = grad_y
            matrix[row_start + 2, 16 + node_corner] = grad_z
            matrix[row_start + 3, node_corner] = grad_y
            matrix[row_start + 3, 8 + node_corner] = grad_x
            matrix[row_start + 4, 8 + node_corner] = grad_z
            matrix[row_start + 4, 16 + node_corner] = grad_y
            matrix[row_start + 5, 16 + node_corner] = grad_x
            matrix[row_start + 5, node_corner] = grad_z
    return matrix


def component_major():
    order = [6 * gauss_point + comp for comp in range(6) for gauss_point in range(8)]
    return strain_matrix()[order]


def take_lanes(row, lanes):
    return jnp.take_along_axis(jnp.broadcast_to(row, lanes.shape), lanes, axis=1, mode="promise_in_bounds")


def pick(values_ref, index, first=0):
    lane = lax.broadcasted_iota(jnp.int32, (8, 128), 1)
    table = jnp.zeros((8, 128), jnp.float32)
    for zone in range(values_ref.shape[0]):
        table = jnp.where(lane == first + zone, values_ref[zone], table)
    return table if index is None else take_lanes(table, index)


def fetch(pairs, sems):
    copies = [pltpu.make_async_copy(source, target, sems.at[i]) for i, (source, target) in enumerate(pairs)]
    for copy in copies:
        copy.start()
    for copy in copies:
        copy.wait()


def pack_section(
    head_hbm, zone_hbm, disp_hbm, shared_hbm, forward_ref, backward_ref, head_ref, zone_ref, disp_ref, shared_ref, sems
):
    fetch([(head_hbm, head_ref), (zone_hbm, zone_ref), (disp_hbm, disp_ref), (shared_hbm, shared_ref)], sems)
    planes, rows = head_ref.shape[0], head_ref.shape[1]
    for x in range(planes):
        for field in range(2):
            first, last = slice(0, WIDE), slice(rows - WIDE, rows)
            at = field * WIDE * planes + WIDE * x
            if field == 0:
                forward_ref[at : at + WIDE, :] = head_ref[x, last, :]
                backward_ref[at : at + WIDE, :] = head_ref[x, first, :]
            else:
                forward_ref[at : at + WIDE, :] = zone_ref[x, last, :].astype(jnp.float32) + 1.0
                backward_ref[at : at + WIDE, :] = zone_ref[x, first, :].astype(jnp.float32) + 1.0
    index = shared_ref[...]
    index = jnp.concatenate([index, index], axis=0)
    lanes, segment = index & 127, index >> 7
    for comp in range(3):
        found = jnp.zeros((8, 128), jnp.float32)
        for s in range(disp_ref.shape[1] // 128):
            row = disp_ref[comp : comp + 1, s * 128 : (s + 1) * 128]
            found = jnp.where(segment == s, take_lanes(row, lanes), found)
        for s in range(4):
            at = 2 * WIDE * planes + 2 * comp + s // 2
            backward_ref[at : at + 1, (s % 2) * 128 : (s % 2 + 1) * 128] = found[s : s + 1]
    backward_ref[30:32, :] = jnp.zeros((2, 256), jnp.float32)


def pack_crest(sections, place_ref, head_ref, zone_ref, before_ref, after_ref, low_ref, high_ref):
    planes, rows = head_ref.shape[0], head_ref.shape[1]
    groups = rows // 8
    behind = jnp.where(place_ref[0] > 0, 1.0, 0.0)
    ahead = jnp.where(place_ref[0] < sections - 1, 1.0, 0.0)
    for field in range(2):
        first = field * (WIDE * groups + 2)
        for x in range(planes):
            for group in range(groups):
                at = slice(8 * group, 8 * group + 8)
                own = head_ref[x, at, :] if field == 0 else zone_ref[x, at, :].astype(jnp.float32) + 1.0
                if x < WIDE:
                    low_ref[first + x * groups + group] = own
                if x >= planes - WIDE:
                    high_ref[first + (x - planes + WIDE) * groups + group] = own
            at = field * WIDE * planes + WIDE * x
            tail = jnp.concatenate(
                [
                    after_ref[at : at + WIDE, :] * ahead,
                    jnp.zeros((2, after_ref.shape[1]), jnp.float32),
                    before_ref[at : at + WIDE, :] * behind,
                ],
                axis=0,
            )
            if x < 2:
                low_ref[first + WIDE * groups + x] = tail
            else:
                high_ref[first + WIDE * groups + x - 2] = tail
    low_ref[2 * (WIDE * groups + 2)] = after_ref[24:32, :]


def choose(values, bits):
    for bit in bits:
        values = [jnp.where(bit, values[i + 1], values[i]) for i in range(0, len(values), 2)]
    return values[0]


def fields(tables_ref, out, x, row, head, zone):
    zones = tables_ref.shape[0] // 4
    tables = [
        [jnp.broadcast_to(tables_ref[f * zones + z : f * zones + z + 1, :], head.shape) for z in range(zones)]
        for f in range(4)
    ]
    zone = zone.astype(jnp.int32) - 1
    bits = [(zone & (1 << bit)) != 0 for bit in range(3)]
    alpha, less, m, root = (choose(table, bits) for table in tables)
    values = (head, alpha, less, m, jnp.where(zone >= 0, root, 0.0), THETA_GAP * alpha * less)
    for ref, value in zip(out, values):
        ref[x, row : row + 8, :] = value


def base(alpha, less, h):
    scaled = alpha * jnp.maximum(-h, 0.0)
    power = jnp.exp(less * jnp.log(jnp.maximum(scaled, 1e-30)))
    plus = 1.0 + power * scaled
    return power, plus, jnp.log(plus)


def retention(h, alpha, less, m, root, gain):
    power, plus, log_plus = base(alpha, less, h)
    fourth = jnp.exp(m * log_plus)
    square = fourth * fourth
    part = power * (square * square)
    return root * fourth * (1.0 - part), TIME_STEP * plus / (STORAGE * plus + gain * part)


def prepare(
    low_ref,
    high_ref,
    wanted_hbm,
    alpha_hbm,
    expo_hbm,
    ks_hbm,
    tables_ref,
    index_ref,
    h,
    alpha_f,
    less_f,
    m_f,
    root_f,
    gain_f,
    r_f,
    cap_f,
    wanted_ref,
    alpha_ref,
    expo_ref,
    ks_ref,
    sems,
):
    fetch([(wanted_hbm, wanted_ref), (alpha_hbm, alpha_ref), (expo_hbm, expo_ref), (ks_hbm, ks_ref)], sems)
    zones, width = alpha_ref.shape[0], tables_ref.shape[1]
    for z in range(zones):
        expo = jnp.full((1, width), expo_ref[z], jnp.float32)
        expo = jnp.where(expo > 0, expo, 2.0)
        tables_ref[z : z + 1, :] = jnp.full((1, width), alpha_ref[z], jnp.float32)
        tables_ref[zones + z : zones + z + 1, :] = expo - 1.0
        tables_ref[2 * zones + z : 2 * zones + z + 1, :] = -0.25 * (1.0 - 1.0 / expo)
        tables_ref[3 * zones + z : 3 * zones + z + 1, :] = jnp.sqrt(jnp.full((1, width), ks_ref[z], jnp.float32))
    wanted = wanted_ref[...]
    index_ref[...] = jnp.concatenate([wanted, pltpu.roll(wanted, wanted.shape[1] // 2, 1)], axis=0).T
    planes, groups = h.shape[0], h.shape[1] // 8 - 1
    out = (h, alpha_f, less_f, m_f, root_f, gain_f)
    for x in range(planes):
        source, plane, tail = (low_ref, x, x) if x < 2 else (high_ref, x - planes + WIDE, x - 2)
        zone_at = WIDE * groups + 2
        for group in range(groups):
            at = plane * groups + group
            fields(tables_ref, out, x, 8 * group, source[at], source[zone_at + at])
        at = WIDE * groups + tail
        fields(tables_ref, out, x, 8 * groups, source[at], source[zone_at + at])
        r_f[x], cap_f[x] = retention(*(ref[x] for ref in out))


def seepage(
    crests,
    place_ref,
    tables_ref,
    index,
    own_h,
    own_alpha,
    own_less,
    own_m,
    own_root,
    own_gain,
    own_r,
    own_cap,
    before_ref,
    after_ref,
    head_ref,
    out_ref,
    order_ref,
    h,
    alpha_f,
    less_f,
    m_f,
    root_f,
    gain_f,
    r_f,
    cap_f,
    table,
    deep,
):
    planes = head_ref.shape[0]
    rows = head_ref.shape[1]
    total = planes + 2 * WIDE
    height, depth = h.shape[1], h.shape[2]
    groups = rows // 8
    zone_at = WIDE * groups + 2
    lane8 = lax.broadcasted_iota(jnp.int32, (8, 128), 1)
    behind = jnp.where(place_ref[1] > 0, 1.0, 0.0)
    ahead = jnp.where(place_ref[1] < crests - 1, 1.0, 0.0)
    out = (h, alpha_f, less_f, m_f, root_f, gain_f)

    for source, first, tail, inside in ((before_ref, 0, 1, behind), (after_ref, WIDE + planes, 0, ahead)):
        for plane in range(WIDE):
            for group in range(groups):
                at = plane * groups + group
                fields(tables_ref, out, first + plane, 8 * group, source[at], source[zone_at + at] * inside)
        for plane in range(2):
            at = WIDE * groups + plane
            fields(tables_ref, out, first + tail + plane, rows, source[at], source[zone_at + at] * inside)
    for x in (0, total - 1):
        for ref in out:
            ref[x, rows:height, :] = jnp.zeros((height - rows, depth), jnp.float32)
    for x in range(planes):
        h[WIDE + x] = own_h[x]

    own = dict(zip(map(id, (alpha_f, less_f, m_f, root_f, gain_f)), (own_alpha, own_less, own_m, own_root, own_gain)))

    def param(ref, x):
        return own[id(ref)][x - WIDE] if WIDE <= x < WIDE + planes else ref[x]

    inner_z = lax.broadcasted_iota(jnp.int32, (height, depth), 1) < depth - 1

    for sweep in range(SWEEPS):
        held = {}
        for x in range(sweep, total - sweep):
            if sweep == 0 and WIDE <= x < WIDE + planes:
                held[x] = (own_r, own_cap, x - WIDE)
            else:
                values = (param(ref, x) for ref in (alpha_f, less_f, m_f, root_f, gain_f))
                r_f[x], cap_f[x] = retention(h[x], *values)
                held[x] = (r_f, cap_f, x)

        def r_of(x):
            return held[x][0][held[x][2]]

        def face(x):
            return r_of(x) * r_of(x + 1) * (h[x + 1] - h[x])

        came = face(sweep)
        for x in range(sweep + 1, total - sweep - 1):
            here, r = h[x], r_of(x)
            goes = face(x)
            flux_y = r * pltpu.roll(r, height - 1, 0) * (pltpu.roll(here, height - 1, 0) - here)
            flux_z = r * pltpu.roll(r, depth - 1, 1) * (pltpu.roll(here, depth - 1, 1) - here + 1.0)
            flux_z = jnp.where(inner_z, flux_z, 0.0)
            inflow = goes - came + (flux_y - pltpu.roll(flux_y, 1, 0)) + (flux_z - pltpu.roll(flux_z, 1, 1))
            h[x] = here + held[x][1][held[x][2]] * inflow
            came = goes

    for x in range(planes):
        here = h[WIDE + x]
        _, _, log_plus = base(own_alpha[x], own_less[x], here)
        head_ref[x] = here[0:rows]
        table[x * rows : (x + 1) * rows, :] = (jnp.exp(4.0 * own_m[x] * log_plus) * here)[0:rows]
    deep[...] = table[...].T
    order_ref[...] = deep[0:8, :]
    bands = depth // BAND
    half = out_ref.shape[0] // 2

    for b in range(bands):
        upper = deep[b * BAND : b * BAND + 8, :]
        lower = deep[b * BAND + 8 : b * BAND + 16, :]
        for d in range(b, half, bands):
            columns = jnp.broadcast_to(index[d : d + 1, :], (8, 128))
            first, second = take_lanes(upper, columns), pltpu.roll(take_lanes(lower, columns), 64, 1)
            out_ref[d] = jnp.where(lane8 < 64, first, second)
            out_ref[half + d] = jnp.where(lane8 < 64, second, first)


def element_rows(value):
    return jnp.concatenate([value[r : r + 1] for r in range(8)], axis=1)


def selectors(
    partitions,
    place_ref,
    order_ref,
    disp_hbm,
    stress_hbm,
    conn_hbm,
    strain_hbm,
    force_hbm,
    slot_hbm,
    depth_hbm,
    zone_hbm,
    cohesion_hbm,
    friction_hbm,
    disp_ref,
    stress_ref,
    conn_ref,
    strain_ref,
    force_ref,
    strength_ref,
    at_ref,
    slot_ref,
    depth_ref,
    zone_ref,
    cohesion_ref,
    friction_ref,
    sems,
):
    del order_ref
    fetch(
        [
            (conn_hbm, conn_ref),
            (slot_hbm, slot_ref),
            (depth_hbm, depth_ref),
            (zone_hbm, zone_ref),
            (cohesion_hbm, cohesion_ref),
            (friction_hbm, friction_ref),
            (disp_hbm, disp_ref),
            (stress_hbm, stress_ref),
            (strain_hbm, strain_ref),
            (force_hbm, force_ref),
        ],
        sems,
    )
    elems = conn_ref.shape[1]
    slot, depth = slot_ref[...], depth_ref[...]
    swap = jnp.where(place_ref[2] >= partitions // 2, 1, 0)
    at_ref[0:1, :] = element_rows((slot >> 6) * 8 + (depth & 7))
    at_ref[1:2, :] = element_rows(((depth >> 3) ^ swap) * 64 + (slot & 63))
    zone = zone_ref[...]
    tan_red = pick(friction_ref, zone) * (1.0 / REDUCTION)
    cos_red = 1.0 / jnp.sqrt(1.0 + tan_red * tan_red)
    sin_red = tan_red * cos_red
    common = 6.0 / (np.sqrt(3.0).astype(np.float32) * (3.0 - sin_red))
    strength_ref[0:1, :] = element_rows(common * (pick(cohesion_ref, zone) * (1.0 / REDUCTION)) * cos_red)
    strength_ref[1:2, :] = element_rows(common * sin_red)


def trial_state(
    sections, place_ref, matrix_ref, disp_ref, after_ref, tail_ref, conn_ref, stress_ref, trial_ref, nodes, corners
):
    ghost = jnp.where(place_ref[0] < sections - 1, after_ref[24:32, :], tail_ref[tail_ref.shape[0] - 1])
    for comp in range(3):
        for s in range(8):
            nodes[comp * 12 + s : comp * 12 + s + 1, :] = disp_ref[comp : comp + 1, s * 128 : (s + 1) * 128]
        for s in range(4):
            at = 2 * comp + s // 2
            nodes[comp * 12 + 8 + s : comp * 12 + 9 + s, :] = ghost[at : at + 1, (s % 2) * 128 : (s % 2 + 1) * 128]
    elems = conn_ref.shape[1]

    @pl.loop(0, elems, step=128)
    def _(e):
        e = pl.multiple_of(e, 128)
        index = conn_ref[:, pl.ds(e, 128)]
        lanes, segment = index & 127, index >> 7
        found = [jnp.zeros((8, 128), jnp.float32) for _ in range(3)]
        for s in range(12):
            here = segment == s
            for comp in range(3):
                row = nodes[comp * 12 + s : comp * 12 + s + 1, :]
                found[comp] = jnp.where(here, take_lanes(row, lanes), found[comp])
        for comp in range(3):
            corners[comp * 8 : comp * 8 + 8, pl.ds(e, 128)] = found[comp]

    strain = jnp.dot(
        matrix_ref[...], corners[...], precision=lax.Precision.HIGHEST, preferred_element_type=jnp.float32
    )
    lame_first = YOUNG * POISSON / ((1.0 + POISSON) * (1.0 - 2.0 * POISSON))
    modulus = YOUNG / (2.0 * (1.0 + POISSON))
    part = [strain[8 * i : 8 * i + 8] for i in range(6)]
    volume = lame_first * (part[0] + part[1] + part[2])
    normals = [stress_ref[i] + volume + 2.0 * modulus * part[i] for i in range(3)]
    shears = [stress_ref[i] + modulus * part[i] for i in range(3, 6)]
    mean = (normals[0] + normals[1] + normals[2]) * (1.0 / 3.0)
    devs = [value - mean for value in normals]
    trial_ref[6] = mean
    trial_ref[7] = jnp.sqrt(
        0.5 * (devs[0] ** 2 + devs[1] ** 2 + devs[2] ** 2) + shears[0] ** 2 + shears[1] ** 2 + shears[2] ** 2
    )
    for i in range(3):
        trial_ref[i] = devs[i]
        trial_ref[3 + i] = shears[i]


def halves(value):
    high = value.astype(jnp.bfloat16).astype(jnp.float32)
    return high, value - high


def node_lanes(node, elems):
    in_lane = lax.broadcasted_iota(jnp.int32, (128, elems), 0)
    return jnp.where(jnp.broadcast_to(node & 127, in_lane.shape) == in_lane, 1.0, 0.0).astype(jnp.bfloat16)


def final_state(
    matrix_ref, band_ref, at_ref, strength_ref, trial_ref, conn_ref, stress_ref, release_ref, force_ref, ghost_ref
):
    elems = conn_ref.shape[1]
    count = band_ref.shape[0]
    split = count // 2
    high, low = halves(band_ref[0:split, :])
    in_row = lax.broadcasted_iota(jnp.int32, (split, elems), 0) == at_ref[0:1, :]
    found = lax.dot_general(
        jnp.concatenate([high, low], axis=1).astype(jnp.bfloat16),
        jnp.where(in_row, 1.0, 0.0).astype(jnp.bfloat16),
        (((0,), (0,)), ((), ())),
        preferred_element_type=jnp.float32,
    )
    found = found[0:128] + found[128:256]
    in_lane = lax.broadcasted_iota(jnp.int32, (128, elems), 0)
    pore = jnp.sum(jnp.where(in_lane == at_ref[1:2, :], found, 0.0), axis=0, keepdims=True)
    row8, lane8 = (
        jnp.concatenate([at_ref[i : i + 1, r * 128 : (r + 1) * 128] for r in range(8)], axis=0) for i in range(2)
    )
    parts = [jnp.zeros((8, 128), jnp.float32) for _ in range(4)]
    for r in range(split, count):
        parts[r % 4] = jnp.where(row8 == r, take_lanes(band_ref[r : r + 1, :], lane8), parts[r % 4])
    pore = pore + element_rows((parts[0] + parts[1]) + (parts[2] + parts[3]))
    allow = jnp.maximum(strength_ref[0:1, :] - strength_ref[1:2, :] * (trial_ref[6] + pore), 0.0)
    deviator = trial_ref[7]
    yielded = deviator > allow
    scale = jnp.where(yielded, allow / jnp.where(yielded, deviator, 1.0), 1.0)
    release_ref[...] = (1.0 - scale) * deviator
    mean = trial_ref[6]
    parts = [mean + scale * trial_ref[i] for i in range(3)] + [scale * trial_ref[3 + i] for i in range(3)]
    for i in range(6):
        stress_ref[i] = parts[i]
    force = jnp.dot(
        matrix_ref[...],
        jnp.concatenate(parts, axis=0),
        precision=lax.Precision.HIGHEST,
        preferred_element_type=jnp.float32,
    )
    force_ref[...] = force
    high, low = halves(force)
    tile = lax.broadcasted_iota(jnp.int32, (8, elems), 0)
    total = jnp.zeros((32, 128), jnp.float32)
    for corner in range(8):
        node = conn_ref[corner : corner + 1, :]
        here = jnp.broadcast_to(node >> 7, tile.shape) == 8 + (tile & 3)
        rows = []
        for comp in range(3):
            at = slice(comp * 8 + corner, comp * 8 + corner + 1)
            value = jnp.where(tile < 4, jnp.broadcast_to(high[at], tile.shape), jnp.broadcast_to(low[at], tile.shape))
            rows.append(jnp.where(here, value, 0.0))
        rows.append(jnp.zeros(tile.shape, jnp.float32))
        left = jnp.concatenate(rows, axis=0).astype(jnp.bfloat16)
        total += lax.dot_general(
            left, node_lanes(node, elems), (((1,), (1,)), ((), ())), preferred_element_type=jnp.float32
        )
    for comp in range(3):
        ghost_ref[comp * 4 : comp * 4 + 4, :] = total[comp * 8 : comp * 8 + 4] + total[comp * 8 + 4 : comp * 8 + 8]


def own_forces(force_ref, conn_ref, own_ref):
    elems = conn_ref.shape[1]
    high, low = halves(force_ref[...])
    tile = lax.broadcasted_iota(jnp.int32, (8, elems), 0)
    total = jnp.zeros((48, 128), jnp.float32)
    for corner in range(8):
        node = conn_ref[corner : corner + 1, :]
        here = jnp.broadcast_to(node >> 7, tile.shape) == tile
        rows = []
        for comp in range(3):
            for source in (high, low):
                value = source[comp * 8 + corner : comp * 8 + corner + 1]
                rows.append(jnp.where(here, jnp.broadcast_to(value, tile.shape), 0.0))
        left = jnp.concatenate(rows, axis=0).astype(jnp.bfloat16)
        total += lax.dot_general(
            left, node_lanes(node, elems), (((1,), (1,)), ((), ())), preferred_element_type=jnp.float32
        )
    for comp in range(3):
        own_ref[comp * 8 : comp * 8 + 8, :] = total[comp * 16 : comp * 16 + 8] + total[comp * 16 + 8 : comp * 16 + 16]


def add_returned(own_ref, ghost_ref, shared_ref, out_ref):
    shared = shared_ref[...]
    in_lane = lax.broadcasted_iota(jnp.int32, (128, 128), 0)
    in_segment = lax.broadcasted_iota(jnp.int32, (8, 128), 0)
    lefts, rights = [], []
    for s in range(4):
        node = shared[s : s + 1]
        rights.append(jnp.where(jnp.broadcast_to(node & 127, in_lane.shape) == in_lane, 1.0, 0.0))
        here = jnp.broadcast_to(node >> 7, in_segment.shape) == in_segment
        rows = []
        for comp in range(3):
            value = ghost_ref[comp * 4 + s : comp * 4 + s + 1, :]
            high, low = halves(value)
            for piece in (high, low):
                rows.append(jnp.where(here, jnp.broadcast_to(piece, in_segment.shape), 0.0))
        lefts.append(jnp.concatenate(rows, axis=0))
    left = jnp.concatenate(lefts, axis=1).astype(jnp.bfloat16)
    right = jnp.concatenate(rights, axis=1).astype(jnp.bfloat16)
    added = lax.dot_general(left, right, (((1,), (1,)), ((), ())), preferred_element_type=jnp.float32)
    for comp in range(3):
        total = own_ref[comp * 8 : comp * 8 + 8, :] + added[comp * 16 : comp * 16 + 8] + added[comp * 16 + 8 : comp * 16 + 16]
        for s in range(8):
            out_ref[comp : comp + 1, s * 128 : (s + 1) * 128] = total[s : s + 1]


VM = pl.BlockSpec(memory_space=pltpu.VMEM)
SM = pl.BlockSpec(memory_space=pltpu.SMEM)


HBM = pl.BlockSpec(memory_space=pltpu.HBM)


def call(body, specs, outs, scratch, name, types=None):
    types = types or [jnp.float32] * len(outs)
    return pl.pallas_call(
        body,
        in_specs=specs,
        out_specs=tuple(VM for _ in outs),
        out_shape=tuple(jax.ShapeDtypeStruct(shape, kind) for shape, kind in zip(outs, types)),
        scratch_shapes=scratch,
        compiler_params=pltpu.CompilerParams(vmem_limit_bytes=VMEM_LIMIT),
        name=name,
    )


def in_hbm(value):
    return pltpu.with_memory_space_constraint(value, pltpu.HBM)


def steps(count, by):
    return [(i, (i + by) % count) for i in range(count)]


def per_device(
    pressure_head,
    zone_ids,
    retention_alpha,
    retention_exponent,
    conductivity,
    sent_columns,
    displacement,
    stress_old,
    connectivity,
    shared_nodes,
    element_zone,
    element_slot,
    element_depth,
    cohesion,
    friction,
):
    crest, section = (lax.axis_size(axis) for axis in AXES)
    devices = crest * section
    planes, rows, depth = pressure_head.shape
    height = rows + 8
    elems = connectivity.shape[1]
    nodes = displacement.shape[1]
    shared = shared_nodes.reshape(4, 128)
    zones = retention_alpha.shape[0]
    place = jnp.stack([lax.axis_index("section"), lax.axis_index("crest"), lax.axis_index(AXES)])
    i32, f32 = jnp.int32, jnp.float32

    forward, backward, head, zone = call(
        pack_section,
        [HBM] * 4,
        [(2 * WIDE * planes, depth), (32, depth), pressure_head.shape, zone_ids.shape],
        [pltpu.VMEM(displacement.shape, f32), pltpu.VMEM(shared.shape, i32), pltpu.SemaphoreType.DMA((4,))],
        "pack_section",
        [f32, f32, f32, i32],
    )(*(in_hbm(x) for x in (pressure_head, zone_ids, displacement, shared)))
    before = lax.ppermute(forward, "section", steps(section, 1))
    after = lax.ppermute(backward, "section", steps(section, -1))

    groups = rows // 8
    edge = (2 * (WIDE * groups + 2), 8, depth)
    low, high = call(
        functools.partial(pack_crest, section),
        [SM] + [VM] * 4,
        [(edge[0] + 1, 8, depth), edge],
        [],
        "pack_crest",
    )(place, head, zone, before, after)
    west = lax.ppermute(high, "crest", steps(crest, 1))
    east = lax.ppermute(low, "crest", steps(crest, -1))

    tables, index, *own = call(
        prepare,
        [VM] * 2 + [HBM] * 4,
        [(4 * zones, depth), (devices, 128)] + [(planes, height, depth)] * 8,
        [pltpu.VMEM((64, devices), i32)] + [pltpu.SMEM((zones,), f32)] * 3 + [pltpu.SemaphoreType.DMA((4,))],
        "prepare",
        [f32, i32] + [f32] * 8,
    )(low, high, *(in_hbm(x) for x in (sent_columns[0].T, retention_alpha, retention_exponent, conductivity)))

    field = pltpu.VMEM((planes + 2 * WIDE, height, depth), f32)
    head_out, outgoing, order = call(
        functools.partial(seepage, crest),
        [SM] + [VM] * 12,
        [pressure_head.shape, (devices, 8, 128), (8, 128)],
        [field] * 8 + [pltpu.VMEM((planes * rows, depth), f32), pltpu.VMEM((depth, planes * rows), f32)],
        "seepage",
    )(place, tables, index, *own, west, east)

    matrix = component_major()
    disp, stress, conn, strain_rows, force_rows, strength, places = call(
        functools.partial(selectors, devices),
        [SM, VM] + [HBM] * 10,
        [
            displacement.shape,
            (6, 8, elems),
            connectivity.shape,
            (48, 24),
            (24, 48),
            (2, elems),
            (2, elems),
        ],
        [pltpu.VMEM((8, 128), i32)] * 3 + [pltpu.SMEM((zones,), f32)] * 2 + [pltpu.SemaphoreType.DMA((10,))],
        "selectors",
        [f32, f32, i32, f32, f32, f32, i32],
    )(
        place,
        order,
        *(
            in_hbm(x)
            for x in (
                displacement,
                stress_old.transpose(1, 0, 2),
                connectivity,
                jnp.asarray(matrix, f32),
                jnp.asarray(matrix.T * 0.125, f32),
                element_slot.reshape(8, 128),
                element_depth.reshape(8, 128),
                element_zone.reshape(8, 128),
                cohesion,
                friction,
            )
        ),
    )
    (trial,) = call(
        functools.partial(trial_state, section),
        [SM] + [VM] * 6,
        [(8, 8, elems)],
        [pltpu.VMEM((40, 128), f32), pltpu.VMEM((24, elems), f32)],
        "trial_state",
    )(place, strain_rows, disp, after, east, conn, stress)
    incoming = lax.all_to_all(outgoing, AXES, split_axis=0, concat_axis=0, tiled=True)

    stress_new, release, force, ghost = call(
        final_state,
        [VM] * 6,
        [(6, 8, elems), (8, elems), (24, elems), (12, 128)],
        [],
        "final_state",
    )(force_rows, incoming.reshape(devices * 8, 128), places, strength, trial, conn)
    returned = lax.ppermute(ghost, AXES, steps(devices, 1))
    (own,) = call(own_forces, [VM] * 2, [(24, 128)], [], "own_forces")(force, conn)
    (node_forces,) = call(add_returned, [VM] * 3, [(3, nodes)], [], "add_returned")(own, returned, shared)
    return (head_out, stress_new.transpose(1, 0, 2), release, node_forces)


def solution(mesh):
    return jax.shard_map(
        per_device,
        mesh=mesh,
        in_specs=(
            P("crest", "section", None),
            P("crest", "section", None),
            P(),
            P(),
            P(),
            P(("crest", "section"), None, None),
            P(None, ("crest", "section")),
            P(None, None, ("crest", "section")),
            P(None, ("crest", "section")),
            P(("crest", "section")),
            P(("crest", "section")),
            P(("crest", "section")),
            P(("crest", "section")),
            P(),
            P(),
        ),
        out_specs=(
            P("crest", "section", None),
            P(None, None, ("crest", "section")),
            P(None, ("crest", "section")),
            P(None, ("crest", "section")),
        ),
        check_vma=False,
    )
```

```python
import functools

import jax
import jax.numpy as jnp
import numpy as np
from jax import lax
from jax.experimental import pallas as pl
from jax.experimental.pallas import tpu as pltpu
from jax.sharding import PartitionSpec as P

BAND = 16
SWEEPS = 3
WIDE = 3

STORAGE = 0.5
THETA_GAP = 0.35
TIME_STEP = 0.05
REDUCTION = 1.4
YOUNG = 200.0
POISSON = 0.3

AXES = ("crest", "section")
VMEM_LIMIT = 32 * 1024 * 1024


def corner_signs(index):
    return (2 * (index & 1) - 1, 2 * (index >> 1 & 1) - 1, 2 * (index >> 2 & 1) - 1)


def strain_matrix():
    matrix = np.zeros((48, 24))
    inv_root = 1.0 / np.sqrt(3.0)
    for gauss_point in range(8):
        gauss = [value * inv_root for value in corner_signs(gauss_point)]
        row_start = 6 * gauss_point
        for node_corner in range(8):
            sign_x, sign_y, sign_z = corner_signs(node_corner)
            grad_x = 0.25 * sign_x * (1 + gauss[1] * sign_y) * (1 + gauss[2] * sign_z)
            grad_y = 0.25 * sign_y * (1 + gauss[0] * sign_x) * (1 + gauss[2] * sign_z)
            grad_z = 0.25 * sign_z * (1 + gauss[0] * sign_x) * (1 + gauss[1] * sign_y)
            matrix[row_start + 0, node_corner] = grad_x
            matrix[row_start + 1, 8 + node_corner] = grad_y
            matrix[row_start + 2, 16 + node_corner] = grad_z
            matrix[row_start + 3, node_corner] = grad_y
            matrix[row_start + 3, 8 + node_corner] = grad_x
            matrix[row_start + 4, 8 + node_corner] = grad_z
            matrix[row_start + 4, 16 + node_corner] = grad_y
            matrix[row_start + 5, 16 + node_corner] = grad_x
            matrix[row_start + 5, node_corner] = grad_z
    return matrix


def component_major():
    order = [6 * gauss_point + comp for comp in range(6) for gauss_point in range(8)]
    return strain_matrix()[order]


def take_lanes(row, lanes):
    return jnp.take_along_axis(jnp.broadcast_to(row, lanes.shape), lanes, axis=1, mode="promise_in_bounds")


def pick(values_ref, index, first=0):
    lane = lax.broadcasted_iota(jnp.int32, (8, 128), 1)
    table = jnp.zeros((8, 128), jnp.float32)
    for zone in range(values_ref.shape[0]):
        table = jnp.where(lane == first + zone, values_ref[zone], table)
    return table if index is None else take_lanes(table, index)


def fetch(pairs, sems):
    copies = [pltpu.make_async_copy(source, target, sems.at[i]) for i, (source, target) in enumerate(pairs)]
    for copy in copies:
        copy.start()
    for copy in copies:
        copy.wait()


def pack_section(
    head_hbm, zone_hbm, disp_hbm, shared_hbm, forward_ref, backward_ref, head_ref, zone_ref, disp_ref, shared_ref, sems
):
    fetch([(head_hbm, head_ref), (zone_hbm, zone_ref), (disp_hbm, disp_ref), (shared_hbm, shared_ref)], sems)
    planes, rows = head_ref.shape[0], head_ref.shape[1]
    for x in range(planes):
        for field in range(2):
            first, last = slice(0, WIDE), slice(rows - WIDE, rows)
            at = field * WIDE * planes + WIDE * x
            if field == 0:
                forward_ref[at : at + WIDE, :] = head_ref[x, last, :]
                backward_ref[at : at + WIDE, :] = head_ref[x, first, :]
            else:
                forward_ref[at : at + WIDE, :] = zone_ref[x, last, :].astype(jnp.float32) + 1.0
                backward_ref[at : at + WIDE, :] = zone_ref[x, first, :].astype(jnp.float32) + 1.0
    index = shared_ref[...]
    index = jnp.concatenate([index, index], axis=0)
    lanes, segment = index & 127, index >> 7
    for comp in range(3):
        found = jnp.zeros((8, 128), jnp.float32)
        for s in range(disp_ref.shape[1] // 128):
            row = disp_ref[comp : comp + 1, s * 128 : (s + 1) * 128]
            found = jnp.where(segment == s, take_lanes(row, lanes), found)
        for s in range(4):
            at = 2 * WIDE * planes + 2 * comp + s // 2
            backward_ref[at : at + 1, (s % 2) * 128 : (s % 2 + 1) * 128] = found[s : s + 1]
    backward_ref[30:32, :] = jnp.zeros((2, 256), jnp.float32)


def pack_crest(sections, place_ref, head_ref, zone_ref, flux_ref, before_ref, after_ref, low_ref, high_ref):
    planes, rows = head_ref.shape[0], head_ref.shape[1]
    groups = rows // 8
    behind = jnp.where(place_ref[0] > 0, 1.0, 0.0)
    ahead = jnp.where(place_ref[0] < sections - 1, 1.0, 0.0)
    zone_at = 2 * groups + 2
    for x in range(planes):
        target, plane = (low_ref, x) if x < 2 else (high_ref, x - 2)
        for field in range(2):
            first = field * zone_at
            for group in range(groups):
                at = slice(8 * group, 8 * group + 8)
                own = head_ref[x, at, :] if field == 0 else zone_ref[x, at, :].astype(jnp.float32) + 1.0
                target[first + plane * groups + group] = own
            at = field * WIDE * planes + WIDE * x
            target[first + 2 * groups + plane] = jnp.concatenate(
                [
                    after_ref[at : at + WIDE, :] * ahead,
                    jnp.zeros((2, after_ref.shape[1]), jnp.float32),
                    before_ref[at : at + WIDE, :] * behind,
                ],
                axis=0,
            )
    for group in range(groups):
        low_ref[2 * zone_at + group] = flux_ref[group]
        high_ref[2 * zone_at + group] = flux_ref[group]
    low_ref[2 * zone_at + groups] = after_ref[24:32, :]


def choose(values, bits):
    for bit in bits:
        values = [jnp.where(bit, values[i + 1], values[i]) for i in range(0, len(values), 2)]
    return values[0]


def params(tables_ref, zone):
    zones = tables_ref.shape[0] // 4
    tables = [
        [jnp.broadcast_to(tables_ref[f * zones + z : f * zones + z + 1, :], zone.shape) for z in range(zones)]
        for f in range(4)
    ]
    zone = zone.astype(jnp.int32) - 1
    bits = [(zone & (1 << bit)) != 0 for bit in range(3)]
    alpha, less, m, root = (choose(table, bits) for table in tables)
    return alpha, less, m, jnp.where(zone >= 0, root, 0.0), THETA_GAP * alpha * less


def fields(tables_ref, out, x, row, head, zone):
    for ref, value in zip(out, (head,) + params(tables_ref, zone)):
        ref[x, row : row + 8, :] = value


def base(alpha, less, h):
    scaled = alpha * jnp.maximum(-h, 0.0)
    power = jnp.exp(less * jnp.log(jnp.maximum(scaled, 1e-30)))
    plus = 1.0 + power * scaled
    return power, plus, jnp.log(plus)


def retention(h, alpha, less, m, root, gain):
    power, plus, log_plus = base(alpha, less, h)
    fourth = jnp.exp(m * log_plus)
    square = fourth * fourth
    part = power * (square * square)
    return root * fourth * (1.0 - part), TIME_STEP * plus / (STORAGE * plus + gain * part)


def inner_flux(
    head_ref,
    zone_ref,
    wanted_hbm,
    alpha_hbm,
    expo_hbm,
    ks_hbm,
    tables_ref,
    index_ref,
    flux_ref,
    wanted_ref,
    alpha_ref,
    expo_ref,
    ks_ref,
    sems,
):
    fetch([(wanted_hbm, wanted_ref), (alpha_hbm, alpha_ref), (expo_hbm, expo_ref), (ks_hbm, ks_ref)], sems)
    zones, width = alpha_ref.shape[0], tables_ref.shape[1]
    for z in range(zones):
        expo = jnp.full((1, width), expo_ref[z], jnp.float32)
        expo = jnp.where(expo > 0, expo, 2.0)
        tables_ref[z : z + 1, :] = jnp.full((1, width), alpha_ref[z], jnp.float32)
        tables_ref[zones + z : zones + z + 1, :] = expo - 1.0
        tables_ref[2 * zones + z : 2 * zones + z + 1, :] = -0.25 * (1.0 - 1.0 / expo)
        tables_ref[3 * zones + z : 3 * zones + z + 1, :] = jnp.sqrt(jnp.full((1, width), ks_ref[z], jnp.float32))
    wanted = wanted_ref[...]
    index_ref[...] = jnp.concatenate([wanted, pltpu.roll(wanted, wanted.shape[1] // 2, 1)], axis=0).T
    for group in range(flux_ref.shape[0]):
        at = slice(8 * group, 8 * group + 8)
        near, far = head_ref[1, at, :], head_ref[2, at, :]
        r_near, _ = retention(near, *params(tables_ref, zone_ref[1, at, :] + 1))
        r_far, _ = retention(far, *params(tables_ref, zone_ref[2, at, :] + 1))
        flux_ref[group] = r_near * r_far * (far - near)


def prepare(tables_ref, low_ref, high_ref, h, alpha_f, less_f, m_f, root_f, gain_f, r_f, cap_f):
    planes, groups = h.shape[0], h.shape[1] // 8 - 1
    zone_at = 2 * groups + 2
    out = (h, alpha_f, less_f, m_f, root_f, gain_f)
    for x in range(planes):
        source, plane = (low_ref, x) if x < 2 else (high_ref, x - 2)
        for group in range(groups):
            at = plane * groups + group
            fields(tables_ref, out, x, 8 * group, source[at], source[zone_at + at])
        at = 2 * groups + plane
        fields(tables_ref, out, x, 8 * groups, source[at], source[zone_at + at])
        r_f[x], cap_f[x] = retention(*(ref[x] for ref in out))


def seepage(
    crests,
    place_ref,
    tables_ref,
    index,
    own_h,
    own_alpha,
    own_less,
    own_m,
    own_root,
    own_gain,
    own_r,
    own_cap,
    before_ref,
    after_ref,
    head_ref,
    out_ref,
    order_ref,
    h,
    alpha_f,
    less_f,
    m_f,
    root_f,
    gain_f,
    r_f,
    cap_f,
    table,
    deep,
):
    planes = head_ref.shape[0]
    rows = head_ref.shape[1]
    total = planes + 2 * WIDE
    height, depth = h.shape[1], h.shape[2]
    groups = rows // 8
    zone_at = 2 * groups + 2
    lane8 = lax.broadcasted_iota(jnp.int32, (8, 128), 1)
    behind = jnp.where(place_ref[1] > 0, 1.0, 0.0)
    ahead = jnp.where(place_ref[1] < crests - 1, 1.0, 0.0)
    out = (h, alpha_f, less_f, m_f, root_f, gain_f)

    ends = []
    for source, first, inside in ((before_ref, 1, behind), (after_ref, WIDE + planes, ahead)):
        for plane in range(2):
            for group in range(groups):
                at = plane * groups + group
                fields(tables_ref, out, first + plane, 8 * group, source[at], source[zone_at + at] * inside)
            at = 2 * groups + plane
            fields(tables_ref, out, first + plane, rows, source[at], source[zone_at + at] * inside)
        flux = [source[2 * zone_at + group] * inside for group in range(groups)]
        ends.append(jnp.concatenate(flux + [jnp.zeros((height - rows, depth), jnp.float32)], axis=0))
    for x in range(planes):
        h[WIDE + x] = own_h[x]

    own = dict(zip(map(id, (alpha_f, less_f, m_f, root_f, gain_f)), (own_alpha, own_less, own_m, own_root, own_gain)))

    def param(ref, x):
        return own[id(ref)][x - WIDE] if WIDE <= x < WIDE + planes else ref[x]

    inner_z = lax.broadcasted_iota(jnp.int32, (height, depth), 1) < depth - 1

    for sweep in range(SWEEPS):
        held = {}
        for x in range(max(sweep, 1), total - max(sweep, 1)):
            if sweep == 0 and WIDE <= x < WIDE + planes:
                held[x] = (own_r, own_cap, x - WIDE)
            else:
                values = (param(ref, x) for ref in (alpha_f, less_f, m_f, root_f, gain_f))
                r_f[x], cap_f[x] = retention(h[x], *values)
                held[x] = (r_f, cap_f, x)

        def r_of(x):
            return held[x][0][held[x][2]]

        def face(x):
            return r_of(x) * r_of(x + 1) * (h[x + 1] - h[x])

        came = face(sweep) if sweep > 0 else ends[0]
        for x in range(sweep + 1, total - sweep - 1):
            here, r = h[x], r_of(x)
            goes = face(x) if x < total - 2 or sweep > 0 else ends[1]
            flux_y = r * pltpu.roll(r, height - 1, 0) * (pltpu.roll(here, height - 1, 0) - here)
            flux_z = r * pltpu.roll(r, depth - 1, 1) * (pltpu.roll(here, depth - 1, 1) - here + 1.0)
            flux_z = jnp.where(inner_z, flux_z, 0.0)
            inflow = goes - came + (flux_y - pltpu.roll(flux_y, 1, 0)) + (flux_z - pltpu.roll(flux_z, 1, 1))
            h[x] = here + held[x][1][held[x][2]] * inflow
            came = goes

    for x in range(planes):
        here = h[WIDE + x]
        _, _, log_plus = base(own_alpha[x], own_less[x], here)
        head_ref[x] = here[0:rows]
        table[x * rows : (x + 1) * rows, :] = (jnp.exp(4.0 * own_m[x] * log_plus) * here)[0:rows]
    deep[...] = table[...].T
    order_ref[...] = deep[0:8, :]
    bands = depth // BAND
    half = out_ref.shape[0] // 2

    for b in range(bands):
        upper = deep[b * BAND : b * BAND + 8, :]
        lower = deep[b * BAND + 8 : b * BAND + 16, :]
        for d in range(b, half, bands):
            columns = jnp.broadcast_to(index[d : d + 1, :], (8, 128))
            first, second = take_lanes(upper, columns), pltpu.roll(take_lanes(lower, columns), 64, 1)
            out_ref[d] = jnp.where(lane8 < 64, first, second)
            out_ref[half + d] = jnp.where(lane8 < 64, second, first)


def element_rows(value):
    return jnp.concatenate([value[r : r + 1] for r in range(8)], axis=1)


def selectors(
    partitions,
    place_ref,
    order_ref,
    disp_hbm,
    stress_hbm,
    conn_hbm,
    strain_hbm,
    force_hbm,
    slot_hbm,
    depth_hbm,
    zone_hbm,
    cohesion_hbm,
    friction_hbm,
    disp_ref,
    stress_ref,
    conn_ref,
    strain_ref,
    force_ref,
    strength_ref,
    at_ref,
    slot_ref,
    depth_ref,
    zone_ref,
    cohesion_ref,
    friction_ref,
    sems,
):
    del order_ref
    fetch(
        [
            (conn_hbm, conn_ref),
            (slot_hbm, slot_ref),
            (depth_hbm, depth_ref),
            (zone_hbm, zone_ref),
            (cohesion_hbm, cohesion_ref),
            (friction_hbm, friction_ref),
            (disp_hbm, disp_ref),
            (stress_hbm, stress_ref),
            (strain_hbm, strain_ref),
            (force_hbm, force_ref),
        ],
        sems,
    )
    elems = conn_ref.shape[1]
    slot, depth = slot_ref[...], depth_ref[...]
    swap = jnp.where(place_ref[2] >= partitions // 2, 1, 0)
    at_ref[0:1, :] = element_rows((slot >> 6) * 8 + (depth & 7))
    at_ref[1:2, :] = element_rows(((depth >> 3) ^ swap) * 64 + (slot & 63))
    zone = zone_ref[...]
    tan_red = pick(friction_ref, zone) * (1.0 / REDUCTION)
    cos_red = 1.0 / jnp.sqrt(1.0 + tan_red * tan_red)
    sin_red = tan_red * cos_red
    common = 6.0 / (np.sqrt(3.0).astype(np.float32) * (3.0 - sin_red))
    strength_ref[0:1, :] = element_rows(common * (pick(cohesion_ref, zone) * (1.0 / REDUCTION)) * cos_red)
    strength_ref[1:2, :] = element_rows(common * sin_red)


def trial_state(
    sections, place_ref, matrix_ref, disp_ref, after_ref, tail_ref, conn_ref, stress_ref, trial_ref, nodes, corners
):
    ghost = jnp.where(place_ref[0] < sections - 1, after_ref[24:32, :], tail_ref[tail_ref.shape[0] - 1])
    for comp in range(3):
        for s in range(8):
            nodes[comp * 12 + s : comp * 12 + s + 1, :] = disp_ref[comp : comp + 1, s * 128 : (s + 1) * 128]
        for s in range(4):
            at = 2 * comp + s // 2
            nodes[comp * 12 + 8 + s : comp * 12 + 9 + s, :] = ghost[at : at + 1, (s % 2) * 128 : (s % 2 + 1) * 128]
    elems = conn_ref.shape[1]

    @pl.loop(0, elems, step=128)
    def _(e):
        e = pl.multiple_of(e, 128)
        index = conn_ref[:, pl.ds(e, 128)]
        lanes, segment = index & 127, index >> 7
        found = [jnp.zeros((8, 128), jnp.float32) for _ in range(3)]
        for s in range(12):
            here = segment == s
            for comp in range(3):
                row = nodes[comp * 12 + s : comp * 12 + s + 1, :]
                found[comp] = jnp.where(here, take_lanes(row, lanes), found[comp])
        for comp in range(3):
            corners[comp * 8 : comp * 8 + 8, pl.ds(e, 128)] = found[comp]

    strain = jnp.dot(
        matrix_ref[...], corners[...], precision=lax.Precision.HIGHEST, preferred_element_type=jnp.float32
    )
    lame_first = YOUNG * POISSON / ((1.0 + POISSON) * (1.0 - 2.0 * POISSON))
    modulus = YOUNG / (2.0 * (1.0 + POISSON))
    part = [strain[8 * i : 8 * i + 8] for i in range(6)]
    volume = lame_first * (part[0] + part[1] + part[2])
    normals = [stress_ref[i] + volume + 2.0 * modulus * part[i] for i in range(3)]
    shears = [stress_ref[i] + modulus * part[i] for i in range(3, 6)]
    mean = (normals[0] + normals[1] + normals[2]) * (1.0 / 3.0)
    devs = [value - mean for value in normals]
    trial_ref[6] = mean
    trial_ref[7] = jnp.sqrt(
        0.5 * (devs[0] ** 2 + devs[1] ** 2 + devs[2] ** 2) + shears[0] ** 2 + shears[1] ** 2 + shears[2] ** 2
    )
    for i in range(3):
        trial_ref[i] = devs[i]
        trial_ref[3 + i] = shears[i]


def halves(value):
    high = value.astype(jnp.bfloat16).astype(jnp.float32)
    return high, value - high


def node_lanes(node, elems):
    in_lane = lax.broadcasted_iota(jnp.int32, (128, elems), 0)
    return jnp.where(jnp.broadcast_to(node & 127, in_lane.shape) == in_lane, 1.0, 0.0).astype(jnp.bfloat16)


def final_state(
    matrix_ref, band_ref, at_ref, strength_ref, trial_ref, conn_ref, stress_ref, release_ref, force_ref, ghost_ref
):
    elems = conn_ref.shape[1]
    count = band_ref.shape[0]
    split = count // 2
    high, low = halves(band_ref[0:split, :])
    in_row = lax.broadcasted_iota(jnp.int32, (split, elems), 0) == at_ref[0:1, :]
    found = lax.dot_general(
        jnp.concatenate([high, low], axis=1).astype(jnp.bfloat16),
        jnp.where(in_row, 1.0, 0.0).astype(jnp.bfloat16),
        (((0,), (0,)), ((), ())),
        preferred_element_type=jnp.float32,
    )
    found = found[0:128] + found[128:256]
    in_lane = lax.broadcasted_iota(jnp.int32, (128, elems), 0)
    pore = jnp.sum(jnp.where(in_lane == at_ref[1:2, :], found, 0.0), axis=0, keepdims=True)
    row8, lane8 = (
        jnp.concatenate([at_ref[i : i + 1, r * 128 : (r + 1) * 128] for r in range(8)], axis=0) for i in range(2)
    )
    parts = [jnp.zeros((8, 128), jnp.float32) for _ in range(4)]
    for r in range(split, count):
        parts[r % 4] = jnp.where(row8 == r, take_lanes(band_ref[r : r + 1, :], lane8), parts[r % 4])
    pore = pore + element_rows((parts[0] + parts[1]) + (parts[2] + parts[3]))
    allow = jnp.maximum(strength_ref[0:1, :] - strength_ref[1:2, :] * (trial_ref[6] + pore), 0.0)
    deviator = trial_ref[7]
    yielded = deviator > allow
    scale = jnp.where(yielded, allow / jnp.where(yielded, deviator, 1.0), 1.0)
    release_ref[...] = (1.0 - scale) * deviator
    mean = trial_ref[6]
    parts = [mean + scale * trial_ref[i] for i in range(3)] + [scale * trial_ref[3 + i] for i in range(3)]
    for i in range(6):
        stress_ref[i] = parts[i]
    force = jnp.dot(
        matrix_ref[...],
        jnp.concatenate(parts, axis=0),
        precision=lax.Precision.HIGHEST,
        preferred_element_type=jnp.float32,
    )
    force_ref[...] = force
    high, low = halves(force)
    tile = lax.broadcasted_iota(jnp.int32, (8, elems), 0)
    total = jnp.zeros((32, 128), jnp.float32)
    for corner in range(8):
        node = conn_ref[corner : corner + 1, :]
        here = jnp.broadcast_to(node >> 7, tile.shape) == 8 + (tile & 3)
        rows = []
        for comp in range(3):
            at = slice(comp * 8 + corner, comp * 8 + corner + 1)
            value = jnp.where(tile < 4, jnp.broadcast_to(high[at], tile.shape), jnp.broadcast_to(low[at], tile.shape))
            rows.append(jnp.where(here, value, 0.0))
        rows.append(jnp.zeros(tile.shape, jnp.float32))
        left = jnp.concatenate(rows, axis=0).astype(jnp.bfloat16)
        total += lax.dot_general(
            left, node_lanes(node, elems), (((1,), (1,)), ((), ())), preferred_element_type=jnp.float32
        )
    for comp in range(3):
        ghost_ref[comp * 4 : comp * 4 + 4, :] = total[comp * 8 : comp * 8 + 4] + total[comp * 8 + 4 : comp * 8 + 8]


def own_forces(force_ref, conn_ref, own_ref):
    elems = conn_ref.shape[1]
    high, low = halves(force_ref[...])
    tile = lax.broadcasted_iota(jnp.int32, (8, elems), 0)
    total = jnp.zeros((48, 128), jnp.float32)
    for corner in range(8):
        node = conn_ref[corner : corner + 1, :]
        here = jnp.broadcast_to(node >> 7, tile.shape) == tile
        rows = []
        for comp in range(3):
            for source in (high, low):
                value = source[comp * 8 + corner : comp * 8 + corner + 1]
                rows.append(jnp.where(here, jnp.broadcast_to(value, tile.shape), 0.0))
        left = jnp.concatenate(rows, axis=0).astype(jnp.bfloat16)
        total += lax.dot_general(
            left, node_lanes(node, elems), (((1,), (1,)), ((), ())), preferred_element_type=jnp.float32
        )
    for comp in range(3):
        own_ref[comp * 8 : comp * 8 + 8, :] = total[comp * 16 : comp * 16 + 8] + total[comp * 16 + 8 : comp * 16 + 16]


def add_returned(own_ref, ghost_ref, shared_ref, out_ref):
    shared = shared_ref[...]
    in_lane = lax.broadcasted_iota(jnp.int32, (128, 128), 0)
    in_segment = lax.broadcasted_iota(jnp.int32, (8, 128), 0)
    lefts, rights = [], []
    for s in range(4):
        node = shared[s : s + 1]
        rights.append(jnp.where(jnp.broadcast_to(node & 127, in_lane.shape) == in_lane, 1.0, 0.0))
        here = jnp.broadcast_to(node >> 7, in_segment.shape) == in_segment
        rows = []
        for comp in range(3):
            value = ghost_ref[comp * 4 + s : comp * 4 + s + 1, :]
            high, low = halves(value)
            for piece in (high, low):
                rows.append(jnp.where(here, jnp.broadcast_to(piece, in_segment.shape), 0.0))
        lefts.append(jnp.concatenate(rows, axis=0))
    left = jnp.concatenate(lefts, axis=1).astype(jnp.bfloat16)
    right = jnp.concatenate(rights, axis=1).astype(jnp.bfloat16)
    added = lax.dot_general(left, right, (((1,), (1,)), ((), ())), preferred_element_type=jnp.float32)
    for comp in range(3):
        total = own_ref[comp * 8 : comp * 8 + 8, :] + added[comp * 16 : comp * 16 + 8] + added[comp * 16 + 8 : comp * 16 + 16]
        for s in range(8):
            out_ref[comp : comp + 1, s * 128 : (s + 1) * 128] = total[s : s + 1]


VM = pl.BlockSpec(memory_space=pltpu.VMEM)
SM = pl.BlockSpec(memory_space=pltpu.SMEM)


HBM = pl.BlockSpec(memory_space=pltpu.HBM)


def call(body, specs, outs, scratch, name, types=None):
    types = types or [jnp.float32] * len(outs)
    return pl.pallas_call(
        body,
        in_specs=specs,
        out_specs=tuple(VM for _ in outs),
        out_shape=tuple(jax.ShapeDtypeStruct(shape, kind) for shape, kind in zip(outs, types)),
        scratch_shapes=scratch,
        compiler_params=pltpu.CompilerParams(vmem_limit_bytes=VMEM_LIMIT),
        name=name,
    )


def in_hbm(value):
    return pltpu.with_memory_space_constraint(value, pltpu.HBM)


def steps(count, by):
    return [(i, (i + by) % count) for i in range(count)]


def per_device(
    pressure_head,
    zone_ids,
    retention_alpha,
    retention_exponent,
    conductivity,
    sent_columns,
    displacement,
    stress_old,
    connectivity,
    shared_nodes,
    element_zone,
    element_slot,
    element_depth,
    cohesion,
    friction,
):
    crest, section = (lax.axis_size(axis) for axis in AXES)
    devices = crest * section
    planes, rows, depth = pressure_head.shape
    height = rows + 8
    elems = connectivity.shape[1]
    nodes = displacement.shape[1]
    shared = shared_nodes.reshape(4, 128)
    zones = retention_alpha.shape[0]
    place = jnp.stack([lax.axis_index("section"), lax.axis_index("crest"), lax.axis_index(AXES)])
    i32, f32 = jnp.int32, jnp.float32

    forward, backward, head, zone = call(
        pack_section,
        [HBM] * 4,
        [(2 * WIDE * planes, depth), (32, depth), pressure_head.shape, zone_ids.shape],
        [pltpu.VMEM(displacement.shape, f32), pltpu.VMEM(shared.shape, i32), pltpu.SemaphoreType.DMA((4,))],
        "pack_section",
        [f32, f32, f32, i32],
    )(*(in_hbm(x) for x in (pressure_head, zone_ids, displacement, shared)))
    before = lax.ppermute(forward, "section", steps(section, 1))
    after = lax.ppermute(backward, "section", steps(section, -1))

    groups = rows // 8
    tables, index, flux = call(
        inner_flux,
        [VM] * 2 + [HBM] * 4,
        [(4 * zones, depth), (devices, 128), (groups, 8, depth)],
        [pltpu.VMEM((64, devices), i32)] + [pltpu.SMEM((zones,), f32)] * 3 + [pltpu.SemaphoreType.DMA((4,))],
        "inner_flux",
        [f32, i32, f32],
    )(head, zone, *(in_hbm(x) for x in (sent_columns[0].T, retention_alpha, retention_exponent, conductivity)))

    edge = (2 * (2 * groups + 2) + groups, 8, depth)
    low, high = call(
        functools.partial(pack_crest, section),
        [SM] + [VM] * 5,
        [(edge[0] + 1, 8, depth), edge],
        [],
        "pack_crest",
    )(place, head, zone, flux, before, after)
    west = lax.ppermute(high, "crest", steps(crest, 1))
    east = lax.ppermute(low, "crest", steps(crest, -1))
    own = call(prepare, [VM] * 3, [(planes, height, depth)] * 8, [], "prepare")(tables, low, high)

    field = pltpu.VMEM((planes + 2 * WIDE, height, depth), f32)
    head_out, outgoing, order = call(
        functools.partial(seepage, crest),
        [SM] + [VM] * 12,
        [pressure_head.shape, (devices, 8, 128), (8, 128)],
        [field] * 8 + [pltpu.VMEM((planes * rows, depth), f32), pltpu.VMEM((depth, planes * rows), f32)],
        "seepage",
    )(place, tables, index, *own, west, east)

    matrix = component_major()
    disp, stress, conn, strain_rows, force_rows, strength, places = call(
        functools.partial(selectors, devices),
        [SM, VM] + [HBM] * 10,
        [
            displacement.shape,
            (6, 8, elems),
            connectivity.shape,
            (48, 24),
            (24, 48),
            (2, elems),
            (2, elems),
        ],
        [pltpu.VMEM((8, 128), i32)] * 3 + [pltpu.SMEM((zones,), f32)] * 2 + [pltpu.SemaphoreType.DMA((10,))],
        "selectors",
        [f32, f32, i32, f32, f32, f32, i32],
    )(
        place,
        order,
        *(
            in_hbm(x)
            for x in (
                displacement,
                stress_old.transpose(1, 0, 2),
                connectivity,
                jnp.asarray(matrix, f32),
                jnp.asarray(matrix.T * 0.125, f32),
                element_slot.reshape(8, 128),
                element_depth.reshape(8, 128),
                element_zone.reshape(8, 128),
                cohesion,
                friction,
            )
        ),
    )
    (trial,) = call(
        functools.partial(trial_state, section),
        [SM] + [VM] * 6,
        [(8, 8, elems)],
        [pltpu.VMEM((40, 128), f32), pltpu.VMEM((24, elems), f32)],
        "trial_state",
    )(place, strain_rows, disp, after, east, conn, stress)
    incoming = lax.all_to_all(outgoing, AXES, split_axis=0, concat_axis=0, tiled=True)

    stress_new, release, force, ghost = call(
        final_state,
        [VM] * 6,
        [(6, 8, elems), (8, elems), (24, elems), (12, 128)],
        [],
        "final_state",
    )(force_rows, incoming.reshape(devices * 8, 128), places, strength, trial, conn)
    returned = lax.ppermute(ghost, AXES, steps(devices, 1))
    (own,) = call(own_forces, [VM] * 2, [(24, 128)], [], "own_forces")(force, conn)
    (node_forces,) = call(add_returned, [VM] * 3, [(3, nodes)], [], "add_returned")(own, returned, shared)
    return (head_out, stress_new.transpose(1, 0, 2), release, node_forces)


def solution(mesh):
    return jax.shard_map(
        per_device,
        mesh=mesh,
        in_specs=(
            P("crest", "section", None),
            P("crest", "section", None),
            P(),
            P(),
            P(),
            P(("crest", "section"), None, None),
            P(None, ("crest", "section")),
            P(None, None, ("crest", "section")),
            P(None, ("crest", "section")),
            P(("crest", "section")),
            P(("crest", "section")),
            P(("crest", "section")),
            P(("crest", "section")),
            P(),
            P(),
        ),
        out_specs=(
            P("crest", "section", None),
            P(None, None, ("crest", "section")),
            P(None, ("crest", "section")),
            P(None, ("crest", "section")),
        ),
        check_vma=False,
    )
```

```python
import functools

import jax
import jax.numpy as jnp
import numpy as np
from jax import lax
from jax.experimental import pallas as pl
from jax.experimental.pallas import tpu as pltpu
from jax.sharding import PartitionSpec as P

BAND = 16
SWEEPS = 3
WIDE = 3

STORAGE = 0.5
THETA_GAP = 0.35
TIME_STEP = 0.05
REDUCTION = 1.4
YOUNG = 200.0
POISSON = 0.3

AXES = ("crest", "section")
VMEM_LIMIT = 32 * 1024 * 1024


def corner_signs(index):
    return (2 * (index & 1) - 1, 2 * (index >> 1 & 1) - 1, 2 * (index >> 2 & 1) - 1)


def strain_matrix():
    matrix = np.zeros((48, 24))
    inv_root = 1.0 / np.sqrt(3.0)
    for gauss_point in range(8):
        gauss = [value * inv_root for value in corner_signs(gauss_point)]
        row_start = 6 * gauss_point
        for node_corner in range(8):
            sign_x, sign_y, sign_z = corner_signs(node_corner)
            grad_x = 0.25 * sign_x * (1 + gauss[1] * sign_y) * (1 + gauss[2] * sign_z)
            grad_y = 0.25 * sign_y * (1 + gauss[0] * sign_x) * (1 + gauss[2] * sign_z)
            grad_z = 0.25 * sign_z * (1 + gauss[0] * sign_x) * (1 + gauss[1] * sign_y)
            matrix[row_start + 0, node_corner] = grad_x
            matrix[row_start + 1, 8 + node_corner] = grad_y
            matrix[row_start + 2, 16 + node_corner] = grad_z
            matrix[row_start + 3, node_corner] = grad_y
            matrix[row_start + 3, 8 + node_corner] = grad_x
            matrix[row_start + 4, 8 + node_corner] = grad_z
            matrix[row_start + 4, 16 + node_corner] = grad_y
            matrix[row_start + 5, 16 + node_corner] = grad_x
            matrix[row_start + 5, node_corner] = grad_z
    return matrix


def component_major():
    order = [6 * gauss_point + comp for comp in range(6) for gauss_point in range(8)]
    return strain_matrix()[order]


def take_lanes(row, lanes):
    return jnp.take_along_axis(jnp.broadcast_to(row, lanes.shape), lanes, axis=1, mode="promise_in_bounds")


def pick(values_ref, index, first=0):
    lane = lax.broadcasted_iota(jnp.int32, (8, 128), 1)
    table = jnp.zeros((8, 128), jnp.float32)
    for zone in range(values_ref.shape[0]):
        table = jnp.where(lane == first + zone, values_ref[zone], table)
    return table if index is None else take_lanes(table, index)


def fetch(pairs, sems):
    copies = [pltpu.make_async_copy(source, target, sems.at[i]) for i, (source, target) in enumerate(pairs)]
    for copy in copies:
        copy.start()
    for copy in copies:
        copy.wait()


def pack_section(
    head_hbm, zone_hbm, disp_hbm, shared_hbm, forward_ref, backward_ref, head_ref, zone_ref, disp_ref, shared_ref, sems
):
    fetch([(head_hbm, head_ref), (zone_hbm, zone_ref), (disp_hbm, disp_ref), (shared_hbm, shared_ref)], sems)
    planes, rows = head_ref.shape[0], head_ref.shape[1]
    for x in range(planes):
        for field in range(2):
            first, last = slice(0, WIDE), slice(rows - WIDE, rows)
            at = field * WIDE * planes + WIDE * x
            if field == 0:
                forward_ref[at : at + WIDE, :] = head_ref[x, last, :]
                backward_ref[at : at + WIDE, :] = head_ref[x, first, :]
            else:
                forward_ref[at : at + WIDE, :] = zone_ref[x, last, :].astype(jnp.float32) + 1.0
                backward_ref[at : at + WIDE, :] = zone_ref[x, first, :].astype(jnp.float32) + 1.0
    index = shared_ref[...]
    index = jnp.concatenate([index, index], axis=0)
    lanes, segment = index & 127, index >> 7
    for comp in range(3):
        found = jnp.zeros((8, 128), jnp.float32)
        for s in range(disp_ref.shape[1] // 128):
            row = disp_ref[comp : comp + 1, s * 128 : (s + 1) * 128]
            found = jnp.where(segment == s, take_lanes(row, lanes), found)
        for s in range(4):
            at = 2 * WIDE * planes + 2 * comp + s // 2
            backward_ref[at : at + 1, (s % 2) * 128 : (s % 2 + 1) * 128] = found[s : s + 1]
    backward_ref[30:32, :] = jnp.zeros((2, 256), jnp.float32)


def pack_crest(sections, place_ref, head_ref, zone_ref, flux_ref, before_ref, after_ref, low_ref, high_ref, tail_ref):
    planes, rows = head_ref.shape[0], head_ref.shape[1]
    groups = rows // 8
    behind = jnp.where(place_ref[0] > 0, 1.0, 0.0)
    ahead = jnp.where(place_ref[0] < sections - 1, 1.0, 0.0)
    zone_at = 2 * groups + 1
    row = lax.broadcasted_iota(jnp.int32, (8, after_ref.shape[1]), 0)
    for field in range(2):
        tails = []
        for x in range(planes):
            target, plane = (low_ref, x) if x < 2 else (high_ref, x - 2)
            first = field * zone_at
            for group in range(groups):
                at = slice(8 * group, 8 * group + 8)
                own = head_ref[x, at, :] if field == 0 else zone_ref[x, at, :].astype(jnp.float32) + 1.0
                target[first + plane * groups + group] = own
            at = field * WIDE * planes + WIDE * x
            tails.append(
                jnp.concatenate(
                    [
                        after_ref[at : at + WIDE, :] * ahead,
                        jnp.zeros((2, after_ref.shape[1]), jnp.float32),
                        before_ref[at : at + WIDE, :] * behind,
                    ],
                    axis=0,
                )
            )
            tail_ref[field * planes + x] = tails[-1]
        for target, near, next_one in ((low_ref, 0, 1), (high_ref, 3, 2)):
            inner = jnp.where(row < 4, pltpu.roll(tails[next_one], 2, 0), pltpu.roll(tails[next_one], 6, 0))
            shared = jnp.where((row == 2) | (row == 5), inner, tails[near])
            target[field * zone_at + 2 * groups] = shared
    for group in range(groups):
        low_ref[2 * zone_at + group] = flux_ref[group]
        high_ref[2 * zone_at + group] = flux_ref[group]
    low_ref[2 * zone_at + groups] = after_ref[24:32, :]


def choose(values, bits):
    for bit in bits:
        values = [jnp.where(bit, values[i + 1], values[i]) for i in range(0, len(values), 2)]
    return values[0]


def params(tables_ref, zone):
    zones = tables_ref.shape[0] // 4
    tables = [
        [jnp.broadcast_to(tables_ref[f * zones + z : f * zones + z + 1, :], zone.shape) for z in range(zones)]
        for f in range(4)
    ]
    zone = zone.astype(jnp.int32) - 1
    bits = [(zone & (1 << bit)) != 0 for bit in range(3)]
    alpha, less, m, root = (choose(table, bits) for table in tables)
    return alpha, less, m, jnp.where(zone >= 0, root, 0.0), THETA_GAP * alpha * less


def fields(tables_ref, out, x, row, head, zone):
    for ref, value in zip(out, (head,) + params(tables_ref, zone)):
        ref[x, row : row + 8, :] = value


def base(alpha, less, h):
    scaled = alpha * jnp.maximum(-h, 0.0)
    power = jnp.exp(less * jnp.log(jnp.maximum(scaled, 1e-30)))
    plus = 1.0 + power * scaled
    return power, plus, jnp.log(plus)


def retention(h, alpha, less, m, root, gain):
    power, plus, log_plus = base(alpha, less, h)
    fourth = jnp.exp(m * log_plus)
    square = fourth * fourth
    part = power * (square * square)
    return root * fourth * (1.0 - part), TIME_STEP * plus / (STORAGE * plus + gain * part)


def inner_flux(
    head_ref,
    zone_ref,
    wanted_hbm,
    alpha_hbm,
    expo_hbm,
    ks_hbm,
    tables_ref,
    index_ref,
    flux_ref,
    wanted_ref,
    alpha_ref,
    expo_ref,
    ks_ref,
    sems,
):
    fetch([(wanted_hbm, wanted_ref), (alpha_hbm, alpha_ref), (expo_hbm, expo_ref), (ks_hbm, ks_ref)], sems)
    zones, width = alpha_ref.shape[0], tables_ref.shape[1]
    for z in range(zones):
        expo = jnp.full((1, width), expo_ref[z], jnp.float32)
        expo = jnp.where(expo > 0, expo, 2.0)
        tables_ref[z : z + 1, :] = jnp.full((1, width), alpha_ref[z], jnp.float32)
        tables_ref[zones + z : zones + z + 1, :] = expo - 1.0
        tables_ref[2 * zones + z : 2 * zones + z + 1, :] = -0.25 * (1.0 - 1.0 / expo)
        tables_ref[3 * zones + z : 3 * zones + z + 1, :] = jnp.sqrt(jnp.full((1, width), ks_ref[z], jnp.float32))
    wanted = wanted_ref[...]
    index_ref[...] = jnp.concatenate([wanted, pltpu.roll(wanted, wanted.shape[1] // 2, 1)], axis=0).T
    for group in range(flux_ref.shape[0]):
        at = slice(8 * group, 8 * group + 8)
        near, far = head_ref[1, at, :], head_ref[2, at, :]
        r_near, _ = retention(near, *params(tables_ref, zone_ref[1, at, :] + 1))
        r_far, _ = retention(far, *params(tables_ref, zone_ref[2, at, :] + 1))
        flux_ref[group] = r_near * r_far * (far - near)


def prepare(tables_ref, low_ref, high_ref, tail_ref, h, alpha_f, less_f, m_f, root_f, gain_f, r_f, cap_f):
    planes, groups = h.shape[0], h.shape[1] // 8 - 1
    zone_at = 2 * groups + 1
    out = (h, alpha_f, less_f, m_f, root_f, gain_f)
    for x in range(planes):
        source, plane = (low_ref, x) if x < 2 else (high_ref, x - 2)
        for group in range(groups):
            at = plane * groups + group
            fields(tables_ref, out, x, 8 * group, source[at], source[zone_at + at])
        fields(tables_ref, out, x, 8 * groups, tail_ref[x], tail_ref[planes + x])
        r_f[x], cap_f[x] = retention(*(ref[x] for ref in out))


def seepage(
    crests,
    place_ref,
    tables_ref,
    index,
    own_h,
    own_alpha,
    own_less,
    own_m,
    own_root,
    own_gain,
    own_r,
    own_cap,
    before_ref,
    after_ref,
    head_ref,
    out_ref,
    order_ref,
    h,
    alpha_f,
    less_f,
    m_f,
    root_f,
    gain_f,
    r_f,
    cap_f,
    table,
    deep,
):
    planes = head_ref.shape[0]
    rows = head_ref.shape[1]
    total = planes + 2 * WIDE
    height, depth = h.shape[1], h.shape[2]
    groups = rows // 8
    zone_at = 2 * groups + 1
    lane8 = lax.broadcasted_iota(jnp.int32, (8, 128), 1)
    behind = jnp.where(place_ref[1] > 0, 1.0, 0.0)
    ahead = jnp.where(place_ref[1] < crests - 1, 1.0, 0.0)
    out = (h, alpha_f, less_f, m_f, root_f, gain_f)

    row = lax.broadcasted_iota(jnp.int32, (8, depth), 0)

    def tail_of(shared, near):
        if near:
            return jnp.where((row < 2) | (row > 5), shared, 0.0)
        return jnp.where(row == 0, pltpu.roll(shared, 6, 0), jnp.where(row == 7, pltpu.roll(shared, 2, 0), 0.0))

    ends = []
    for source, first, inside in ((before_ref, 1, behind), (after_ref, WIDE + planes, ahead)):
        for plane in range(2):
            for group in range(groups):
                at = plane * groups + group
                fields(tables_ref, out, first + plane, 8 * group, source[at], source[zone_at + at] * inside)
            near = (first + plane) in (WIDE - 1, WIDE + planes)
            head, zone = tail_of(source[2 * groups], near), tail_of(source[zone_at + 2 * groups], near)
            fields(tables_ref, out, first + plane, rows, head, zone * inside)
        flux = [source[2 * zone_at + group] * inside for group in range(groups)]
        ends.append(jnp.concatenate(flux + [jnp.zeros((height - rows, depth), jnp.float32)], axis=0))
    for x in range(planes):
        h[WIDE + x] = own_h[x]

    own = dict(zip(map(id, (alpha_f, less_f, m_f, root_f, gain_f)), (own_alpha, own_less, own_m, own_root, own_gain)))

    def param(ref, x):
        return own[id(ref)][x - WIDE] if WIDE <= x < WIDE + planes else ref[x]

    inner_z = lax.broadcasted_iota(jnp.int32, (height, depth), 1) < depth - 1

    for sweep in range(SWEEPS):
        held = {}
        for x in range(max(sweep, 1), total - max(sweep, 1)):
            if sweep == 0 and WIDE <= x < WIDE + planes:
                held[x] = (own_r, own_cap, x - WIDE)
            else:
                values = (param(ref, x) for ref in (alpha_f, less_f, m_f, root_f, gain_f))
                r_f[x], cap_f[x] = retention(h[x], *values)
                held[x] = (r_f, cap_f, x)

        def r_of(x):
            return held[x][0][held[x][2]]

        def face(x):
            return r_of(x) * r_of(x + 1) * (h[x + 1] - h[x])

        came = face(sweep) if sweep > 0 else ends[0]
        for x in range(sweep + 1, total - sweep - 1):
            here, r = h[x], r_of(x)
            goes = face(x) if x < total - 2 or sweep > 0 else ends[1]
            flux_y = r * pltpu.roll(r, height - 1, 0) * (pltpu.roll(here, height - 1, 0) - here)
            flux_z = r * pltpu.roll(r, depth - 1, 1) * (pltpu.roll(here, depth - 1, 1) - here + 1.0)
            flux_z = jnp.where(inner_z, flux_z, 0.0)
            inflow = goes - came + (flux_y - pltpu.roll(flux_y, 1, 0)) + (flux_z - pltpu.roll(flux_z, 1, 1))
            h[x] = here + held[x][1][held[x][2]] * inflow
            came = goes

    for x in range(planes):
        here = h[WIDE + x]
        _, _, log_plus = base(own_alpha[x], own_less[x], here)
        head_ref[x] = here[0:rows]
        table[x * rows : (x + 1) * rows, :] = (jnp.exp(4.0 * own_m[x] * log_plus) * here)[0:rows]
    deep[...] = table[...].T
    order_ref[...] = deep[0:8, :]
    bands = depth // BAND
    half = out_ref.shape[0] // 2

    for b in range(bands):
        upper = deep[b * BAND : b * BAND + 8, :]
        lower = deep[b * BAND + 8 : b * BAND + 16, :]
        for d in range(b, half, bands):
            columns = jnp.broadcast_to(index[d : d + 1, :], (8, 128))
            first, second = take_lanes(upper, columns), pltpu.roll(take_lanes(lower, columns), 64, 1)
            out_ref[d] = jnp.where(lane8 < 64, first, second)
            out_ref[half + d] = jnp.where(lane8 < 64, second, first)


def element_rows(value):
    return jnp.concatenate([value[r : r + 1] for r in range(8)], axis=1)


def selectors(
    partitions,
    place_ref,
    order_ref,
    disp_hbm,
    stress_hbm,
    conn_hbm,
    strain_hbm,
    force_hbm,
    slot_hbm,
    depth_hbm,
    zone_hbm,
    cohesion_hbm,
    friction_hbm,
    disp_ref,
    stress_ref,
    conn_ref,
    strain_ref,
    force_ref,
    strength_ref,
    at_ref,
    slot_ref,
    depth_ref,
    zone_ref,
    cohesion_ref,
    friction_ref,
    sems,
):
    del order_ref
    fetch(
        [
            (conn_hbm, conn_ref),
            (slot_hbm, slot_ref),
            (depth_hbm, depth_ref),
            (zone_hbm, zone_ref),
            (cohesion_hbm, cohesion_ref),
            (friction_hbm, friction_ref),
            (disp_hbm, disp_ref),
            (stress_hbm, stress_ref),
            (strain_hbm, strain_ref),
            (force_hbm, force_ref),
        ],
        sems,
    )
    elems = conn_ref.shape[1]
    slot, depth = slot_ref[...], depth_ref[...]
    swap = jnp.where(place_ref[2] >= partitions // 2, 1, 0)
    at_ref[0:1, :] = element_rows((slot >> 6) * 8 + (depth & 7))
    at_ref[1:2, :] = element_rows(((depth >> 3) ^ swap) * 64 + (slot & 63))
    zone = zone_ref[...]
    tan_red = pick(friction_ref, zone) * (1.0 / REDUCTION)
    cos_red = 1.0 / jnp.sqrt(1.0 + tan_red * tan_red)
    sin_red = tan_red * cos_red
    common = 6.0 / (np.sqrt(3.0).astype(np.float32) * (3.0 - sin_red))
    strength_ref[0:1, :] = element_rows(common * (pick(cohesion_ref, zone) * (1.0 / REDUCTION)) * cos_red)
    strength_ref[1:2, :] = element_rows(common * sin_red)


def trial_state(
    sections, place_ref, matrix_ref, disp_ref, after_ref, tail_ref, conn_ref, stress_ref, trial_ref, nodes, corners
):
    ghost = jnp.where(place_ref[0] < sections - 1, after_ref[24:32, :], tail_ref[tail_ref.shape[0] - 1])
    for comp in range(3):
        for s in range(8):
            nodes[comp * 12 + s : comp * 12 + s + 1, :] = disp_ref[comp : comp + 1, s * 128 : (s + 1) * 128]
        for s in range(4):
            at = 2 * comp + s // 2
            nodes[comp * 12 + 8 + s : comp * 12 + 9 + s, :] = ghost[at : at + 1, (s % 2) * 128 : (s % 2 + 1) * 128]
    elems = conn_ref.shape[1]

    @pl.loop(0, elems, step=128)
    def _(e):
        e = pl.multiple_of(e, 128)
        index = conn_ref[:, pl.ds(e, 128)]
        lanes, segment = index & 127, index >> 7
        found = [jnp.zeros((8, 128), jnp.float32) for _ in range(3)]
        for s in range(12):
            here = segment == s
            for comp in range(3):
                row = nodes[comp * 12 + s : comp * 12 + s + 1, :]
                found[comp] = jnp.where(here, take_lanes(row, lanes), found[comp])
        for comp in range(3):
            corners[comp * 8 : comp * 8 + 8, pl.ds(e, 128)] = found[comp]

    strain = jnp.dot(
        matrix_ref[...], corners[...], precision=lax.Precision.HIGHEST, preferred_element_type=jnp.float32
    )
    lame_first = YOUNG * POISSON / ((1.0 + POISSON) * (1.0 - 2.0 * POISSON))
    modulus = YOUNG / (2.0 * (1.0 + POISSON))
    part = [strain[8 * i : 8 * i + 8] for i in range(6)]
    volume = lame_first * (part[0] + part[1] + part[2])
    normals = [stress_ref[i] + volume + 2.0 * modulus * part[i] for i in range(3)]
    shears = [stress_ref[i] + modulus * part[i] for i in range(3, 6)]
    mean = (normals[0] + normals[1] + normals[2]) * (1.0 / 3.0)
    devs = [value - mean for value in normals]
    trial_ref[6] = mean
    trial_ref[7] = jnp.sqrt(
        0.5 * (devs[0] ** 2 + devs[1] ** 2 + devs[2] ** 2) + shears[0] ** 2 + shears[1] ** 2 + shears[2] ** 2
    )
    for i in range(3):
        trial_ref[i] = devs[i]
        trial_ref[3 + i] = shears[i]


def halves(value):
    high = value.astype(jnp.bfloat16).astype(jnp.float32)
    return high, value - high


def node_lanes(node, elems):
    in_lane = lax.broadcasted_iota(jnp.int32, (128, elems), 0)
    return jnp.where(jnp.broadcast_to(node & 127, in_lane.shape) == in_lane, 1.0, 0.0).astype(jnp.bfloat16)


def final_state(
    matrix_ref, band_ref, at_ref, strength_ref, trial_ref, conn_ref, stress_ref, release_ref, force_ref, ghost_ref
):
    elems = conn_ref.shape[1]
    count = band_ref.shape[0]
    split = count // 2
    high, low = halves(band_ref[0:split, :])
    in_row = lax.broadcasted_iota(jnp.int32, (split, elems), 0) == at_ref[0:1, :]
    found = lax.dot_general(
        jnp.concatenate([high, low], axis=1).astype(jnp.bfloat16),
        jnp.where(in_row, 1.0, 0.0).astype(jnp.bfloat16),
        (((0,), (0,)), ((), ())),
        preferred_element_type=jnp.float32,
    )
    found = found[0:128] + found[128:256]
    in_lane = lax.broadcasted_iota(jnp.int32, (128, elems), 0)
    pore = jnp.sum(jnp.where(in_lane == at_ref[1:2, :], found, 0.0), axis=0, keepdims=True)
    row8, lane8 = (
        jnp.concatenate([at_ref[i : i + 1, r * 128 : (r + 1) * 128] for r in range(8)], axis=0) for i in range(2)
    )
    parts = [jnp.zeros((8, 128), jnp.float32) for _ in range(4)]
    for r in range(split, count):
        parts[r % 4] = jnp.where(row8 == r, take_lanes(band_ref[r : r + 1, :], lane8), parts[r % 4])
    pore = pore + element_rows((parts[0] + parts[1]) + (parts[2] + parts[3]))
    allow = jnp.maximum(strength_ref[0:1, :] - strength_ref[1:2, :] * (trial_ref[6] + pore), 0.0)
    deviator = trial_ref[7]
    yielded = deviator > allow
    scale = jnp.where(yielded, allow / jnp.where(yielded, deviator, 1.0), 1.0)
    release_ref[...] = (1.0 - scale) * deviator
    mean = trial_ref[6]
    parts = [mean + scale * trial_ref[i] for i in range(3)] + [scale * trial_ref[3 + i] for i in range(3)]
    for i in range(6):
        stress_ref[i] = parts[i]
    force = jnp.dot(
        matrix_ref[...],
        jnp.concatenate(parts, axis=0),
        precision=lax.Precision.HIGHEST,
        preferred_element_type=jnp.float32,
    )
    force_ref[...] = force
    high, low = halves(force)
    tile = lax.broadcasted_iota(jnp.int32, (8, elems), 0)
    total = jnp.zeros((32, 128), jnp.float32)
    for corner in range(8):
        node = conn_ref[corner : corner + 1, :]
        here = jnp.broadcast_to(node >> 7, tile.shape) == 8 + (tile & 3)
        rows = []
        for comp in range(3):
            at = slice(comp * 8 + corner, comp * 8 + corner + 1)
            value = jnp.where(tile < 4, jnp.broadcast_to(high[at], tile.shape), jnp.broadcast_to(low[at], tile.shape))
            rows.append(jnp.where(here, value, 0.0))
        rows.append(jnp.zeros(tile.shape, jnp.float32))
        left = jnp.concatenate(rows, axis=0).astype(jnp.bfloat16)
        total += lax.dot_general(
            left, node_lanes(node, elems), (((1,), (1,)), ((), ())), preferred_element_type=jnp.float32
        )
    for comp in range(3):
        ghost_ref[comp * 4 : comp * 4 + 4, :] = total[comp * 8 : comp * 8 + 4] + total[comp * 8 + 4 : comp * 8 + 8]


def own_forces(force_ref, conn_ref, own_ref):
    elems = conn_ref.shape[1]
    high, low = halves(force_ref[...])
    tile = lax.broadcasted_iota(jnp.int32, (8, elems), 0)
    total = jnp.zeros((48, 128), jnp.float32)
    for corner in range(8):
        node = conn_ref[corner : corner + 1, :]
        here = jnp.broadcast_to(node >> 7, tile.shape) == tile
        rows = []
        for comp in range(3):
            for source in (high, low):
                value = source[comp * 8 + corner : comp * 8 + corner + 1]
                rows.append(jnp.where(here, jnp.broadcast_to(value, tile.shape), 0.0))
        left = jnp.concatenate(rows, axis=0).astype(jnp.bfloat16)
        total += lax.dot_general(
            left, node_lanes(node, elems), (((1,), (1,)), ((), ())), preferred_element_type=jnp.float32
        )
    for comp in range(3):
        own_ref[comp * 8 : comp * 8 + 8, :] = total[comp * 16 : comp * 16 + 8] + total[comp * 16 + 8 : comp * 16 + 16]


def add_returned(own_ref, ghost_ref, shared_ref, out_ref):
    shared = shared_ref[...]
    in_lane = lax.broadcasted_iota(jnp.int32, (128, 128), 0)
    in_segment = lax.broadcasted_iota(jnp.int32, (8, 128), 0)
    lefts, rights = [], []
    for s in range(4):
        node = shared[s : s + 1]
        rights.append(jnp.where(jnp.broadcast_to(node & 127, in_lane.shape) == in_lane, 1.0, 0.0))
        here = jnp.broadcast_to(node >> 7, in_segment.shape) == in_segment
        rows = []
        for comp in range(3):
            value = ghost_ref[comp * 4 + s : comp * 4 + s + 1, :]
            high, low = halves(value)
            for piece in (high, low):
                rows.append(jnp.where(here, jnp.broadcast_to(piece, in_segment.shape), 0.0))
        lefts.append(jnp.concatenate(rows, axis=0))
    left = jnp.concatenate(lefts, axis=1).astype(jnp.bfloat16)
    right = jnp.concatenate(rights, axis=1).astype(jnp.bfloat16)
    added = lax.dot_general(left, right, (((1,), (1,)), ((), ())), preferred_element_type=jnp.float32)
    for comp in range(3):
        total = own_ref[comp * 8 : comp * 8 + 8, :] + added[comp * 16 : comp * 16 + 8] + added[comp * 16 + 8 : comp * 16 + 16]
        for s in range(8):
            out_ref[comp : comp + 1, s * 128 : (s + 1) * 128] = total[s : s + 1]


VM = pl.BlockSpec(memory_space=pltpu.VMEM)
SM = pl.BlockSpec(memory_space=pltpu.SMEM)


HBM = pl.BlockSpec(memory_space=pltpu.HBM)


def call(body, specs, outs, scratch, name, types=None):
    types = types or [jnp.float32] * len(outs)
    return pl.pallas_call(
        body,
        in_specs=specs,
        out_specs=tuple(VM for _ in outs),
        out_shape=tuple(jax.ShapeDtypeStruct(shape, kind) for shape, kind in zip(outs, types)),
        scratch_shapes=scratch,
        compiler_params=pltpu.CompilerParams(vmem_limit_bytes=VMEM_LIMIT),
        name=name,
    )


def in_hbm(value):
    return pltpu.with_memory_space_constraint(value, pltpu.HBM)


def steps(count, by):
    return [(i, (i + by) % count) for i in range(count)]


def per_device(
    pressure_head,
    zone_ids,
    retention_alpha,
    retention_exponent,
    conductivity,
    sent_columns,
    displacement,
    stress_old,
    connectivity,
    shared_nodes,
    element_zone,
    element_slot,
    element_depth,
    cohesion,
    friction,
):
    crest, section = (lax.axis_size(axis) for axis in AXES)
    devices = crest * section
    planes, rows, depth = pressure_head.shape
    height = rows + 8
    elems = connectivity.shape[1]
    nodes = displacement.shape[1]
    shared = shared_nodes.reshape(4, 128)
    zones = retention_alpha.shape[0]
    place = jnp.stack([lax.axis_index("section"), lax.axis_index("crest"), lax.axis_index(AXES)])
    i32, f32 = jnp.int32, jnp.float32

    forward, backward, head, zone = call(
        pack_section,
        [HBM] * 4,
        [(2 * WIDE * planes, depth), (32, depth), pressure_head.shape, zone_ids.shape],
        [pltpu.VMEM(displacement.shape, f32), pltpu.VMEM(shared.shape, i32), pltpu.SemaphoreType.DMA((4,))],
        "pack_section",
        [f32, f32, f32, i32],
    )(*(in_hbm(x) for x in (pressure_head, zone_ids, displacement, shared)))
    before = lax.ppermute(forward, "section", steps(section, 1))
    after = lax.ppermute(backward, "section", steps(section, -1))

    groups = rows // 8
    tables, index, flux = call(
        inner_flux,
        [VM] * 2 + [HBM] * 4,
        [(4 * zones, depth), (devices, 128), (groups, 8, depth)],
        [pltpu.VMEM((64, devices), i32)] + [pltpu.SMEM((zones,), f32)] * 3 + [pltpu.SemaphoreType.DMA((4,))],
        "inner_flux",
        [f32, i32, f32],
    )(head, zone, *(in_hbm(x) for x in (sent_columns[0].T, retention_alpha, retention_exponent, conductivity)))

    edge = (2 * (2 * groups + 1) + groups, 8, depth)
    low, high, tails = call(
        functools.partial(pack_crest, section),
        [SM] + [VM] * 5,
        [(edge[0] + 1, 8, depth), edge, (2 * planes, 8, depth)],
        [],
        "pack_crest",
    )(place, head, zone, flux, before, after)
    west = lax.ppermute(high, "crest", steps(crest, 1))
    east = lax.ppermute(low, "crest", steps(crest, -1))
    own = call(prepare, [VM] * 4, [(planes, height, depth)] * 8, [], "prepare")(tables, low, high, tails)

    field = pltpu.VMEM((planes + 2 * WIDE, height, depth), f32)
    head_out, outgoing, order = call(
        functools.partial(seepage, crest),
        [SM] + [VM] * 12,
        [pressure_head.shape, (devices, 8, 128), (8, 128)],
        [field] * 8 + [pltpu.VMEM((planes * rows, depth), f32), pltpu.VMEM((depth, planes * rows), f32)],
        "seepage",
    )(place, tables, index, *own, west, east)

    matrix = component_major()
    disp, stress, conn, strain_rows, force_rows, strength, places = call(
        functools.partial(selectors, devices),
        [SM, VM] + [HBM] * 10,
        [
            displacement.shape,
            (6, 8, elems),
            connectivity.shape,
            (48, 24),
            (24, 48),
            (2, elems),
            (2, elems),
        ],
        [pltpu.VMEM((8, 128), i32)] * 3 + [pltpu.SMEM((zones,), f32)] * 2 + [pltpu.SemaphoreType.DMA((10,))],
        "selectors",
        [f32, f32, i32, f32, f32, f32, i32],
    )(
        place,
        order,
        *(
            in_hbm(x)
            for x in (
                displacement,
                stress_old.transpose(1, 0, 2),
                connectivity,
                jnp.asarray(matrix, f32),
                jnp.asarray(matrix.T * 0.125, f32),
                element_slot.reshape(8, 128),
                element_depth.reshape(8, 128),
                element_zone.reshape(8, 128),
                cohesion,
                friction,
            )
        ),
    )
    (trial,) = call(
        functools.partial(trial_state, section),
        [SM] + [VM] * 6,
        [(8, 8, elems)],
        [pltpu.VMEM((40, 128), f32), pltpu.VMEM((24, elems), f32)],
        "trial_state",
    )(place, strain_rows, disp, after, east, conn, stress)
    incoming = lax.all_to_all(outgoing, AXES, split_axis=0, concat_axis=0, tiled=True)

    stress_new, release, force, ghost = call(
        final_state,
        [VM] * 6,
        [(6, 8, elems), (8, elems), (24, elems), (12, 128)],
        [],
        "final_state",
    )(force_rows, incoming.reshape(devices * 8, 128), places, strength, trial, conn)
    returned = lax.ppermute(ghost, AXES, steps(devices, 1))
    (own,) = call(own_forces, [VM] * 2, [(24, 128)], [], "own_forces")(force, conn)
    (node_forces,) = call(add_returned, [VM] * 3, [(3, nodes)], [], "add_returned")(own, returned, shared)
    return (head_out, stress_new.transpose(1, 0, 2), release, node_forces)


def solution(mesh):
    return jax.shard_map(
        per_device,
        mesh=mesh,
        in_specs=(
            P("crest", "section", None),
            P("crest", "section", None),
            P(),
            P(),
            P(),
            P(("crest", "section"), None, None),
            P(None, ("crest", "section")),
            P(None, None, ("crest", "section")),
            P(None, ("crest", "section")),
            P(("crest", "section")),
            P(("crest", "section")),
            P(("crest", "section")),
            P(("crest", "section")),
            P(),
            P(),
        ),
        out_specs=(
            P("crest", "section", None),
            P(None, None, ("crest", "section")),
            P(None, ("crest", "section")),
            P(None, ("crest", "section")),
        ),
        check_vma=False,
    )
```

```python
import functools

import jax
import jax.numpy as jnp
import numpy as np
from jax import lax
from jax.experimental import pallas as pl
from jax.experimental.pallas import tpu as pltpu
from jax.sharding import PartitionSpec as P

BAND = 16
SWEEPS = 3
WIDE = 3

STORAGE = 0.5
THETA_GAP = 0.35
TIME_STEP = 0.05
REDUCTION = 1.4
YOUNG = 200.0
POISSON = 0.3

AXES = ("crest", "section")
VMEM_LIMIT = 32 * 1024 * 1024


def corner_signs(index):
    return (2 * (index & 1) - 1, 2 * (index >> 1 & 1) - 1, 2 * (index >> 2 & 1) - 1)


def strain_matrix():
    matrix = np.zeros((48, 24))
    inv_root = 1.0 / np.sqrt(3.0)
    for gauss_point in range(8):
        gauss = [value * inv_root for value in corner_signs(gauss_point)]
        row_start = 6 * gauss_point
        for node_corner in range(8):
            sign_x, sign_y, sign_z = corner_signs(node_corner)
            grad_x = 0.25 * sign_x * (1 + gauss[1] * sign_y) * (1 + gauss[2] * sign_z)
            grad_y = 0.25 * sign_y * (1 + gauss[0] * sign_x) * (1 + gauss[2] * sign_z)
            grad_z = 0.25 * sign_z * (1 + gauss[0] * sign_x) * (1 + gauss[1] * sign_y)
            matrix[row_start + 0, node_corner] = grad_x
            matrix[row_start + 1, 8 + node_corner] = grad_y
            matrix[row_start + 2, 16 + node_corner] = grad_z
            matrix[row_start + 3, node_corner] = grad_y
            matrix[row_start + 3, 8 + node_corner] = grad_x
            matrix[row_start + 4, 8 + node_corner] = grad_z
            matrix[row_start + 4, 16 + node_corner] = grad_y
            matrix[row_start + 5, 16 + node_corner] = grad_x
            matrix[row_start + 5, node_corner] = grad_z
    return matrix


def component_major():
    order = [6 * gauss_point + comp for comp in range(6) for gauss_point in range(8)]
    return strain_matrix()[order]


def take_lanes(row, lanes):
    return jnp.take_along_axis(jnp.broadcast_to(row, lanes.shape), lanes, axis=1, mode="promise_in_bounds")


def pick(values_ref, index, first=0):
    lane = lax.broadcasted_iota(jnp.int32, (8, 128), 1)
    table = jnp.zeros((8, 128), jnp.float32)
    for zone in range(values_ref.shape[0]):
        table = jnp.where(lane == first + zone, values_ref[zone], table)
    return table if index is None else take_lanes(table, index)


def fetch(pairs, sems):
    copies = [pltpu.make_async_copy(source, target, sems.at[i]) for i, (source, target) in enumerate(pairs)]
    for copy in copies:
        copy.start()
    for copy in copies:
        copy.wait()


def pack_section(
    head_hbm, zone_hbm, disp_hbm, shared_hbm, forward_ref, backward_ref, head_ref, zone_ref, disp_ref, shared_ref, sems
):
    fetch([(head_hbm, head_ref), (zone_hbm, zone_ref), (disp_hbm, disp_ref), (shared_hbm, shared_ref)], sems)
    planes, rows = head_ref.shape[0], head_ref.shape[1]
    for x in range(planes):
        for field in range(2):
            first, last = slice(0, WIDE), slice(rows - WIDE, rows)
            at = field * WIDE * planes + WIDE * x
            if field == 0:
                forward_ref[at : at + WIDE, :] = head_ref[x, last, :]
                backward_ref[at : at + WIDE, :] = head_ref[x, first, :]
            else:
                forward_ref[at : at + WIDE, :] = zone_ref[x, last, :].astype(jnp.float32) + 1.0
                backward_ref[at : at + WIDE, :] = zone_ref[x, first, :].astype(jnp.float32) + 1.0
    index = shared_ref[...]
    index = jnp.concatenate([index, index], axis=0)
    lanes, segment = index & 127, index >> 7
    for comp in range(3):
        found = jnp.zeros((8, 128), jnp.float32)
        for s in range(disp_ref.shape[1] // 128):
            row = disp_ref[comp : comp + 1, s * 128 : (s + 1) * 128]
            found = jnp.where(segment == s, take_lanes(row, lanes), found)
        for s in range(4):
            at = 2 * WIDE * planes + 2 * comp + s // 2
            backward_ref[at : at + 1, (s % 2) * 128 : (s % 2 + 1) * 128] = found[s : s + 1]
    backward_ref[30:32, :] = jnp.zeros((2, 256), jnp.float32)


def pack_crest(sections, place_ref, head_ref, zone_ref, flux_ref, before_ref, after_ref, low_ref, high_ref, tail_ref):
    planes, rows = head_ref.shape[0], head_ref.shape[1]
    groups = rows // 8
    behind = jnp.where(place_ref[0] > 0, 1.0, 0.0)
    ahead = jnp.where(place_ref[0] < sections - 1, 1.0, 0.0)
    zone_at = 2 * groups + 1
    row = lax.broadcasted_iota(jnp.int32, (8, after_ref.shape[1]), 0)
    for field in range(2):
        tails = []
        for x in range(planes):
            target, plane = (low_ref, x) if x < 2 else (high_ref, x - 2)
            first = field * zone_at
            for group in range(groups):
                at = slice(8 * group, 8 * group + 8)
                own = head_ref[x, at, :] if field == 0 else zone_ref[x, at, :].astype(jnp.float32) + 1.0
                target[first + plane * groups + group] = own
            at = field * WIDE * planes + WIDE * x
            tails.append(
                jnp.concatenate(
                    [
                        after_ref[at : at + WIDE, :] * ahead,
                        jnp.zeros((2, after_ref.shape[1]), jnp.float32),
                        before_ref[at : at + WIDE, :] * behind,
                    ],
                    axis=0,
                )
            )
            tail_ref[field * planes + x] = tails[-1]
        for target, near, next_one in ((low_ref, 0, 1), (high_ref, 3, 2)):
            inner = jnp.where(row < 4, pltpu.roll(tails[next_one], 2, 0), pltpu.roll(tails[next_one], 6, 0))
            shared = jnp.where((row == 2) | (row == 5), inner, tails[near])
            target[field * zone_at + 2 * groups] = shared
    for group in range(groups):
        low_ref[2 * zone_at + group] = flux_ref[group]
        high_ref[2 * zone_at + group] = flux_ref[group]
    low_ref[2 * zone_at + groups] = after_ref[24:32, :]


def choose(values, bits):
    for bit in bits:
        values = [jnp.where(bit, values[i + 1], values[i]) for i in range(0, len(values), 2)]
    return values[0]


def params(tables_ref, zone):
    zones = tables_ref.shape[0] // 4
    tables = [
        [jnp.broadcast_to(tables_ref[f * zones + z : f * zones + z + 1, :], zone.shape) for z in range(zones)]
        for f in range(4)
    ]
    zone = zone.astype(jnp.int32) - 1
    bits = [(zone & (1 << bit)) != 0 for bit in range(3)]
    alpha, less, m, root = (choose(table, bits) for table in tables)
    return alpha, less, m, jnp.where(zone >= 0, root, 0.0), THETA_GAP * alpha * less


def fields(tables_ref, out, x, row, head, zone):
    for ref, value in zip(out, (head,) + params(tables_ref, zone)):
        ref[x, row : row + 8, :] = value


def base(alpha, less, h):
    scaled = alpha * jnp.maximum(-h, 0.0)
    power = jnp.exp(less * jnp.log(jnp.maximum(scaled, 1e-30)))
    plus = 1.0 + power * scaled
    return power, plus, jnp.log(plus)


def retention(h, alpha, less, m, root, gain):
    power, plus, log_plus = base(alpha, less, h)
    fourth = jnp.exp(m * log_plus)
    square = fourth * fourth
    part = power * (square * square)
    return root * fourth * (1.0 - part), TIME_STEP * plus / (STORAGE * plus + gain * part)


def inner_flux(
    head_ref,
    zone_ref,
    wanted_hbm,
    alpha_hbm,
    expo_hbm,
    ks_hbm,
    tables_ref,
    index_ref,
    flux_ref,
    wanted_ref,
    alpha_ref,
    expo_ref,
    ks_ref,
    sems,
):
    fetch([(wanted_hbm, wanted_ref), (alpha_hbm, alpha_ref), (expo_hbm, expo_ref), (ks_hbm, ks_ref)], sems)
    zones, width = alpha_ref.shape[0], tables_ref.shape[1]
    for z in range(zones):
        expo = jnp.full((1, width), expo_ref[z], jnp.float32)
        expo = jnp.where(expo > 0, expo, 2.0)
        tables_ref[z : z + 1, :] = jnp.full((1, width), alpha_ref[z], jnp.float32)
        tables_ref[zones + z : zones + z + 1, :] = expo - 1.0
        tables_ref[2 * zones + z : 2 * zones + z + 1, :] = -0.25 * (1.0 - 1.0 / expo)
        tables_ref[3 * zones + z : 3 * zones + z + 1, :] = jnp.sqrt(jnp.full((1, width), ks_ref[z], jnp.float32))
    wanted = wanted_ref[...]
    index_ref[...] = jnp.concatenate([wanted, pltpu.roll(wanted, wanted.shape[1] // 2, 1)], axis=0).T
    for group in range(flux_ref.shape[0]):
        at = slice(8 * group, 8 * group + 8)
        near, far = head_ref[1, at, :], head_ref[2, at, :]
        r_near, _ = retention(near, *params(tables_ref, zone_ref[1, at, :] + 1))
        r_far, _ = retention(far, *params(tables_ref, zone_ref[2, at, :] + 1))
        flux_ref[group] = r_near * r_far * (far - near)


def prepare(tables_ref, low_ref, high_ref, tail_ref, h, alpha_f, less_f, m_f, root_f, gain_f, r_f, cap_f):
    planes, groups = h.shape[0], h.shape[1] // 8 - 1
    zone_at = 2 * groups + 1
    out = (h, alpha_f, less_f, m_f, root_f, gain_f)
    for x in range(planes):
        source, plane = (low_ref, x) if x < 2 else (high_ref, x - 2)
        for group in range(groups):
            at = plane * groups + group
            fields(tables_ref, out, x, 8 * group, source[at], source[zone_at + at])
        fields(tables_ref, out, x, 8 * groups, tail_ref[x], tail_ref[planes + x])
        r_f[x], cap_f[x] = retention(*(ref[x] for ref in out))


def seepage(
    crests,
    place_ref,
    tables_ref,
    index,
    own_h,
    own_alpha,
    own_less,
    own_m,
    own_root,
    own_gain,
    own_r,
    own_cap,
    before_ref,
    after_ref,
    head_ref,
    out_ref,
    order_ref,
    h,
    alpha_f,
    less_f,
    m_f,
    root_f,
    gain_f,
    r_f,
    cap_f,
    table,
    deep,
):
    planes = head_ref.shape[0]
    rows = head_ref.shape[1]
    total = planes + 2 * WIDE
    height, depth = h.shape[1], h.shape[2]
    groups = rows // 8
    zone_at = 2 * groups + 1
    lane8 = lax.broadcasted_iota(jnp.int32, (8, 128), 1)
    behind = jnp.where(place_ref[1] > 0, 1.0, 0.0)
    ahead = jnp.where(place_ref[1] < crests - 1, 1.0, 0.0)
    out = (h, alpha_f, less_f, m_f, root_f, gain_f)

    row = lax.broadcasted_iota(jnp.int32, (8, depth), 0)

    def tail_of(shared, near):
        if near:
            return jnp.where((row < 2) | (row > 5), shared, 0.0)
        return jnp.where(row == 0, pltpu.roll(shared, 6, 0), jnp.where(row == 7, pltpu.roll(shared, 2, 0), 0.0))

    ends = []
    for source, first, inside in ((before_ref, 1, behind), (after_ref, WIDE + planes, ahead)):
        for plane in range(2):
            for group in range(groups):
                at = plane * groups + group
                fields(tables_ref, out, first + plane, 8 * group, source[at], source[zone_at + at] * inside)
            near = (first + plane) in (WIDE - 1, WIDE + planes)
            head, zone = tail_of(source[2 * groups], near), tail_of(source[zone_at + 2 * groups], near)
            fields(tables_ref, out, first + plane, rows, head, zone * inside)
        flux = [source[2 * zone_at + group] * inside for group in range(groups)]
        ends.append(jnp.concatenate(flux + [jnp.zeros((height - rows, depth), jnp.float32)], axis=0))
    for x in range(planes):
        h[WIDE + x] = own_h[x]

    own = dict(zip(map(id, (alpha_f, less_f, m_f, root_f, gain_f)), (own_alpha, own_less, own_m, own_root, own_gain)))

    def param(ref, x):
        return own[id(ref)][x - WIDE] if WIDE <= x < WIDE + planes else ref[x]

    inner_z = lax.broadcasted_iota(jnp.int32, (height, depth), 1) < depth - 1

    for sweep in range(SWEEPS):
        held = {}
        for x in range(max(sweep, 1), total - max(sweep, 1)):
            if sweep == 0 and WIDE <= x < WIDE + planes:
                held[x] = (own_r, own_cap, x - WIDE)
            else:
                values = (param(ref, x) for ref in (alpha_f, less_f, m_f, root_f, gain_f))
                r_f[x], cap_f[x] = retention(h[x], *values)
                held[x] = (r_f, cap_f, x)

        def r_of(x):
            return held[x][0][held[x][2]]

        def face(x):
            return r_of(x) * r_of(x + 1) * (h[x + 1] - h[x])

        came = face(sweep) if sweep > 0 else ends[0]
        for x in range(sweep + 1, total - sweep - 1):
            here, r = h[x], r_of(x)
            goes = face(x) if x < total - 2 or sweep > 0 else ends[1]
            flux_y = r * pltpu.roll(r, height - 1, 0) * (pltpu.roll(here, height - 1, 0) - here)
            flux_z = r * pltpu.roll(r, depth - 1, 1) * (pltpu.roll(here, depth - 1, 1) - here + 1.0)
            flux_z = jnp.where(inner_z, flux_z, 0.0)
            inflow = goes - came + (flux_y - pltpu.roll(flux_y, 1, 0)) + (flux_z - pltpu.roll(flux_z, 1, 1))
            h[x] = here + held[x][1][held[x][2]] * inflow
            came = goes

    for x in range(planes):
        here = h[WIDE + x]
        _, _, log_plus = base(own_alpha[x], own_less[x], here)
        head_ref[x] = here[0:rows]
        table[x * rows : (x + 1) * rows, :] = (jnp.exp(4.0 * own_m[x] * log_plus) * here)[0:rows]
    deep[...] = table[...].T
    order_ref[...] = deep[0:8, :]
    bands = depth // BAND
    half = out_ref.shape[0] // 2

    for b in range(bands):
        upper = deep[b * BAND : b * BAND + 8, :]
        lower = deep[b * BAND + 8 : b * BAND + 16, :]
        for d in range(b, half, bands):
            columns = jnp.broadcast_to(index[d : d + 1, :], (8, 128))
            first, second = take_lanes(upper, columns), pltpu.roll(take_lanes(lower, columns), 64, 1)
            out_ref[d] = jnp.where(lane8 < 64, first, second)
            out_ref[half + d] = jnp.where(lane8 < 64, second, first)


def element_rows(value):
    return jnp.concatenate([value[r : r + 1] for r in range(8)], axis=1)


def selectors(
    partitions,
    place_ref,
    order_ref,
    disp_hbm,
    stress_hbm,
    conn_hbm,
    strain_hbm,
    force_hbm,
    slot_hbm,
    depth_hbm,
    zone_hbm,
    cohesion_hbm,
    friction_hbm,
    disp_ref,
    stress_ref,
    conn_ref,
    strain_ref,
    force_ref,
    strength_ref,
    at_ref,
    slot_ref,
    depth_ref,
    zone_ref,
    cohesion_ref,
    friction_ref,
    sems,
):
    del order_ref
    fetch(
        [
            (conn_hbm, conn_ref),
            (slot_hbm, slot_ref),
            (depth_hbm, depth_ref),
            (zone_hbm, zone_ref),
            (cohesion_hbm, cohesion_ref),
            (friction_hbm, friction_ref),
            (disp_hbm, disp_ref),
            (stress_hbm, stress_ref),
            (strain_hbm, strain_ref),
            (force_hbm, force_ref),
        ],
        sems,
    )
    elems = conn_ref.shape[1]
    slot, depth = slot_ref[...], depth_ref[...]
    swap = jnp.where(place_ref[2] >= partitions // 2, 1, 0)
    at_ref[0:1, :] = element_rows((slot >> 6) * 8 + (depth & 7))
    at_ref[1:2, :] = element_rows(((depth >> 3) ^ swap) * 64 + (slot & 63))
    zone = zone_ref[...]
    tan_red = pick(friction_ref, zone) * (1.0 / REDUCTION)
    cos_red = 1.0 / jnp.sqrt(1.0 + tan_red * tan_red)
    sin_red = tan_red * cos_red
    common = 6.0 / (np.sqrt(3.0).astype(np.float32) * (3.0 - sin_red))
    strength_ref[0:1, :] = element_rows(common * (pick(cohesion_ref, zone) * (1.0 / REDUCTION)) * cos_red)
    strength_ref[1:2, :] = element_rows(common * sin_red)


def trial_state(
    sections, place_ref, matrix_ref, disp_ref, after_ref, tail_ref, conn_ref, stress_ref, trial_ref, nodes, corners
):
    ghost = jnp.where(place_ref[0] < sections - 1, after_ref[24:32, :], tail_ref[tail_ref.shape[0] - 1])
    for comp in range(3):
        for s in range(8):
            nodes[comp * 12 + s : comp * 12 + s + 1, :] = disp_ref[comp : comp + 1, s * 128 : (s + 1) * 128]
        for s in range(4):
            at = 2 * comp + s // 2
            nodes[comp * 12 + 8 + s : comp * 12 + 9 + s, :] = ghost[at : at + 1, (s % 2) * 128 : (s % 2 + 1) * 128]
    elems = conn_ref.shape[1]

    @pl.loop(0, elems, step=128)
    def _(e):
        e = pl.multiple_of(e, 128)
        index = conn_ref[:, pl.ds(e, 128)]
        lanes, segment = index & 127, index >> 7
        found = [jnp.zeros((8, 128), jnp.float32) for _ in range(3)]
        for s in range(12):
            here = segment == s
            for comp in range(3):
                row = nodes[comp * 12 + s : comp * 12 + s + 1, :]
                found[comp] = jnp.where(here, take_lanes(row, lanes), found[comp])
        for comp in range(3):
            corners[comp * 8 : comp * 8 + 8, pl.ds(e, 128)] = found[comp]

    strain = jnp.dot(
        matrix_ref[...], corners[...], precision=lax.Precision.HIGHEST, preferred_element_type=jnp.float32
    )
    lame_first = YOUNG * POISSON / ((1.0 + POISSON) * (1.0 - 2.0 * POISSON))
    modulus = YOUNG / (2.0 * (1.0 + POISSON))
    part = [strain[8 * i : 8 * i + 8] for i in range(6)]
    volume = lame_first * (part[0] + part[1] + part[2])
    normals = [stress_ref[i] + volume + 2.0 * modulus * part[i] for i in range(3)]
    shears = [stress_ref[i] + modulus * part[i] for i in range(3, 6)]
    mean = (normals[0] + normals[1] + normals[2]) * (1.0 / 3.0)
    devs = [value - mean for value in normals]
    trial_ref[6] = mean
    trial_ref[7] = jnp.sqrt(
        0.5 * (devs[0] ** 2 + devs[1] ** 2 + devs[2] ** 2) + shears[0] ** 2 + shears[1] ** 2 + shears[2] ** 2
    )
    for i in range(3):
        trial_ref[i] = devs[i]
        trial_ref[3 + i] = shears[i]


def halves(value):
    high = value.astype(jnp.bfloat16).astype(jnp.float32)
    return high, value - high


def node_lanes(node, elems):
    in_lane = lax.broadcasted_iota(jnp.int32, (128, elems), 0)
    return jnp.where(jnp.broadcast_to(node & 127, in_lane.shape) == in_lane, 1.0, 0.0).astype(jnp.bfloat16)


def final_state(
    matrix_ref, band_ref, at_ref, strength_ref, trial_ref, conn_ref, stress_ref, release_ref, force_ref, ghost_ref
):
    elems = conn_ref.shape[1]
    count = band_ref.shape[0]
    split = count // 2
    high, low = halves(band_ref[0:split, :])
    in_row = lax.broadcasted_iota(jnp.int32, (split, elems), 0) == at_ref[0:1, :]
    found = lax.dot_general(
        jnp.concatenate([high, low], axis=1).astype(jnp.bfloat16),
        jnp.where(in_row, 1.0, 0.0).astype(jnp.bfloat16),
        (((0,), (0,)), ((), ())),
        preferred_element_type=jnp.float32,
    )
    found = found[0:128] + found[128:256]
    in_lane = lax.broadcasted_iota(jnp.int32, (128, elems), 0)
    pore = jnp.sum(jnp.where(in_lane == at_ref[1:2, :], found, 0.0), axis=0, keepdims=True)
    row8, lane8 = (
        jnp.concatenate([at_ref[i : i + 1, r * 128 : (r + 1) * 128] for r in range(8)], axis=0) for i in range(2)
    )
    parts = [jnp.zeros((8, 128), jnp.float32) for _ in range(4)]
    for r in range(split, count):
        parts[r % 4] = jnp.where(row8 == r, take_lanes(band_ref[r : r + 1, :], lane8), parts[r % 4])
    pore = pore + element_rows((parts[0] + parts[1]) + (parts[2] + parts[3]))
    allow = jnp.maximum(strength_ref[0:1, :] - strength_ref[1:2, :] * (trial_ref[6] + pore), 0.0)
    deviator = trial_ref[7]
    yielded = deviator > allow
    scale = jnp.where(yielded, allow / jnp.where(yielded, deviator, 1.0), 1.0)
    release_ref[...] = (1.0 - scale) * deviator
    mean = trial_ref[6]
    parts = [mean + scale * trial_ref[i] for i in range(3)] + [scale * trial_ref[3 + i] for i in range(3)]
    for i in range(6):
        stress_ref[i] = parts[i]
    force = jnp.dot(
        matrix_ref[...],
        jnp.concatenate(parts, axis=0),
        precision=lax.Precision.HIGHEST,
        preferred_element_type=jnp.float32,
    )
    force_ref[...] = force
    high, low = halves(force)
    tile = lax.broadcasted_iota(jnp.int32, (8, elems), 0)
    total = jnp.zeros((32, 128), jnp.float32)
    for corner in range(8):
        node = conn_ref[corner : corner + 1, :]
        here = jnp.broadcast_to(node >> 7, tile.shape) == 8 + (tile & 3)
        rows = []
        for comp in range(3):
            at = slice(comp * 8 + corner, comp * 8 + corner + 1)
            value = jnp.where(tile < 4, jnp.broadcast_to(high[at], tile.shape), jnp.broadcast_to(low[at], tile.shape))
            rows.append(jnp.where(here, value, 0.0))
        rows.append(jnp.zeros(tile.shape, jnp.float32))
        left = jnp.concatenate(rows, axis=0).astype(jnp.bfloat16)
        total += lax.dot_general(
            left, node_lanes(node, elems), (((1,), (1,)), ((), ())), preferred_element_type=jnp.float32
        )
    for comp in range(3):
        ghost_ref[comp * 4 : comp * 4 + 4, :] = total[comp * 8 : comp * 8 + 4] + total[comp * 8 + 4 : comp * 8 + 8]


def own_forces(force_ref, conn_ref, own_ref):
    elems = conn_ref.shape[1]
    high, low = halves(force_ref[...])
    tile = lax.broadcasted_iota(jnp.int32, (8, elems), 0)
    total = jnp.zeros((48, 128), jnp.float32)
    for corner in range(8):
        node = conn_ref[corner : corner + 1, :]
        here = jnp.broadcast_to(node >> 7, tile.shape) == tile
        rows = []
        for comp in range(3):
            for source in (high, low):
                value = source[comp * 8 + corner : comp * 8 + corner + 1]
                rows.append(jnp.where(here, jnp.broadcast_to(value, tile.shape), 0.0))
        left = jnp.concatenate(rows, axis=0).astype(jnp.bfloat16)
        total += lax.dot_general(
            left, node_lanes(node, elems), (((1,), (1,)), ((), ())), preferred_element_type=jnp.float32
        )
    for comp in range(3):
        own_ref[comp * 8 : comp * 8 + 8, :] = total[comp * 16 : comp * 16 + 8] + total[comp * 16 + 8 : comp * 16 + 16]


def add_returned(own_ref, ghost_ref, shared_ref, out_ref):
    shared = shared_ref[...]
    in_lane = lax.broadcasted_iota(jnp.int32, (128, 128), 0)
    in_segment = lax.broadcasted_iota(jnp.int32, (8, 128), 0)
    lefts, rights = [], []
    for s in range(4):
        node = shared[s : s + 1]
        rights.append(jnp.where(jnp.broadcast_to(node & 127, in_lane.shape) == in_lane, 1.0, 0.0))
        here = jnp.broadcast_to(node >> 7, in_segment.shape) == in_segment
        rows = []
        for comp in range(3):
            value = ghost_ref[comp * 4 + s : comp * 4 + s + 1, :]
            high, low = halves(value)
            for piece in (high, low):
                rows.append(jnp.where(here, jnp.broadcast_to(piece, in_segment.shape), 0.0))
        lefts.append(jnp.concatenate(rows, axis=0))
    left = jnp.concatenate(lefts, axis=1).astype(jnp.bfloat16)
    right = jnp.concatenate(rights, axis=1).astype(jnp.bfloat16)
    added = lax.dot_general(left, right, (((1,), (1,)), ((), ())), preferred_element_type=jnp.float32)
    for comp in range(3):
        total = own_ref[comp * 8 : comp * 8 + 8, :] + added[comp * 16 : comp * 16 + 8] + added[comp * 16 + 8 : comp * 16 + 16]
        for s in range(8):
            out_ref[comp : comp + 1, s * 128 : (s + 1) * 128] = total[s : s + 1]


VM = pl.BlockSpec(memory_space=pltpu.VMEM)
SM = pl.BlockSpec(memory_space=pltpu.SMEM)


HBM = pl.BlockSpec(memory_space=pltpu.HBM)


def call(body, specs, outs, scratch, name, types=None, pinned=()):
    types = types or [jnp.float32] * len(outs)
    return pl.pallas_call(
        body,
        in_specs=specs,
        out_specs=tuple(VM for _ in outs),
        out_shape=tuple(
            (pltpu.VMEM if i in pinned else jax.ShapeDtypeStruct)(shape, kind)
            for i, (shape, kind) in enumerate(zip(outs, types))
        ),
        scratch_shapes=scratch,
        compiler_params=pltpu.CompilerParams(vmem_limit_bytes=VMEM_LIMIT),
        name=name,
    )


def in_hbm(value):
    return pltpu.with_memory_space_constraint(value, pltpu.HBM)


def steps(count, by):
    return [(i, (i + by) % count) for i in range(count)]


def per_device(
    pressure_head,
    zone_ids,
    retention_alpha,
    retention_exponent,
    conductivity,
    sent_columns,
    displacement,
    stress_old,
    connectivity,
    shared_nodes,
    element_zone,
    element_slot,
    element_depth,
    cohesion,
    friction,
):
    crest, section = (lax.axis_size(axis) for axis in AXES)
    devices = crest * section
    planes, rows, depth = pressure_head.shape
    height = rows + 8
    elems = connectivity.shape[1]
    nodes = displacement.shape[1]
    shared = shared_nodes.reshape(4, 128)
    zones = retention_alpha.shape[0]
    place = jnp.stack([lax.axis_index("section"), lax.axis_index("crest"), lax.axis_index(AXES)])
    i32, f32 = jnp.int32, jnp.float32

    forward, backward, head, zone = call(
        pack_section,
        [HBM] * 4,
        [(2 * WIDE * planes, depth), (32, depth), pressure_head.shape, zone_ids.shape],
        [pltpu.VMEM(displacement.shape, f32), pltpu.VMEM(shared.shape, i32), pltpu.SemaphoreType.DMA((4,))],
        "pack_section",
        [f32, f32, f32, i32],
    )(*(in_hbm(x) for x in (pressure_head, zone_ids, displacement, shared)))
    before = lax.ppermute(forward, "section", steps(section, 1))
    after = lax.ppermute(backward, "section", steps(section, -1))

    groups = rows // 8
    tables, index, flux = call(
        inner_flux,
        [VM] * 2 + [HBM] * 4,
        [(4 * zones, depth), (devices, 128), (groups, 8, depth)],
        [pltpu.VMEM((64, devices), i32)] + [pltpu.SMEM((zones,), f32)] * 3 + [pltpu.SemaphoreType.DMA((4,))],
        "inner_flux",
        [f32, i32, f32],
    )(head, zone, *(in_hbm(x) for x in (sent_columns[0].T, retention_alpha, retention_exponent, conductivity)))

    edge = (2 * (2 * groups + 1) + groups, 8, depth)
    low, high, tails = call(
        functools.partial(pack_crest, section),
        [SM] + [VM] * 5,
        [(edge[0] + 1, 8, depth), edge, (2 * planes, 8, depth)],
        [],
        "pack_crest",
    )(place, head, zone, flux, before, after)
    west = lax.ppermute(high, "crest", steps(crest, 1))
    east = lax.ppermute(low, "crest", steps(crest, -1))
    own = call(prepare, [VM] * 4, [(planes, height, depth)] * 8, [], "prepare")(tables, low, high, tails)

    field = pltpu.VMEM((planes + 2 * WIDE, height, depth), f32)
    head_out, outgoing, order = call(
        functools.partial(seepage, crest),
        [SM] + [VM] * 12,
        [pressure_head.shape, (devices, 8, 128), (8, 128)],
        [field] * 8 + [pltpu.VMEM((planes * rows, depth), f32), pltpu.VMEM((depth, planes * rows), f32)],
        "seepage",
        pinned=(1,),
    )(place, tables, index, *own, west, east)

    matrix = component_major()
    disp, stress, conn, strain_rows, force_rows, strength, places = call(
        functools.partial(selectors, devices),
        [SM, VM] + [HBM] * 10,
        [
            displacement.shape,
            (6, 8, elems),
            connectivity.shape,
            (48, 24),
            (24, 48),
            (2, elems),
            (2, elems),
        ],
        [pltpu.VMEM((8, 128), i32)] * 3 + [pltpu.SMEM((zones,), f32)] * 2 + [pltpu.SemaphoreType.DMA((10,))],
        "selectors",
        [f32, f32, i32, f32, f32, f32, i32],
    )(
        place,
        order,
        *(
            in_hbm(x)
            for x in (
                displacement,
                stress_old.transpose(1, 0, 2),
                connectivity,
                jnp.asarray(matrix, f32),
                jnp.asarray(matrix.T * 0.125, f32),
                element_slot.reshape(8, 128),
                element_depth.reshape(8, 128),
                element_zone.reshape(8, 128),
                cohesion,
                friction,
            )
        ),
    )
    (trial,) = call(
        functools.partial(trial_state, section),
        [SM] + [VM] * 6,
        [(8, 8, elems)],
        [pltpu.VMEM((40, 128), f32), pltpu.VMEM((24, elems), f32)],
        "trial_state",
    )(place, strain_rows, disp, after, east, conn, stress)
    incoming = lax.all_to_all(outgoing, AXES, split_axis=0, concat_axis=0, tiled=True)

    stress_new, release, force, ghost = call(
        final_state,
        [VM] * 6,
        [(6, 8, elems), (8, elems), (24, elems), (12, 128)],
        [],
        "final_state",
    )(force_rows, incoming.reshape(devices * 8, 128), places, strength, trial, conn)
    returned = lax.ppermute(ghost, AXES, steps(devices, 1))
    (own,) = call(own_forces, [VM] * 2, [(24, 128)], [], "own_forces")(force, conn)
    (node_forces,) = call(add_returned, [VM] * 3, [(3, nodes)], [], "add_returned")(own, returned, shared)
    return (head_out, stress_new.transpose(1, 0, 2), release, node_forces)


def solution(mesh):
    return jax.shard_map(
        per_device,
        mesh=mesh,
        in_specs=(
            P("crest", "section", None),
            P("crest", "section", None),
            P(),
            P(),
            P(),
            P(("crest", "section"), None, None),
            P(None, ("crest", "section")),
            P(None, None, ("crest", "section")),
            P(None, ("crest", "section")),
            P(("crest", "section")),
            P(("crest", "section")),
            P(("crest", "section")),
            P(("crest", "section")),
            P(),
            P(),
        ),
        out_specs=(
            P("crest", "section", None),
            P(None, None, ("crest", "section")),
            P(None, ("crest", "section")),
            P(None, ("crest", "section")),
        ),
        check_vma=False,
    )
```
